32 devices in a mesh: dom: 8 (over z, y), rep: 4 (over x, core).
Axes of the slice: x: 2, y: 2, z: 4, core: 2. Of those that a mesh axis runs over, the one named last changes fastest.
Arguments:
- features: float32 [4, 2, 2048, 128], P('rep', None, 'dom'), may hold values from -6 to 6
- edge_src: int32 [4, 2, 2048, 10], P('rep', None, 'dom'), may hold values from 0 to 319, as said below
- node_degree: int32 [4, 2, 2048], P('rep', None, 'dom'), may hold values from 1 to 10, as said below
- send_rows: int32 [4, 2, 64, 8], P('rep', None, 'dom'), may hold values from 0 to 255
- pair_src: int32 [4, 2, 4096], P('rep', None, 'dom'), may hold values from 0 to 255
- pair_dst: int32 [4, 2, 4096], P('rep', None, 'dom'), may hold values from 0 to 319
- pair_live: int32 [4, 2, 8], P('rep', None, 'dom'), may hold values from 1 to 256, as said below
- proj_one: float32 [128, 768], replicated, may hold values from -0.5 to 0.5
- proj_two: float32 [256, 576], replicated, may hold values from -0.375 to 0.375
- head_weight: float32 [64, 64], replicated, may hold values from -0.5 to 0.5
- vectors: float32 [5, 256], replicated, may hold values from -1.5 to 1.5
- biases: float32 [2, 64], replicated, may hold values from -1.5 to 1.5
- first_one: float32 [128, 768], replicated, may hold values from -0.0078125 to 0.0078125
- first_two: float32 [256, 576], replicated, may hold values from -0.0078125 to 0.0078125
- first_head: float32 [64, 64], replicated, may hold values from -0.0078125 to 0.0078125
- first_vectors: float32 [5, 256], replicated, may hold values from -0.0234375 to 0.0234375
- first_biases: float32 [2, 64], replicated, may hold values from -0.0234375 to 0.0234375
- second_one: float32 [128, 768], replicated, may hold values from 1.525879e-08 to 1.2207032e-07
- second_two: float32 [256, 576], replicated, may hold values from 1.525879e-08 to 1.2207032e-07
- second_head: float32 [64, 64], replicated, may hold values from 1.525879e-08 to 1.2207032e-07
- second_vectors: float32 [5, 256], replicated, may hold values from 1.373291e-07 to 1.0986328e-06
- second_biases: float32 [2, 64], replicated, may hold values from 1.373291e-07 to 1.0986328e-06
Outputs:
- loss_sum: float32 [], replicated
- pair_count: float32 [], replicated
- next_first_one: float32 [128, 768], replicated
- next_second_one: float32 [128, 768], replicated
- next_proj_one: float32 [128, 768], replicated
- next_first_two: float32 [256, 576], replicated
- next_second_two: float32 [256, 576], replicated
- next_proj_two: float32 [256, 576], replicated
- next_first_head: float32 [64, 64], replicated
- next_second_head: float32 [64, 64], replicated
- next_head_weight: float32 [64, 64], replicated
- next_first_vectors: float32 [5, 256], replicated
- next_second_vectors: float32 [5, 256], replicated
- next_vectors: float32 [5, 256], replicated
- next_first_biases: float32 [2, 64], replicated
- next_second_biases: float32 [2, 64], replicated
- next_biases: float32 [2, 64], replicated
The draws below stay inside these ranges and needn't reach their ends.
Inputs may be any that keep to these rules, and one draw needn't show every extreme that they name: `node_degree`: every node has at least one live edge slot; every eighth node of a partition has all 10. `edge_src`: indices below 256 name own rows; the others name received rows. `pair_live`: the last partition has all its slots live.
All inputs are finite; a program needn't handle non-finite values.
Results may differ from the reference program's by a relative error of at most 0.0063.
Values may be sent and summed in bfloat16 or wider, within the bound.
A program may use at most 192 MiB of HBM per device.

```python
import math
import jax
import jax.numpy as jnp
from jax import lax

IN = 128
HID = 256
HEADS = 4
HEAD = 64
FAN = 10
NODES_DEV = 256
PEER = 8
PAIRS = 512
MB = 2
STEP = 5
NODES = 2048
EXT = 320
N_DOM = 8
N_REP = 4


def draw_edge_src(key, part):
    key = jax.random.fold_in(key, 11)
    pick_key, near_key, far_key = jax.random.split(key, 3)
    shape = (N_REP, MB, NODES, FAN)
    pick = jax.random.randint(pick_key, shape, 0, 10)
    near = jax.random.randint(near_key, shape, 0, NODES_DEV)
    far = jax.random.randint(far_key, shape, NODES_DEV, EXT)
    return jnp.where(pick < 6, near, far).astype(jnp.int32)


def draw_node_degree(key, part):
    key = jax.random.fold_in(key, 12)
    value = jax.random.randint(key, (N_REP, MB, NODES), 1, FAN + 1)
    index = jnp.arange(NODES, dtype=jnp.int32)[None, None, :]
    return jnp.where(index % 8 == 0, FAN, value).astype(jnp.int32)


def draw_pair_live(key, part):
    key = jax.random.fold_in(key, 13)
    half = PAIRS // 2
    spread = max(N_DOM - 1, 1)
    device = jnp.arange(N_DOM, dtype=jnp.int32)
    base = half * (spread + 2 * device) // (3 * spread)
    jitter = jax.random.randint(key, (N_REP, MB, N_DOM), 0, max(half // 8, 1) + 1)
    value = jnp.where(device == N_DOM - 1, half, base - jitter)
    return jnp.clip(value, 1, half).astype(jnp.int32)


def draw_vectors(key, part):
    key = jax.random.fold_in(key, 14)
    noise_key, gain_key = jax.random.split(key, 2)
    noise = jnp.clip(0.3 * jax.random.normal(noise_key, (5, HID), jnp.float32), -1.5, 1.5)
    gain = jax.random.uniform(gain_key, (HID,), jnp.float32, 0.7, 1.3)
    return noise.at[2].set(gain)


def plant(values, key, low, largest):
    spot = [jax.random.randint(jax.random.fold_in(key, axis), (), 0, length) for axis, length in enumerate(values.shape)]
    widest = values.shape.index(max(values.shape))
    neighbour = spot[:widest] + [(spot[widest] + 1) % values.shape[widest]] + spot[widest + 1:]
    return values.at[tuple(spot)].set(low).at[tuple(neighbour)].set(largest)


def shard_levels(stream_key, shape, pieces, least, largest):
    factor_of = 1.0
    for dim, shards_of in pieces:
        draws = jax.random.uniform(jax.random.fold_in(jax.random.fold_in(stream_key, 6), dim), (shards_of,), jnp.float32, least / len(pieces), largest / len(pieces))
        factor_of = factor_of * jnp.repeat(jnp.exp(draws), shape[dim] // shards_of).reshape((-1,) + (1,) * (len(shape) - 1 - dim))
    return factor_of


def scatter_about(stream_key, dims, width, limit, shards=(), kind=jnp.bfloat16):
    values = jax.random.normal(stream_key, dims, jnp.float32) * width
    if len(shards) > 0:
        values = shard_levels(stream_key, dims, shards, -0.22, 0.18) * values
    return jnp.clip(values, min=-limit, max=limit).astype(kind)


def setup_inputs(seed: int = 0) -> dict:
    streams_of = jax.random.split(jax.random.key(seed), 23)
    features = scatter_about(streams_of[0], (N_REP, MB, NODES, IN), 1.0, 6.0, ((0, 4), (2, 8)), jnp.float32)
    edge_src = draw_edge_src(jax.random.fold_in(streams_of[22], 71), 0)
    node_degree = draw_node_degree(jax.random.fold_in(streams_of[22], 71), 0)
    send_rows = plant(jax.random.randint(streams_of[3], (N_REP, MB, N_DOM * N_DOM, PEER), 0, NODES_DEV), jax.random.fold_in(streams_of[3], 1), 0, NODES_DEV - 1).astype(jnp.int32)
    pair_src = plant(jax.random.randint(streams_of[4], (N_REP, MB, N_DOM * PAIRS), 0, NODES_DEV), jax.random.fold_in(streams_of[4], 1), 0, NODES_DEV - 1).astype(jnp.int32)
    pair_dst = plant(jax.random.randint(streams_of[5], (N_REP, MB, N_DOM * PAIRS), 0, EXT), jax.random.fold_in(streams_of[5], 1), 0, EXT - 1).astype(jnp.int32)
    pair_live = draw_pair_live(jax.random.fold_in(streams_of[22], 71), 0)
    proj_one = scatter_about(streams_of[7], (IN, 3 * HID), IN ** -0.5, 0.5, (), jnp.float32)
    proj_two = scatter_about(streams_of[8], (HID, 2 * HID + HEAD), HID ** -0.5, 0.375, (), jnp.float32)
    head_weight = scatter_about(streams_of[9], (HEAD, HEAD), (2 * HEAD) ** -0.5, 0.5, (), jnp.float32)
    vectors = draw_vectors(jax.random.fold_in(streams_of[22], 71), 0)
    biases = scatter_about(streams_of[11], (2, HEAD), 0.3, 1.5, (), jnp.float32)
    first_one = scatter_about(streams_of[12], (IN, 3 * HID), (0.1 * (N_DOM * N_REP * MB * PAIRS) ** -0.5), 0.0078125, (), jnp.float32)
    first_two = scatter_about(streams_of[13], (HID, 2 * HID + HEAD), (0.1 * (N_DOM * N_REP * MB * PAIRS) ** -0.5), 0.0078125, (), jnp.float32)
    first_head = scatter_about(streams_of[14], (HEAD, HEAD), (0.1 * (N_DOM * N_REP * MB * PAIRS) ** -0.5), 0.0078125, (), jnp.float32)
    first_vectors = scatter_about(streams_of[15], (5, HID), (0.3 * (N_DOM * N_REP * MB * PAIRS) ** -0.5), 0.0234375, (), jnp.float32)
    first_biases = scatter_about(streams_of[16], (2, HEAD), (0.3 * (N_DOM * N_REP * MB * PAIRS) ** -0.5), 0.0234375, (), jnp.float32)
    second_one = jnp.clip(jnp.exp(jax.random.uniform(streams_of[17], (IN, 3 * HID), jnp.float32, math.log(1.525878978725359e-08), math.log(1.2207031829802872e-07))), 1.525878978725359e-08, 1.2207031829802872e-07)
    second_two = jnp.clip(jnp.exp(jax.random.uniform(streams_of[18], (HID, 2 * HID + HEAD), jnp.float32, math.log(1.525878978725359e-08), math.log(1.2207031829802872e-07))), 1.525878978725359e-08, 1.2207031829802872e-07)
    second_head = jnp.clip(jnp.exp(jax.random.uniform(streams_of[19], (HEAD, HEAD), jnp.float32, math.log(1.525878978725359e-08), math.log(1.2207031829802872e-07))), 1.525878978725359e-08, 1.2207031829802872e-07)
    second_vectors = jnp.clip(jnp.exp(jax.random.uniform(streams_of[20], (5, HID), jnp.float32, math.log(1.3732909565078444e-07), math.log(1.0986327652062755e-06))), 1.3732909565078444e-07, 1.0986327652062755e-06)
    second_biases = jnp.clip(jnp.exp(jax.random.uniform(streams_of[21], (2, HEAD), jnp.float32, math.log(1.3732909565078444e-07), math.log(1.0986327652062755e-06))), 1.3732909565078444e-07, 1.0986327652062755e-06)
    return {"features": features, "edge_src": edge_src, "node_degree": node_degree, "send_rows": send_rows, "pair_src": pair_src, "pair_dst": pair_dst, "pair_live": pair_live, "proj_one": proj_one, "proj_two": proj_two, "head_weight": head_weight, "vectors": vectors, "biases": biases, "first_one": first_one, "first_two": first_two, "first_head": first_head, "first_vectors": first_vectors, "first_biases": first_biases, "second_one": second_one, "second_two": second_two, "second_head": second_head, "second_vectors": second_vectors, "second_biases": second_biases}


@jax.custom_vjp
def low(v):
    return lax.optimization_barrier(v.astype(jnp.bfloat16)).astype(jnp.float32)

@jax.custom_vjp
def low_back(v):
    return v

def low_keep(v):
    return (low(v), None)

def low_pass(kept, grad):
    return (grad,)

def back_keep(v):
    return (v, None)

def back_low(kept, grad):
    return (low(grad),)
low.defvjp(low_keep, low_pass)
low_back.defvjp(back_keep, back_low)
HIGH = lax.Precision.HIGHEST
eps_norm = 1e-05
beta_one = 0.9
beta_two = 0.999
rate_step = 0.05
decay_rate = 0.01
eps_adam = 1e-08

def attend(gathered, target, resid, vecs, degree):
    rows = gathered.shape[0]
    mixed = jax.nn.silu(gathered + target[:, None, :])
    score = lax.optimization_barrier(jnp.sum((mixed * vecs[0]).reshape(rows, FAN, HEADS, -1), axis=-1))
    live = (jnp.arange(FAN)[None, :] < degree[:, None])[:, :, None]
    score = jnp.where(live, score, -1e+30)
    top = lax.optimization_barrier(jnp.max(score, axis=1, keepdims=True))
    weight = jnp.where(live, jnp.exp(score - top), 0.0)
    alpha = weight / lax.optimization_barrier(jnp.sum(weight, axis=1, keepdims=True))
    message = lax.optimization_barrier(jnp.sum(alpha[..., None] * gathered.reshape(rows, FAN, HEADS, -1), axis=1))
    if len(vecs) == 4:
        summed = message.reshape(rows, -1) + vecs[1] + resid
        centred = summed - lax.optimization_barrier(jnp.mean(summed, axis=-1, keepdims=True))
        spread = lax.optimization_barrier(jnp.mean(centred * centred, axis=-1, keepdims=True))
        normed = centred * lax.rsqrt(spread + eps_norm) * vecs[2] + vecs[3]
        return jax.nn.elu(normed)
    return lax.optimization_barrier(jnp.mean(message, axis=1)) + vecs[1] + resid

def layer_one(feats, weight, vecs, ext_map, owner, edge_src, degree):
    rest = low_back(jnp.dot(low(feats), low(weight[:, HID:]), precision=HIGH))
    ext_src = low(low_back(jnp.dot(low(feats[ext_map.reshape(-1)]), low(weight[:, :HID]), precision=HIGH)))
    gathered = ext_src[owner[:, None] * EXT + edge_src]
    return attend(gathered, rest[:, :HID], rest[:, HID:], vecs, degree)

def layer(hidden, weight, vecs, src_global, degree):
    proj = low_back(jnp.dot(low(hidden), low(weight), precision=HIGH))
    source = low(proj[:, :HID])
    return attend(source[src_global], proj[:, HID:2 * HID], proj[:, 2 * HID:], vecs, degree)

def micro_loss(params, feats, edge_src, degree, send_rows, pair_src, pair_dst, pair_live):
    proj_one, proj_two, head_weight, vectors, biases = params
    device = jnp.arange(N_DOM, dtype=jnp.int32)
    sent = send_rows.reshape(N_DOM, N_DOM, PEER)
    halo = jnp.transpose(sent, (1, 0, 2)) + (device * NODES_DEV)[None, :, None]
    local = device[:, None] * NODES_DEV + jnp.arange(NODES_DEV, dtype=jnp.int32)[None, :]
    ext_map = jnp.concatenate([local, halo.reshape(N_DOM, -1)], axis=1)
    owner = jnp.arange(NODES, dtype=jnp.int32) // NODES_DEV
    src_global = ext_map[owner[:, None], edge_src]
    first_out = layer_one(feats, proj_one, (vectors[0], vectors[1], vectors[2], vectors[3]), ext_map, owner, edge_src, degree)
    second_out = layer(first_out, proj_two, (vectors[4], biases[0]), src_global, degree)
    embed = low_back(jnp.dot(low(second_out), low(head_weight), precision=HIGH)) + biases[1]
    pair_dev = jnp.arange(N_DOM * PAIRS, dtype=jnp.int32) // PAIRS
    first = embed[pair_dev * NODES_DEV + pair_src]
    second = embed[ext_map[pair_dev, pair_dst]]
    score = lax.optimization_barrier(jnp.sum(first * second, axis=-1))
    slot = jnp.arange(N_DOM * PAIRS, dtype=jnp.int32) % PAIRS
    positive = slot < PAIRS // 2
    live = slot % (PAIRS // 2) < pair_live[pair_dev]
    terms = jnp.where(positive, jax.nn.softplus(-score), jax.nn.softplus(score))
    return jnp.sum(jnp.where(live, terms, 0.0))

def adamw(param, grad, first, second):
    first = beta_one * first + (1.0 - beta_one) * grad
    second = beta_two * second + (1.0 - beta_two) * grad * grad
    fhat = first / (1.0 - beta_one ** STEP)
    shat = second / (1.0 - beta_two ** STEP)
    return (first, second, param - rate_step * (fhat / (jnp.sqrt(shat) + eps_adam) + decay_rate * param))

def reference(features, edge_src, node_degree, send_rows, pair_src, pair_dst, pair_live, proj_one, proj_two, head_weight, vectors, biases, first_one, first_two, first_head, first_vectors, first_biases, second_one, second_two, second_head, second_vectors, second_biases):
    params = (proj_one, proj_two, head_weight, vectors, biases)

    def flat(array):
        return array.reshape((N_REP * MB,) + array.shape[2:])
    data = tuple((flat(a) for a in (features, edge_src, node_degree, send_rows, pair_src, pair_dst, pair_live)))
    zero = jax.tree.map(jnp.zeros_like, params)

    def step(carry, batch):
        total, grads = carry

        def loss_of(values):
            return micro_loss(values, *batch)
        value, pullback = jax.vjp(loss_of, params)
        more, = pullback(jnp.ones_like(value))
        return ((total + value, jax.tree.map(jnp.add, grads, more)), None)
    (loss_sum, grads), _ = lax.scan(step, (jnp.zeros((), jnp.float32), zero), data)
    pair_count = 2.0 * jnp.sum(pair_live).astype(jnp.float32)
    firsts = (first_one, first_two, first_head, first_vectors, first_biases)
    seconds = (second_one, second_two, second_head, second_vectors, second_biases)
    outs = []
    for param, grad, first, second in zip(params, grads, firsts, seconds):
        outs.extend(adamw(param, grad / pair_count, first, second))
    return (loss_sum, pair_count, outs[0], outs[1], outs[2], outs[3], outs[4], outs[5], outs[6], outs[7], outs[8], outs[9], outs[10], outs[11], outs[12], outs[13], outs[14])
```

```python
import functools
from types import SimpleNamespace

import jax
import jax.numpy as jnp
from jax import lax
from jax.experimental import pallas as pl
from jax.experimental.pallas import tpu as pltpu
from jax.sharding import PartitionSpec as P

HEADS = 4
STEP = 5
LANES = 128

eps_norm = 1e-05
beta_one = 0.9
beta_two = 0.999
rate_step = 0.05
decay_rate = 0.01
eps_adam = 1e-08

F32 = jnp.float32
BF16 = jnp.bfloat16
MESH = pl.DeviceIdType.MESH


def contract(left, right, left_dim, right_dim):
    return lax.dot_general(
        left, right, (((left_dim,), (right_dim,)), ((), ())), preferred_element_type=F32
    )


def nn(left, right):
    return contract(left, right, 1, 0)


def nt(left, right):
    return contract(left, right, 1, 1)


def tn(left, right):
    return contract(left, right, 0, 0)


def split(value):
    high = value.astype(BF16)
    return high, (value - high.astype(F32)).astype(BF16)


def sigmoid(value):
    return 0.5 * jnp.tanh(0.5 * value) + 0.5


def row_iota(rows, columns):
    return lax.broadcasted_iota(jnp.int32, (rows, columns), 0)


def lane_iota(rows, columns):
    return lax.broadcasted_iota(jnp.int32, (rows, columns), 1)


def aligned(index, size):
    return pl.ds(pl.multiple_of(index * size, size), size)


def step_kernel(dims, names, *refs):
    (feats, edges, degree, sends, psrc, pdst, plive, w1, w2, wh, vec, bias, gbig, gsmall) = refs[:14]
    s = SimpleNamespace(**dict(zip(names, refs[14:])))
    nd, nr, mb, nodes, fan, hid, head, ext, halo, pairs, rows_all = dims
    half = pairs // 2
    tiles = nodes // LANES
    me = lax.axis_index("dom")
    mine = lax.axis_index("rep")
    rep_rows = rows_all // nr
    dom_rows = rep_rows // nd

    def peers(axis, index, count, send):
        def one(step, carry):
            send(lax.rem(index + step, count))
            return carry

        lax.fori_loop(1, count, one, 0)

    def push(axis, peer, src, dst, send_sem, recv_sem):
        pltpu.make_async_remote_copy(
            src_ref=src,
            dst_ref=dst,
            send_sem=send_sem,
            recv_sem=recv_sem,
            device_id={axis: peer},
            device_id_type=MESH,
        ).start()

    def arrived(ref, sem):
        pltpu.make_async_copy(ref, ref, sem).wait()

    def scatter_out(src, dst, number):
        send_sem, recv_sem = s.send_sems.at[number], s.recv_sems.at[number]
        peers(
            "dom",
            me,
            nd,
            lambda peer: push("dom", peer, src.at[peer], dst.at[me], send_sem, recv_sem),
        )
        pltpu.make_async_copy(src.at[me], dst.at[me], recv_sem).start()

    barrier = pltpu.get_barrier_semaphore()
    peers(
        "dom",
        me,
        nd,
        lambda peer: pl.semaphore_signal(barrier, inc=1, device_id={"dom": peer}, device_id_type=MESH),
    )
    peers(
        "rep",
        mine,
        nr,
        lambda peer: pl.semaphore_signal(barrier, inc=1, device_id={"rep": peer}, device_id_type=MESH),
    )

    for b in range(mb):
        spread = (
            lax.div(row_iota(halo, nd), halo // nd) == lane_iota(halo, nd)
        ).astype(F32).astype(BF16)
        listed = nn(spread, sends[b].astype(F32).astype(BF16))
        pick = lax.rem(row_iota(halo, halo // nd), halo // nd) == lane_iota(halo, halo // nd)
        column = jnp.sum(jnp.where(pick, listed, 0.0), axis=1, keepdims=True)
        s.ohs[b] = (lane_iota(halo, nodes).astype(F32) == column).astype(F32).astype(BF16)
        s.fext[b, :nodes, :] = feats[b].astype(BF16)

    parts = [
        nn(s.ohs[b], s.fext[b, :nodes, :]).reshape(nd, halo // nd, LANES) for b in range(mb)
    ]
    s.fsend[...] = jnp.concatenate(parts, axis=1).astype(BF16)
    pl.semaphore_wait(barrier, nd + nr - 2)
    scatter_out(s.fsend, s.frecv, 0)

    s.w1t[...] = w1[...].T.astype(BF16)
    s.w2b[...] = w2[...].astype(BF16)
    s.w2t[: 2 * hid, :] = w2[:, : 2 * hid].T.astype(BF16)
    s.w2t[2 * hid :, :] = w2[:, 2 * hid :].T.astype(BF16)
    whb = wh[...].astype(BF16)
    for j in range(5):
        s.vb[j] = jnp.broadcast_to(vec[j : j + 1, :], (LANES, hid)).T
    s.bb[...] = jnp.broadcast_to(bias[0:1, :], (LANES, head)).T
    s.acc[...] = jnp.zeros_like(s.acc)
    s.accb[...] = jnp.zeros_like(s.accb)
    s.sm[...] = jnp.zeros_like(s.sm)
    s.tmp[...] = jnp.zeros_like(s.tmp)

    for b in range(mb):
        s.tmp[:, :fan] = edges[b].astype(F32)
        s.et[b] = s.tmp[...].T[:16, :]

        def one_hot(k, carry):
            index = s.et[b, pl.ds(k, 1), :]
            s.oht[b, :, aligned(k, nodes)] = (
                (row_iota(ext, nodes).astype(F32) == index).astype(F32).astype(BF16)
            )
            return carry

        lax.fori_loop(0, fan, one_hot, 0)

        rest = nt(s.w1t[hid:, :], s.fext[b, :nodes, :])
        s.tgt[0, b] = rest[:hid]
        s.res1[b] = rest[hid:]

        slot = lax.rem(lane_iota(1, pairs), half)
        live = slot < plive[b : b + 1, :]
        from_src = (row_iota(nodes, pairs) == psrc[b : b + 1, :]).astype(F32).astype(BF16)
        to_dst = (
            ((row_iota(ext, pairs) == pdst[b : b + 1, :]) & live).astype(F32).astype(BF16)
        )
        s.cpos[b] = nt(from_src[:, :half], to_dst[:, :half])
        s.cneg[b] = nt(from_src[:, half:], to_dst[:, half:])

    def place(index):
        tile, which = lax.div(index, HEADS), lax.rem(index, HEADS)
        return tile, which, aligned(which, head), aligned(tile, LANES)

    def slot_at(k, tile):
        return pl.ds(pl.multiple_of(k * nodes + tile * LANES, LANES), LANES)

    def gather_rows(layer, b):
        def one(k, carry):
            s.g[layer, b, :, aligned(k, nodes)] = nn(s.tab[b], s.oht[b, :, aligned(k, nodes)])
            return carry

        lax.fori_loop(0, fan, one, 0)

    def attend(layer, b):
        att = 0 if layer == 0 else 4
        gather_rows(layer, b)

        def one(index, carry):
            tile, which, rows, cols = place(index)
            target = s.tgt[layer, b, rows, cols]
            weight = s.vb[att, rows, :]
            count = degree[b : b + 1, cols]
            scores = []
            for k in range(fan):
                u = s.g[layer, b, rows, slot_at(k, tile)] + target
                mixed = u * sigmoid(u)
                score = jnp.sum(mixed * weight, axis=0, keepdims=True)
                scores.append(jnp.where(count > k, score, -1e30))
            top = functools.reduce(jnp.maximum, scores)
            weights = [
                jnp.where(count > k, jnp.exp(scores[k] - top), 0.0) for k in range(fan)
            ]
            inverse = 1.0 / functools.reduce(jnp.add, weights)
            message = jnp.zeros((head, LANES), F32)
            for k in range(fan):
                alpha = weights[k] * inverse
                s.al[layer, b, index, k : k + 1, :] = alpha
                message = message + alpha * s.g[layer, b, rows, slot_at(k, tile)]
            s.msg[rows, cols] = message
            return carry

        lax.fori_loop(0, tiles * HEADS, one, 0)

    def attend_back(layer, b):
        att = 0 if layer == 0 else 4

        def one(index, carry):
            tile, which, rows, cols = place(index)
            target = s.tgt[layer, b, rows, cols]
            weight = s.vb[att, rows, :]
            if layer == 0:
                d_message = s.dmsg[rows, cols]
            else:
                d_message = s.dmsg[:head, cols]
            alphas = [s.al[layer, b, index, k : k + 1, :] for k in range(fan)]
            d_alphas = [
                jnp.sum(d_message * s.g[layer, b, rows, slot_at(k, tile)], axis=0, keepdims=True)
                for k in range(fan)
            ]
            total = functools.reduce(jnp.add, [a * d for a, d in zip(alphas, d_alphas)])
            d_target = jnp.zeros((head, LANES), F32)
            d_att = jnp.zeros((head, LANES), F32)
            for k in range(fan):
                d_score = alphas[k] * (d_alphas[k] - total)
                u = s.g[layer, b, rows, slot_at(k, tile)] + target
                gate = sigmoid(u)
                mixed = u * gate
                slope = gate * (1.0 + (u - mixed))
                d_u = (d_score * weight) * slope
                d_target = d_target + d_u
                d_att = d_att + d_score * mixed
                s.dg[rows, slot_at(k, tile)] = (alphas[k] * d_message + d_u).astype(BF16)
            s.dtgt[rows, cols] = d_target
            s.acc[att, rows, :] += d_att
            return carry

        lax.fori_loop(0, tiles * HEADS, one, 0)

    def pack_rows(value):
        blocks = value.reshape(nd, halo // nd, hid)
        return jnp.concatenate([blocks[:, :, :LANES], blocks[:, :, LANES:]], axis=1).astype(BF16)

    def unpack_rows(ref):
        blocks = ref[...].astype(F32)
        per = halo // nd
        return jnp.concatenate([blocks[:, :per, :], blocks[:, per:, :]], axis=2).reshape(halo, hid)

    def layer_one(b):
        s.fext[b, nodes:, :] = (
            s.frecv[...].astype(F32)[:, b * (halo // nd) : (b + 1) * (halo // nd), :]
            .reshape(halo, LANES)
            .astype(BF16)
        )
        s.tab[b] = nt(s.w1t[:hid, :], s.fext[b]).astype(BF16)
        attend(0, b)
        for t in range(tiles):
            cols = slice(t * LANES, (t + 1) * LANES)
            y = s.msg[:, cols] + s.vb[1] + s.res1[b, :, cols]
            centred = y - jnp.sum(y, axis=0, keepdims=True) * (1.0 / hid)
            spread = jnp.sum(centred * centred, axis=0, keepdims=True) * (1.0 / hid)
            rstd = lax.rsqrt(spread + eps_norm)
            normed = centred * rstd
            s.xhat[b, :, cols] = normed
            s.rstd[b, 0:1, cols] = rstd
            n = normed * s.vb[2] + s.vb[3]
            s.h1t[b, :, cols] = jnp.where(n > 0.0, n, jnp.exp(jnp.minimum(n, 0.0)) - 1.0).astype(BF16)
        s.hsend[b] = pack_rows(nt(s.ohs[b], s.h1t[b]))
        scatter_out(s.hsend.at[b], s.hrecv.at[b], 1 + b)
        own = nn(s.w2t[...], s.h1t[b])
        s.own2[b] = own[:hid].astype(BF16)
        s.tgt[1, b] = own[hid : 2 * hid]
        s.res2[b] = own[2 * hid :]

    def layer_two(b):
        arrived(s.hrecv.at[b], s.recv_sems.at[1 + b])
        s.tab[b, :, :nodes] = s.own2[b]
        s.tab[b, :, nodes:] = nt(s.w2t[:hid, :], unpack_rows(s.hrecv.at[b]).astype(BF16)).astype(BF16)
        attend(1, b)
        for t in range(tiles):
            cols = slice(t * LANES, (t + 1) * LANES)
            message = functools.reduce(
                jnp.add, [s.msg[h * head : (h + 1) * head, cols] for h in range(HEADS)]
            )
            s.h2[:, cols] = message * (1.0 / HEADS) + s.bb[...] + s.res2[b, :, cols]
        s.h2t[b] = s.h2[...].astype(BF16)
        rows = nt(s.ohs[b], s.h2t[b])
        s.zsend[b, :, :, :head] = rows.reshape(nd, halo // nd, head)
        scatter_out(s.zsend.at[b], s.zrecv.at[b], 3 + b)
        s.h2r[b, :nodes, :] = s.h2[...].T.astype(BF16)

    def pair_loss(b):
        arrived(s.zrecv.at[b], s.recv_sems.at[3 + b])
        s.h2r[b, nodes:, :] = s.zrecv[b].reshape(halo, LANES)[:, :head].astype(BF16)
        z = nn(s.h2r[b], whb) + bias[1:2, :]
        high, low = split(z)
        left = jnp.concatenate([high[:nodes], high[:nodes], low[:nodes]], axis=1)
        right = jnp.concatenate([high, low, high], axis=1)
        score = nt(left, right)
        pos, neg = s.cpos[b], s.cneg[b]
        small = jnp.exp(-jnp.abs(score))
        terms = (
            (pos + neg) * jnp.log1p(small)
            + pos * jnp.maximum(-score, 0.0)
            + neg * jnp.maximum(score, 0.0)
        )
        s.sm[12:13, 0:1] += jnp.sum(jnp.sum(terms, axis=0, keepdims=True), axis=1, keepdims=True)
        big = 1.0 / (1.0 + small)
        little = small * big
        up = score > 0.0
        d_score = neg * jnp.where(up, big, little) - pos * jnp.where(up, little, big)
        d_low = d_score.astype(BF16)
        d_table = tn(d_low, high[:nodes])
        s.dz[b] = nn(d_low, high) + d_table[:nodes]
        s.ysend[b, :, :, :head] = d_table[nodes:].reshape(nd, halo // nd, head)
        scatter_out(s.ysend.at[b], s.yrecv.at[b], 5 + b)

    def add_to(ref, value, b):
        if b == 0:
            ref[...] = value
        else:
            ref[...] += value

    def back_two(b):
        arrived(s.yrecv.at[b], s.recv_sems.at[5 + b])
        returned = s.yrecv[b].reshape(halo, LANES)[:, :head].astype(BF16)
        dz = s.dz[b] + tn(s.ohs[b], returned)
        s.sm[11:12, :head] += jnp.sum(dz, axis=0, keepdims=True)
        dz_low = dz.astype(BF16)
        add_to(s.gwh, nn(s.h2t[b], dz_low), b)
        d_out = nt(whb, dz_low)
        s.dres2[b] = d_out.astype(BF16)
        s.dmsg[:head, :] = d_out * (1.0 / HEADS)
        s.accb[...] += functools.reduce(
            jnp.add, [d_out[:, t * LANES : (t + 1) * LANES] for t in range(tiles)]
        )
        attend_back(1, b)
        s.dproj2[b, hid : 2 * hid, :] = s.dtgt[...].astype(BF16)
        s.dproj2[b, 2 * hid :, :] = s.dres2[b]
        s.gsend[b] = pack_rows(nt(s.oht[b, nodes:, :], s.dg[...]))
        scatter_out(s.gsend.at[b], s.grecv.at[b], 7 + b)
        s.dsrc[b] = nt(s.dg[...], s.oht[b, :nodes, :])

    def finish_two(b):
        arrived(s.grecv.at[b], s.recv_sems.at[7 + b])
        returned = unpack_rows(s.grecv.at[b]).astype(BF16)
        s.dproj2[b, :hid, :] = (s.dsrc[b] + tn(returned, s.ohs[b])).astype(BF16)
        add_to(s.gw2, nt(s.dproj2[b], s.h1t[b]), b)
        s.dh[...] = nn(s.w2b[...], s.dproj2[b])

    def back_one(b):
        for t in range(tiles):
            cols = slice(t * LANES, (t + 1) * LANES)
            normed = s.xhat[b, :, cols]
            n = normed * s.vb[2] + s.vb[3]
            dn = s.dh[:, cols] * jnp.where(n > 0.0, 1.0, jnp.exp(jnp.minimum(n, 0.0)))
            s.acc[3] += dn
            s.acc[2] += dn * normed
            dx = dn * s.vb[2]
            mean = jnp.sum(dx, axis=0, keepdims=True) * (1.0 / hid)
            along = jnp.sum(dx * normed, axis=0, keepdims=True) * (1.0 / hid)
            dy = s.rstd[b, 0:1, cols] * (dx - mean - normed * along)
            s.acc[1] += dy
            s.dmsg[:, cols] = dy
        attend_back(0, b)
        d_table = nt(s.dg[...], s.oht[b]).astype(BF16)
        d_rest = jnp.concatenate([s.dtgt[...], s.dmsg[...]], axis=0).astype(BF16)
        d_source = nn(d_table, s.fext[b])
        d_other = nn(d_rest, s.fext[b, :nodes, :])
        add_to(s.gw1.at[:hid, :], d_source, b)
        add_to(s.gw1.at[hid:, :], d_other, b)

    s.zsend[...] = jnp.zeros_like(s.zsend)
    s.ysend[...] = jnp.zeros_like(s.ysend)
    arrived(s.frecv, s.recv_sems.at[0])
    for stage in (layer_one, layer_two, pair_loss, back_two):
        for b in range(mb):
            stage(b)
    for b in range(mb):
        finish_two(b)
        back_one(b)

    in_one, in_two = 3 * hid, 2 * hid + head
    s.gb[:in_one, :] = s.gw1[...].astype(BF16)
    s.gb[in_one : in_one + in_two, :] = s.gw2[:, :LANES].astype(BF16)
    s.gb[in_one + in_two : in_one + 2 * in_two, :] = s.gw2[:, LANES:].astype(BF16)
    last = in_one + 2 * in_two
    s.gb[last:, :] = jnp.zeros((rows_all - last, LANES), BF16)
    s.gb[last : last + head, :head] = s.gwh[...].astype(BF16)
    for j in range(5):
        total = jnp.sum(s.acc[j].T, axis=0, keepdims=True)
        s.sm[2 * j : 2 * j + 1, :] = total[:, :LANES]
        s.sm[2 * j + 1 : 2 * j + 2, :] = total[:, LANES:]
    s.sm[10:11, :head] = jnp.sum(s.accb[...].T, axis=0, keepdims=True)
    s.sm[13:14, 0:1] = 2.0 * jnp.sum(plive[...].astype(F32), axis=0, keepdims=True)

    def part(ref, index, count):
        return ref.at[aligned(index, count), :]

    peers(
        "rep",
        mine,
        nr,
        lambda peer: push(
            "rep", peer, part(s.gb, peer, rep_rows), s.rb.at[mine], s.send_sems.at[9], s.recv_sems.at[9]
        ),
    )
    peers(
        "rep",
        mine,
        nr,
        lambda peer: push("rep", peer, s.sm, s.sm1.at[mine], s.send_sems.at[10], s.recv_sems.at[10]),
    )
    pltpu.make_async_copy(part(s.gb, mine, rep_rows), s.rb.at[mine], s.recv_sems.at[9]).start()
    pltpu.make_async_copy(s.sm, s.sm1.at[mine], s.recv_sems.at[10]).start()
    arrived(s.sm1, s.recv_sems.at[10])
    s.sms[...] = functools.reduce(jnp.add, [s.sm1[i] for i in range(nr)])
    peers(
        "dom",
        me,
        nd,
        lambda peer: push("dom", peer, s.sms, s.sm2.at[me], s.send_sems.at[11], s.recv_sems.at[11]),
    )
    pltpu.make_async_copy(s.sms, s.sm2.at[me], s.recv_sems.at[11]).start()
    arrived(s.rb, s.recv_sems.at[9])
    s.gd[...] = functools.reduce(jnp.add, [s.rb[i].astype(F32) for i in range(nr)]).astype(BF16)
    peers(
        "dom",
        me,
        nd,
        lambda peer: push(
            "dom", peer, part(s.gd, peer, dom_rows), s.rd.at[me], s.send_sems.at[12], s.recv_sems.at[12]
        ),
    )
    pltpu.make_async_copy(part(s.gd, me, dom_rows), s.rd.at[me], s.recv_sems.at[12]).start()
    arrived(s.rd, s.recv_sems.at[12])
    s.fin[...] = functools.reduce(jnp.add, [s.rd[i].astype(F32) for i in range(nd)]).astype(BF16)
    place_mine = s.ag.at[mine, me]
    peers(
        "dom",
        me,
        nd,
        lambda peer: push("dom", peer, s.fin, place_mine, s.send_sems.at[13], s.recv_sems.at[13]),
    )
    pltpu.make_async_copy(s.fin, place_mine, s.recv_sems.at[13]).start()
    arrived(s.ag.at[mine], s.recv_sems.at[13])
    peers(
        "rep",
        mine,
        nr,
        lambda peer: push(
            "rep", peer, s.ag.at[mine], s.ag.at[mine], s.send_sems.at[14], s.recv_sems.at[14]
        ),
    )
    arrived(s.sm2, s.recv_sems.at[11])
    gsmall[...] = functools.reduce(jnp.add, [s.sm2[i] for i in range(nd)])
    arrived(s.ag.at[pl.ds(0, nr - 1)], s.recv_sems.at[14])
    gbig[...] = s.ag[...].reshape(rows_all, LANES)

    arrived(s.fsend.at[pl.ds(0, nd - 1)], s.send_sems.at[0])
    for first, ref in ((1, s.hsend), (3, s.zsend), (5, s.ysend), (7, s.gsend)):
        for b in range(mb):
            arrived(ref.at[b, pl.ds(0, nd - 1)], s.send_sems.at[first + b])
    arrived(s.rb.at[pl.ds(0, nr - 1)], s.send_sems.at[9])
    arrived(s.sm1.at[pl.ds(0, nr - 1)], s.send_sems.at[10])
    arrived(s.sm2.at[pl.ds(0, nd - 1)], s.send_sems.at[11])
    arrived(s.rd.at[pl.ds(0, nd - 1)], s.send_sems.at[12])
    arrived(s.rd.at[pl.ds(0, nd - 1)], s.send_sems.at[13])
    arrived(s.ag.at[pl.ds(0, nr - 1)], s.send_sems.at[14])


def adamw(param, grad, first, second):
    first = beta_one * first + (1.0 - beta_one) * grad
    second = beta_two * second + (1.0 - beta_two) * grad * grad
    fhat = first * (1.0 / (1.0 - beta_one**STEP))
    shat = second * (1.0 / (1.0 - beta_two**STEP))
    return (
        first,
        second,
        param - rate_step * (fhat / (jnp.sqrt(shat) + eps_adam) + decay_rate * param),
    )


def adamw_kernel(hid, head, gbig, gsmall, *refs):
    params, firsts, seconds, outs = refs[:5], refs[5:10], refs[10:15], refs[15:]
    loss, count = outs[:2]
    outs = outs[2:]
    loss[...] = gsmall[12:13, 0:1]
    total = gsmall[13:14, 0:1]
    count[...] = total
    scale = 1.0 / total

    def update(index, grad, rows=slice(None), cols=slice(None)):
        made = adamw(
            params[index][rows, cols], grad, firsts[index][rows, cols], seconds[index][rows, cols]
        )
        for offset in range(3):
            outs[3 * index + offset][rows, cols] = made[offset]

    in_one, in_two = 3 * hid, 2 * hid + head
    for c in range(in_one // LANES):
        cols = slice(c * LANES, (c + 1) * LANES)
        update(0, gbig[cols, :].astype(F32).T * scale, slice(None), cols)
    for r in range(hid // LANES):
        rows = slice(r * LANES, (r + 1) * LANES)
        for c in range(0, in_two, LANES):
            width = min(LANES, in_two - c)
            start = in_one + r * in_two + c
            update(
                1, gbig[start : start + width, :].astype(F32).T * scale, rows, slice(c, c + width)
            )
    last = in_one + (hid // LANES) * in_two
    update(2, gbig[last : last + head, :].astype(F32)[:, :head] * scale)
    for j in range(5):
        for p in range(hid // LANES):
            row = (hid // LANES) * j + p
            update(
                3, gsmall[row : row + 1, :] * scale, slice(j, j + 1), slice(p * LANES, (p + 1) * LANES)
            )
    for j in range(2):
        update(4, gsmall[10 + j : 11 + j, :head] * scale, slice(j, j + 1))


def body(nd, nr, *args):
    data, weights, firsts, seconds = args[:7], args[7:12], args[12:17], args[17:]
    features, edge_src, node_degree, send_rows, pair_src, pair_dst, pair_live = (
        a.reshape(a.shape[1:]) for a in data
    )
    mb, nodes, width = features.shape
    fan = edge_src.shape[-1]
    per = send_rows.shape[-1]
    halo = nd * per
    ext = nodes + halo
    pairs = pair_src.shape[-1]
    hid = weights[3].shape[1]
    head = weights[2].shape[0]
    in_one, in_two = 3 * hid, 2 * hid + head
    unit = nd * nr * 16
    rows_all = -(-(in_one + 2 * in_two + head) // unit) * unit
    dims = (nd, nr, mb, nodes, fan, hid, head, ext, halo, pairs, rows_all)
    rep_rows = rows_all // nr
    dom_rows = rep_rows // nd
    scratch = dict(
        ohs=pltpu.VMEM((mb, halo, nodes), BF16),
        fext=pltpu.VMEM((mb, ext, width), BF16),
        fsend=pltpu.VMEM((nd, mb * per, LANES), BF16),
        frecv=pltpu.VMEM((nd, mb * per, LANES), BF16),
        w1t=pltpu.VMEM((in_one, width), BF16),
        w2b=pltpu.VMEM((hid, in_two), BF16),
        w2t=pltpu.VMEM((in_two, hid), BF16),
        vb=pltpu.VMEM((5, hid, LANES), F32),
        bb=pltpu.VMEM((head, LANES), F32),
        acc=pltpu.VMEM((5, hid, LANES), F32),
        accb=pltpu.VMEM((head, LANES), F32),
        sm=pltpu.VMEM((16, LANES), F32),
        tmp=pltpu.VMEM((nodes, LANES), F32),
        et=pltpu.VMEM((mb, 16, nodes), F32),
        oht=pltpu.VMEM((mb, ext, fan * nodes), BF16),
        tgt=pltpu.VMEM((2, mb, hid, nodes), F32),
        res1=pltpu.VMEM((mb, hid, nodes), F32),
        res2=pltpu.VMEM((mb, head, nodes), F32),
        cpos=pltpu.VMEM((mb, nodes, ext), F32),
        cneg=pltpu.VMEM((mb, nodes, ext), F32),
        tab=pltpu.VMEM((mb, hid, ext), BF16),
        g=pltpu.VMEM((2, mb, hid, fan * nodes), F32),
        al=pltpu.VMEM((2, mb, (nodes // LANES) * HEADS, 16, LANES), F32),
        msg=pltpu.VMEM((hid, nodes), F32),
        xhat=pltpu.VMEM((mb, hid, nodes), F32),
        rstd=pltpu.VMEM((mb, 8, nodes), F32),
        h1t=pltpu.VMEM((mb, hid, nodes), BF16),
        hsend=pltpu.VMEM((mb, nd, 2 * per, LANES), BF16),
        hrecv=pltpu.VMEM((mb, nd, 2 * per, LANES), BF16),
        own2=pltpu.VMEM((mb, hid, nodes), BF16),
        h2=pltpu.VMEM((head, nodes), F32),
        h2t=pltpu.VMEM((mb, head, nodes), BF16),
        h2r=pltpu.VMEM((mb, ext, head), BF16),
        zsend=pltpu.VMEM((mb, nd, per, LANES), F32),
        zrecv=pltpu.VMEM((mb, nd, per, LANES), F32),
        ysend=pltpu.VMEM((mb, nd, per, LANES), F32),
        yrecv=pltpu.VMEM((mb, nd, per, LANES), F32),
        dz=pltpu.VMEM((mb, nodes, head), F32),
        dmsg=pltpu.VMEM((hid, nodes), F32),
        dres2=pltpu.VMEM((mb, head, nodes), BF16),
        dtgt=pltpu.VMEM((hid, nodes), F32),
        dg=pltpu.VMEM((hid, fan * nodes), BF16),
        dproj2=pltpu.VMEM((mb, in_two, nodes), BF16),
        dsrc=pltpu.VMEM((mb, hid, nodes), F32),
        gsend=pltpu.VMEM((mb, nd, 2 * per, LANES), BF16),
        grecv=pltpu.VMEM((mb, nd, 2 * per, LANES), BF16),
        dh=pltpu.VMEM((hid, nodes), F32),
        gw1=pltpu.VMEM((in_one, LANES), F32),
        gw2=pltpu.VMEM((in_two, hid), F32),
        gwh=pltpu.VMEM((head, head), F32),
        gb=pltpu.VMEM((rows_all, LANES), BF16),
        rb=pltpu.VMEM((nr, rep_rows, LANES), BF16),
        gd=pltpu.VMEM((rep_rows, LANES), BF16),
        rd=pltpu.VMEM((nd, dom_rows, LANES), BF16),
        fin=pltpu.VMEM((dom_rows, LANES), BF16),
        ag=pltpu.VMEM((nr, nd, dom_rows, LANES), BF16),
        sm1=pltpu.VMEM((nr, 16, LANES), F32),
        sms=pltpu.VMEM((16, LANES), F32),
        sm2=pltpu.VMEM((nd, 16, LANES), F32),
        send_sems=pltpu.SemaphoreType.DMA((15,)),
        recv_sems=pltpu.SemaphoreType.DMA((15,)),
    )
    whole = pl.BlockSpec(memory_space=pltpu.VMEM)
    gbig, gsmall = pl.pallas_call(
        functools.partial(step_kernel, dims, tuple(scratch)),
        out_shape=(
            jax.ShapeDtypeStruct((rows_all, LANES), BF16),
            jax.ShapeDtypeStruct((16, LANES), F32),
        ),
        in_specs=[whole] * 12,
        out_specs=(whole, whole),
        scratch_shapes=list(scratch.values()),
        compiler_params=pltpu.CompilerParams(
            collective_id=0, has_side_effects=True, vmem_limit_bytes=48 * 1024 * 1024
        ),
    )(features, edge_src, node_degree, send_rows, pair_src, pair_dst, pair_live, *weights)

    shapes = [jax.ShapeDtypeStruct((1, 1), F32)] * 2
    for weight in weights:
        shapes += [jax.ShapeDtypeStruct(weight.shape, F32)] * 3
    made = pl.pallas_call(
        functools.partial(adamw_kernel, hid, head),
        out_shape=tuple(shapes),
        in_specs=[whole] * 17,
        out_specs=tuple([whole] * 17),
        compiler_params=pltpu.CompilerParams(vmem_limit_bytes=32 * 1024 * 1024),
    )(gbig, gsmall, *weights, *firsts, *seconds)
    return (made[0].reshape(()), made[1].reshape(())) + tuple(made[2:])


def solution(mesh):
    sharded = (
        P("rep", None, "dom", None),
        P("rep", None, "dom", None),
        P("rep", None, "dom"),
        P("rep", None, "dom", None),
        P("rep", None, "dom"),
        P("rep", None, "dom"),
        P("rep", None, "dom"),
    )
    return jax.shard_map(
        functools.partial(body, mesh.shape["dom"], mesh.shape["rep"]),
        mesh=mesh,
        in_specs=sharded + (P(),) * 15,
        out_specs=(P(),) * 17,
        check_vma=False,
    )
```

```python
import functools
from types import SimpleNamespace

import jax
import jax.numpy as jnp
from jax import lax
from jax.experimental import pallas as pl
from jax.experimental.pallas import tpu as pltpu
from jax.sharding import PartitionSpec as P

HEADS = 4
STEP = 5
LANES = 128

eps_norm = 1e-05
beta_one = 0.9
beta_two = 0.999
rate_step = 0.05
decay_rate = 0.01
eps_adam = 1e-08

F32 = jnp.float32
BF16 = jnp.bfloat16
MESH = pl.DeviceIdType.MESH


def contract(left, right, left_dim, right_dim):
    return lax.dot_general(
        left, right, (((left_dim,), (right_dim,)), ((), ())), preferred_element_type=F32
    )


def nn(left, right):
    return contract(left, right, 1, 0)


def nt(left, right):
    return contract(left, right, 1, 1)


def tn(left, right):
    return contract(left, right, 0, 0)


def split(value):
    high = value.astype(BF16)
    return high, (value - high.astype(F32)).astype(BF16)


def sigmoid(value):
    return 0.5 * jnp.tanh(0.5 * value) + 0.5


def row_iota(rows, columns):
    return lax.broadcasted_iota(jnp.int32, (rows, columns), 0)


def lane_iota(rows, columns):
    return lax.broadcasted_iota(jnp.int32, (rows, columns), 1)


def aligned(index, size):
    return pl.ds(pl.multiple_of(index * size, size), size)


def step_kernel(dims, names, *refs):
    held, outs, rest_refs = refs[:22], refs[22:38], refs[38:]
    staged = rest_refs[:22]
    s = SimpleNamespace(**dict(zip(names, rest_refs[22:])))
    (feats, edges, degree, sends, psrc, pdst, plive, w1, w2, wh, vec, bias) = staged[:12]
    firsts, seconds = staged[12:17], staged[17:22]
    nd, nr, mb, nodes, fan, hid, head, ext, halo, pairs, bounds = dims
    half = pairs // 2
    tiles = nodes // LANES
    me = lax.axis_index("dom")
    mine = lax.axis_index("rep")

    def peers(axis, index, count, send):
        def one(step, carry):
            send(lax.rem(index + step, count))
            return carry

        lax.fori_loop(1, count, one, 0)

    def push(axis, peer, src, dst, send_sem, recv_sem):
        pltpu.make_async_remote_copy(
            src_ref=src,
            dst_ref=dst,
            send_sem=send_sem,
            recv_sem=recv_sem,
            device_id={axis: peer},
            device_id_type=MESH,
        ).start()

    incoming, outgoing = {}, []

    def arrived(ref, sem):
        pltpu.make_async_copy(ref, ref, sem).wait()

    def receive(number):
        arrived(incoming.pop(number), s.recv_sems.at[number])

    def finish():
        for number in list(incoming):
            receive(number)
        for number, ref in outgoing:
            arrived(ref, s.send_sems.at[number])

    def load(*which):
        for i in which:
            pltpu.make_async_copy(held[i], staged[i], s.load_sems.at[i]).start()

    def loaded(*which):
        for i in which:
            arrived(staged[i], s.load_sems.at[i])

    def scatter_out(src, dst, number):
        send_sem, recv_sem = s.send_sems.at[number], s.recv_sems.at[number]
        peers(
            "dom",
            me,
            nd,
            lambda peer: push("dom", peer, src.at[peer], dst.at[me], send_sem, recv_sem),
        )
        pltpu.make_async_copy(src.at[me], dst.at[me], recv_sem).start()
        incoming[number] = dst
        outgoing.append((number, src.at[pl.ds(0, nd - 1)]))

    load(3, 0, 7, 8, 9, 10, 11, 1, 2, 4, 5, 6)
    barrier = pltpu.get_barrier_semaphore()
    peers(
        "dom",
        me,
        nd,
        lambda peer: pl.semaphore_signal(barrier, inc=1, device_id={"dom": peer}, device_id_type=MESH),
    )
    peers(
        "rep",
        mine,
        nr,
        lambda peer: pl.semaphore_signal(barrier, inc=1, device_id={"rep": peer}, device_id_type=MESH),
    )

    load(*range(12, 22))
    loaded(3, 0)
    for b in range(mb):
        spread = (
            lax.div(row_iota(halo, nd), halo // nd) == lane_iota(halo, nd)
        ).astype(F32).astype(BF16)
        listed = nn(spread, sends[b].astype(F32).astype(BF16))
        pick = lax.rem(row_iota(halo, halo // nd), halo // nd) == lane_iota(halo, halo // nd)
        column = jnp.sum(jnp.where(pick, listed, 0.0), axis=1, keepdims=True)
        s.ohs[b] = (lane_iota(halo, nodes).astype(F32) == column).astype(F32).astype(BF16)
        s.fext[b, :nodes, :] = feats[b].astype(BF16)

    parts = [
        nn(s.ohs[b], s.fext[b, :nodes, :]).reshape(nd, halo // nd, LANES) for b in range(mb)
    ]
    s.fsend[...] = jnp.concatenate(parts, axis=1).astype(BF16)
    pl.semaphore_wait(barrier, nd + nr - 2)
    scatter_out(s.fsend, s.frecv, 0)

    loaded(7, 8, 9, 10, 11)
    s.w1t[...] = w1[...].T.astype(BF16)
    s.w2t[...] = w2[...].astype(BF16)
    s.w2b[...] = w2[...].T.astype(BF16)
    whb = wh[...].astype(BF16)
    for j in range(5):
        s.vb[j] = jnp.broadcast_to(vec[j : j + 1, :], (LANES, hid)).T
    s.bb[...] = jnp.broadcast_to(bias[0:1, :], (LANES, head)).T
    s.acc[...] = jnp.zeros_like(s.acc)
    s.accb[...] = jnp.zeros_like(s.accb)
    s.sm[...] = jnp.zeros_like(s.sm)
    loaded(1, 2, 4, 5, 6)

    for b in range(mb):

        def one_hot(k, carry):
            index = edges[k, b : b + 1, :]
            s.oht[b, :, aligned(k, nodes)] = (
                (row_iota(ext, nodes) == index).astype(F32).astype(BF16)
            )
            return carry

        lax.fori_loop(0, fan, one_hot, 0)

        rest = nt(s.w1t[hid:, :], s.fext[b, :nodes, :])
        s.tgt[0, b] = rest[:hid]
        s.res1[b] = rest[hid:]

        slot = lax.rem(lane_iota(1, pairs), half)
        count = jnp.sum(
            jnp.where(lane_iota(1, mb) == b, plive[...].astype(F32), 0.0), axis=1, keepdims=True
        )
        live = slot.astype(F32) < count
        from_src = (row_iota(nodes, pairs) == psrc[b : b + 1, :]).astype(F32).astype(BF16)
        to_dst = (
            ((row_iota(ext, pairs) == pdst[b : b + 1, :]) & live).astype(F32).astype(BF16)
        )
        s.cpos[b] = nt(from_src[:, :half], to_dst[:, :half])
        s.cneg[b] = nt(from_src[:, half:], to_dst[:, half:])

    def place(index):
        tile, which = lax.div(index, HEADS), lax.rem(index, HEADS)
        return tile, which, aligned(which, head), aligned(tile, LANES)

    def slot_at(k, tile):
        return pl.ds(pl.multiple_of(k * nodes + tile * LANES, LANES), LANES)

    def attend(layer, b):
        att = 0 if layer == 0 else 4
        s.g[layer, b] = nn(s.tab[b], s.oht[b])

        def one(index, carry):
            tile, which, rows, cols = place(index)
            target = s.tgt[layer, b, rows, cols]
            weight = s.vb[att, rows, :]
            count = degree[b : b + 1, cols]
            scores = []
            for k in range(fan):
                u = s.g[layer, b, rows, slot_at(k, tile)] + target
                mixed = u * sigmoid(u)
                score = jnp.sum(mixed * weight, axis=0, keepdims=True)
                scores.append(jnp.where(count > k, score, -1e30))
            top = functools.reduce(jnp.maximum, scores)
            weights = [
                jnp.where(count > k, jnp.exp(scores[k] - top), 0.0) for k in range(fan)
            ]
            inverse = 1.0 / functools.reduce(jnp.add, weights)
            message = jnp.zeros((head, LANES), F32)
            for k in range(fan):
                alpha = weights[k] * inverse
                s.al[layer, b, index, k : k + 1, :] = alpha
                message = message + alpha * s.g[layer, b, rows, slot_at(k, tile)]
            s.msg[rows, cols] = message
            return carry

        lax.fori_loop(0, tiles * HEADS, one, 0)

    def attend_back(layer, b, first=0, last=None):
        att = 0 if layer == 0 else 4

        def one(index, carry):
            tile, which, rows, cols = place(index)
            target = s.tgt[layer, b, rows, cols]
            weight = s.vb[att, rows, :]
            if layer == 0:
                d_message = s.dmsg[rows, cols]
            else:
                d_message = s.dmsg[:head, cols]
            alphas = [s.al[layer, b, index, k : k + 1, :] for k in range(fan)]
            d_alphas = [
                jnp.sum(d_message * s.g[layer, b, rows, slot_at(k, tile)], axis=0, keepdims=True)
                for k in range(fan)
            ]
            total = functools.reduce(jnp.add, [a * d for a, d in zip(alphas, d_alphas)])
            d_target = jnp.zeros((head, LANES), F32)
            d_att = jnp.zeros((head, LANES), F32)
            for k in range(fan):
                d_score = alphas[k] * (d_alphas[k] - total)
                u = s.g[layer, b, rows, slot_at(k, tile)] + target
                gate = sigmoid(u)
                mixed = u * gate
                slope = gate * (1.0 + (u - mixed))
                d_u = (d_score * weight) * slope
                d_target = d_target + d_u
                d_att = d_att + d_score * mixed
                s.dg[rows, slot_at(k, tile)] = (alphas[k] * d_message + d_u).astype(BF16)
            s.dtgt[rows, cols] = d_target
            s.acc[att, rows, :] += d_att
            return carry

        lax.fori_loop(first, tiles * HEADS if last is None else last, one, 0)

    def pack_rows(value):
        blocks = value.reshape(nd, halo // nd, hid)
        return jnp.concatenate([blocks[:, :, :LANES], blocks[:, :, LANES:]], axis=1).astype(BF16)

    def unpack_rows(ref):
        blocks = ref[...].astype(F32)
        per = halo // nd
        return jnp.concatenate([blocks[:, :per, :], blocks[:, per:, :]], axis=2).reshape(halo, hid)

    def layer_one(b):
        s.fext[b, nodes:, :] = (
            s.frecv[...].astype(F32)[:, b * (halo // nd) : (b + 1) * (halo // nd), :]
            .reshape(halo, LANES)
            .astype(BF16)
        )
        s.tab[b] = nt(s.w1t[:hid, :], s.fext[b]).astype(BF16)
        attend(0, b)
        for t in range(tiles):
            cols = slice(t * LANES, (t + 1) * LANES)
            y = s.msg[:, cols] + s.vb[1] + s.res1[b, :, cols]
            centred = y - jnp.sum(y, axis=0, keepdims=True) * (1.0 / hid)
            spread = jnp.sum(centred * centred, axis=0, keepdims=True) * (1.0 / hid)
            rstd = lax.rsqrt(spread + eps_norm)
            normed = centred * rstd
            s.xhat[b, :, cols] = normed
            s.rstd[b, 0:1, cols] = rstd
            n = normed * s.vb[2] + s.vb[3]
            s.h1t[b, :, cols] = jnp.where(n > 0.0, n, jnp.exp(jnp.minimum(n, 0.0)) - 1.0).astype(BF16)
        s.hsend[b] = pack_rows(nt(s.ohs[b], s.h1t[b]))
        scatter_out(s.hsend.at[b], s.hrecv.at[b], 1 + b)
        own = nn(s.w2t[...], s.h1t[b])
        s.own2[b] = own[:hid].astype(BF16)
        s.tgt[1, b] = own[hid : 2 * hid]
        s.res2[b] = own[2 * hid :]

    def layer_two(b):
        receive(1 + b)
        s.tab[b, :, :nodes] = s.own2[b]
        s.tab[b, :, nodes:] = nt(s.w2t[:hid, :], unpack_rows(s.hrecv.at[b]).astype(BF16)).astype(BF16)
        attend(1, b)
        for t in range(tiles):
            cols = slice(t * LANES, (t + 1) * LANES)
            message = functools.reduce(
                jnp.add, [s.msg[h * head : (h + 1) * head, cols] for h in range(HEADS)]
            )
            s.h2[:, cols] = message * (1.0 / HEADS) + s.bb[...] + s.res2[b, :, cols]
        s.h2t[b] = s.h2[...].astype(BF16)
        rows = nt(s.ohs[b], s.h2t[b])
        s.zsend[b, :, :, :head] = rows.reshape(nd, halo // nd, head)
        scatter_out(s.zsend.at[b], s.zrecv.at[b], 3 + b)
        s.h2r[b, :nodes, :] = s.h2[...].T.astype(BF16)

    def pair_loss(b):
        receive(3 + b)
        s.h2r[b, nodes:, :] = s.zrecv[b].reshape(halo, LANES)[:, :head].astype(BF16)
        z = nn(s.h2r[b], whb) + bias[1:2, :]
        high, low = split(z)
        left = jnp.concatenate([high[:nodes], high[:nodes], low[:nodes]], axis=1)
        right = jnp.concatenate([high, low, high], axis=1)
        score = nt(left, right)
        pos, neg = s.cpos[b], s.cneg[b]
        small = jnp.exp(-jnp.abs(score))
        terms = (
            (pos + neg) * jnp.log1p(small)
            + pos * jnp.maximum(-score, 0.0)
            + neg * jnp.maximum(score, 0.0)
        )
        s.sm[12:13, 0:1] += jnp.sum(jnp.sum(terms, axis=0, keepdims=True), axis=1, keepdims=True)
        big = 1.0 / (1.0 + small)
        little = small * big
        up = score > 0.0
        d_score = neg * jnp.where(up, big, little) - pos * jnp.where(up, little, big)
        d_low = d_score.astype(BF16)
        d_table = tn(d_low, high[:nodes])
        s.dz[b] = nn(d_low, high) + d_table[:nodes]
        s.ysend[b, :, :, :head] = d_table[nodes:].reshape(nd, halo // nd, head)
        scatter_out(s.ysend.at[b], s.yrecv.at[b], 5 + b)

    def add_to(ref, value, b):
        if b == 0:
            ref[...] = value
        else:
            ref[...] += value

    def back_two(b):
        receive(5 + b)
        returned = s.yrecv[b].reshape(halo, LANES)[:, :head].astype(BF16)
        dz = s.dz[b] + tn(s.ohs[b], returned)
        s.sm[11:12, :head] += jnp.sum(dz, axis=0, keepdims=True)
        dz_low = dz.astype(BF16)
        add_to(s.gwh, nn(s.h2t[b], dz_low), b)
        d_out = nt(whb, dz_low)
        s.dres2[b] = d_out.astype(BF16)
        s.dmsg[:head, :] = d_out * (1.0 / HEADS)
        s.accb[...] += functools.reduce(
            jnp.add, [d_out[:, t * LANES : (t + 1) * LANES] for t in range(tiles)]
        )
        attend_back(1, b)
        s.dproj2[b, hid : 2 * hid, :] = s.dtgt[...].astype(BF16)
        s.dproj2[b, 2 * hid :, :] = s.dres2[b]
        s.gsend[b] = pack_rows(nt(s.oht[b, nodes:, :], s.dg[...]))
        scatter_out(s.gsend.at[b], s.grecv.at[b], 7 + b)
        s.dsrc[b] = nt(s.dg[...], s.oht[b, :nodes, :])

    def finish_two(b):
        receive(7 + b)
        returned = unpack_rows(s.grecv.at[b]).astype(BF16)
        s.dproj2[b, :hid, :] = (s.dsrc[b] + tn(returned, s.ohs[b])).astype(BF16)
        add_to(s.gw2, nt(s.dproj2[b], s.h1t[b]), b)
        s.dh[...] = nn(s.w2b[...], s.dproj2[b])

    def norm_back(b):
        for t in range(tiles):
            cols = slice(t * LANES, (t + 1) * LANES)
            normed = s.xhat[b, :, cols]
            n = normed * s.vb[2] + s.vb[3]
            dn = s.dh[:, cols] * jnp.where(n > 0.0, 1.0, jnp.exp(jnp.minimum(n, 0.0)))
            s.acc[3] += dn
            s.acc[2] += dn * normed
            dx = dn * s.vb[2]
            mean = jnp.sum(dx, axis=0, keepdims=True) * (1.0 / hid)
            along = jnp.sum(dx * normed, axis=0, keepdims=True) * (1.0 / hid)
            dy = s.rstd[b, 0:1, cols] * (dx - mean - normed * along)
            s.acc[1] += dy
            s.dmsg[:, cols] = dy
        add_to(s.gw1.at[2 * hid :, :], nn(s.dmsg[...].astype(BF16), s.fext[b, :nodes, :]), b)

    def weights_one(b):
        d_table = nt(s.dg[...], s.oht[b]).astype(BF16)
        add_to(s.gw1.at[:hid, :], nn(d_table, s.fext[b]), b)
        d_target = nn(s.dtgt[...].astype(BF16), s.fext[b, :nodes, :])
        add_to(s.gw1.at[hid : 2 * hid, :], d_target, b)

    def part(ref, index, count):
        return ref.at[aligned(index, count), :]

    def exchange(axis, number, src_of, dst, own=True):
        index, count = (me, nd) if axis == "dom" else (mine, nr)
        send_sem, recv_sem = s.send_sems.at[number], s.recv_sems.at[number]
        peers(
            axis,
            index,
            count,
            lambda peer: push(axis, peer, src_of(peer), dst.at[index], send_sem, recv_sem),
        )
        if own:
            pltpu.make_async_copy(src_of(index), dst.at[index], recv_sem).start()
            incoming[number] = dst
        else:
            incoming[number] = dst.at[pl.ds(0, count - 1)]
        outgoing.append((number, dst.at[pl.ds(0, count - 1)]))

    def summed(ref, count):
        return functools.reduce(jnp.add, [ref[i].astype(F32) for i in range(count)])

    in_one, in_two = 3 * hid, 2 * hid + head
    regions = [(i * in_two, s.gw2, slice(None), slice(i * LANES, (i + 1) * LANES)) for i in range(hid // LANES)]
    start = (hid // LANES) * in_two
    regions.append((start, s.gwh, slice(None), slice(None)))
    regions.append((start + head, s.gw1, slice(2 * hid, None), slice(None)))
    regions.append((bounds[-1] - 2 * hid, s.gw1, slice(0, 2 * hid), slice(None)))

    def spans(chunk):
        low, high = bounds[chunk], bounds[chunk + 1]
        for at, ref, rows, cols in regions:
            first, last, _ = rows.indices(ref.shape[0])
            begin, end = max(low, at), min(high, at + last - first)
            if begin < end:
                width = len(range(*cols.indices(ref.shape[1])))
                yield begin, end, ref, slice(first + begin - at, first + end - at), cols, width

    def pack(chunk):
        for begin, end, ref, rows, cols, width in spans(chunk):
            s.gb[begin:end, :width] = ref[rows, cols].astype(BF16)

    def chunk_of(chunk):
        return [getattr(s, f"{name}{chunk}") for name in ("rb", "gd", "rd", "fin", "ag")]

    def sum_rep(chunk):
        pack(chunk)
        low, high = bounds[chunk], bounds[chunk + 1]
        size = (high - low) // nr
        here = s.gb.at[low:high, :]
        exchange("rep", 11 + 4 * chunk, lambda peer: part(here, peer, size), chunk_of(chunk)[0])

    def sum_dom(chunk):
        rb, gd, rd, fin, ag = chunk_of(chunk)
        receive(11 + 4 * chunk)
        gd[...] = summed(rb, nr).astype(BF16)
        size = gd.shape[0] // nd
        exchange("dom", 12 + 4 * chunk, lambda peer: part(gd, peer, size), rd)

    def share_dom(chunk):
        rb, gd, rd, fin, ag = chunk_of(chunk)
        receive(12 + 4 * chunk)
        fin[...] = summed(rd, nd).astype(BF16)
        exchange("dom", 13 + 4 * chunk, lambda peer: fin, ag.at[mine])

    def share_rep(chunk):
        ag = chunk_of(chunk)[4]
        receive(13 + 4 * chunk)
        exchange("rep", 14 + 4 * chunk, lambda peer: ag.at[mine], ag, own=False)

    def vector_sum(j):
        total = jnp.sum(s.acc[j].T, axis=0, keepdims=True)
        for p in range(hid // LANES):
            row = (hid // LANES) * j + p
            s.sm[row : row + 1, :] = total[:, p * LANES : (p + 1) * LANES]

    def small_rep():
        exchange("rep", 9, lambda peer: s.sm, s.sm1)

    def small_dom():
        receive(9)
        s.sms[...] = summed(s.sm1, nr)
        exchange("dom", 10, lambda peer: s.sms, s.sm2)

    params = (w1, w2, wh, vec, bias)

    def update(index, grad, rows, cols):
        made = adamw(
            params[index][rows, cols], grad, firsts[index][rows, cols], seconds[index][rows, cols]
        )
        for offset in range(3):
            outs[1 + 3 * index + offset][rows, cols] = made[offset]

    def small_update():
        receive(10)
        total = summed(s.sm2, nd)
        outs[0][...] = total
        scale = 1.0 / total[13:14, 0:1]
        s.scale[...] = jnp.broadcast_to(scale, s.scale.shape)
        for j in range(5):
            for p in range(hid // LANES):
                row = (hid // LANES) * j + p
                cols = slice(p * LANES, (p + 1) * LANES)
                update(3, total[row : row + 1, :] * scale, slice(j, j + 1), cols)
        for j in range(2):
            update(4, total[10 + j : 11 + j, :head] * scale, slice(j, j + 1), slice(None))

    def chunk_update(chunk):
        ag = chunk_of(chunk)[4]
        receive(14 + 4 * chunk)
        low, high = bounds[chunk], bounds[chunk + 1]
        whole = ag[...].reshape(high - low, LANES)
        scale = s.scale[0:1, 0:1]
        for begin, end, ref, rows, cols, width in spans(chunk):
            if ref is s.gw1:
                for at in range(0, end - begin, LANES):
                    grad = whole[begin - low + at : begin - low + at + LANES].astype(F32).T * scale
                    update(0, grad, slice(None), slice(rows.start + at, rows.start + at + LANES))
            else:
                grad = whole[begin - low : end - low].astype(F32)[:, :width] * scale
                update(1 if ref is s.gw2 else 2, grad, rows, cols)

    s.zsend[...] = jnp.zeros_like(s.zsend)
    s.ysend[...] = jnp.zeros_like(s.ysend)
    s.gb[...] = jnp.zeros_like(s.gb)
    s.sm[13:14, 0:1] = 2.0 * jnp.sum(plive[...].astype(F32), axis=1, keepdims=True)
    receive(0)
    stages = [(stage, b) for stage in (layer_one, layer_two, pair_loss, back_two) for b in range(mb)]
    for stage, b in stages:
        stage(b)

    chunks = len(bounds) - 1
    split_sum = chunks == 3
    middle = tiles * HEADS // 2
    for b in range(mb):
        final = b == mb - 1
        finish_two(b)
        if final:
            if split_sum:
                sum_rep(0)
            vector_sum(4)
            s.sm[10:11, :head] = jnp.sum(s.accb[...].T, axis=0, keepdims=True)
        norm_back(b)
        if final and split_sum:
            sum_rep(1)
            for j in (1, 2, 3):
                vector_sum(j)
            attend_back(0, b, 0, middle)
            sum_dom(0)
            attend_back(0, b, middle)
        else:
            if final:
                for j in (1, 2, 3):
                    vector_sum(j)
            attend_back(0, b)
        weights_one(b)
    vector_sum(0)
    small_rep()
    sum_rep(chunks - 1)
    loaded(*range(12, 22))
    if split_sum:
        sum_dom(1)
        share_dom(0)
        small_dom()
        sum_dom(2)
        share_dom(1)
        share_rep(0)
        share_dom(2)
        share_rep(1)
        small_update()
        chunk_update(0)
        share_rep(2)
        chunk_update(1)
        chunk_update(2)
    else:
        small_dom()
        for chunk in range(chunks):
            sum_dom(chunk)
        for chunk in range(chunks):
            share_dom(chunk)
        for chunk in range(chunks):
            share_rep(chunk)
        small_update()
        for chunk in range(chunks):
            chunk_update(chunk)
    finish()


def adamw(param, grad, first, second):
    first = beta_one * first + (1.0 - beta_one) * grad
    second = beta_two * second + (1.0 - beta_two) * grad * grad
    fhat = first * (1.0 / (1.0 - beta_one**STEP))
    shat = second * (1.0 / (1.0 - beta_two**STEP))
    return (
        first,
        second,
        param - rate_step * (fhat / (jnp.sqrt(shat) + eps_adam) + decay_rate * param),
    )


def write_kernel(*refs):
    small, held, outs = refs[0], refs[1:16], refs[16:33]
    loss, count, sems = refs[33:]
    loss[...] = small[12:13, 0:1]
    count[...] = small[13:14, 0:1]
    copies = [
        pltpu.make_async_copy(src, dst, sems.at[i])
        for i, (src, dst) in enumerate(zip((loss, count) + held, outs))
    ]
    for copy in copies:
        copy.start()
    for copy in copies:
        copy.wait()


def body(nd, nr, *args):
    data, weights = args[:7], args[7:]
    features, edge_src, node_degree, send_rows, pair_src, pair_dst, pair_live = (
        a.reshape(a.shape[1:]) for a in data
    )
    mb, nodes, width = features.shape
    fan = edge_src.shape[-1]
    per = send_rows.shape[-1]
    halo = nd * per
    ext = nodes + halo
    pairs = pair_src.shape[-1]
    hid = weights[3].shape[1]
    head = weights[2].shape[0]
    in_one, in_two = 3 * hid, 2 * hid + head
    unit = nd * nr * 16
    early = (hid // LANES) * in_two
    rows_all = -(-(early + in_one + head) // unit) * unit
    bounds = (0, rows_all)
    middle = rows_all - 2 * hid
    if middle % unit == 0 and early >= unit and middle >= early + head + hid:
        bounds = (0, early // unit * unit, middle, rows_all)
    dims = (nd, nr, mb, nodes, fan, hid, head, ext, halo, pairs, bounds)
    chunks = {}
    for chunk in range(len(bounds) - 1):
        size = (bounds[chunk + 1] - bounds[chunk]) // nr
        chunks[f"rb{chunk}"] = pltpu.VMEM((nr, size, LANES), BF16)
        chunks[f"gd{chunk}"] = pltpu.VMEM((size, LANES), BF16)
        chunks[f"rd{chunk}"] = pltpu.VMEM((nd, size // nd, LANES), BF16)
        chunks[f"fin{chunk}"] = pltpu.VMEM((size // nd, LANES), BF16)
        chunks[f"ag{chunk}"] = pltpu.VMEM((nr, nd, size // nd, LANES), BF16)
    scratch = dict(
        ohs=pltpu.VMEM((mb, halo, nodes), BF16),
        fext=pltpu.VMEM((mb, ext, width), BF16),
        fsend=pltpu.VMEM((nd, mb * per, LANES), BF16),
        frecv=pltpu.VMEM((nd, mb * per, LANES), BF16),
        w1t=pltpu.VMEM((in_one, width), BF16),
        w2b=pltpu.VMEM((hid, in_two), BF16),
        w2t=pltpu.VMEM((in_two, hid), BF16),
        vb=pltpu.VMEM((5, hid, LANES), F32),
        bb=pltpu.VMEM((head, LANES), F32),
        acc=pltpu.VMEM((5, hid, LANES), F32),
        accb=pltpu.VMEM((head, LANES), F32),
        sm=pltpu.VMEM((16, LANES), F32),
        oht=pltpu.VMEM((mb, ext, fan * nodes), BF16),
        tgt=pltpu.VMEM((2, mb, hid, nodes), F32),
        res1=pltpu.VMEM((mb, hid, nodes), F32),
        res2=pltpu.VMEM((mb, head, nodes), F32),
        cpos=pltpu.VMEM((mb, nodes, ext), F32),
        cneg=pltpu.VMEM((mb, nodes, ext), F32),
        tab=pltpu.VMEM((mb, hid, ext), BF16),
        g=pltpu.VMEM((2, mb, hid, fan * nodes), F32),
        al=pltpu.VMEM((2, mb, (nodes // LANES) * HEADS, 16, LANES), F32),
        msg=pltpu.VMEM((hid, nodes), F32),
        xhat=pltpu.VMEM((mb, hid, nodes), F32),
        rstd=pltpu.VMEM((mb, 8, nodes), F32),
        h1t=pltpu.VMEM((mb, hid, nodes), BF16),
        hsend=pltpu.VMEM((mb, nd, 2 * per, LANES), BF16),
        hrecv=pltpu.VMEM((mb, nd, 2 * per, LANES), BF16),
        own2=pltpu.VMEM((mb, hid, nodes), BF16),
        h2=pltpu.VMEM((head, nodes), F32),
        h2t=pltpu.VMEM((mb, head, nodes), BF16),
        h2r=pltpu.VMEM((mb, ext, head), BF16),
        zsend=pltpu.VMEM((mb, nd, per, LANES), F32),
        zrecv=pltpu.VMEM((mb, nd, per, LANES), F32),
        ysend=pltpu.VMEM((mb, nd, per, LANES), F32),
        yrecv=pltpu.VMEM((mb, nd, per, LANES), F32),
        dz=pltpu.VMEM((mb, nodes, head), F32),
        dmsg=pltpu.VMEM((hid, nodes), F32),
        dres2=pltpu.VMEM((mb, head, nodes), BF16),
        dtgt=pltpu.VMEM((hid, nodes), F32),
        dg=pltpu.VMEM((hid, fan * nodes), BF16),
        dproj2=pltpu.VMEM((mb, in_two, nodes), BF16),
        dsrc=pltpu.VMEM((mb, hid, nodes), F32),
        gsend=pltpu.VMEM((mb, nd, 2 * per, LANES), BF16),
        grecv=pltpu.VMEM((mb, nd, 2 * per, LANES), BF16),
        dh=pltpu.VMEM((hid, nodes), F32),
        gw1=pltpu.VMEM((in_one, LANES), F32),
        gw2=pltpu.VMEM((in_two, hid), F32),
        gwh=pltpu.VMEM((head, head), F32),
        gb=pltpu.VMEM((rows_all, LANES), BF16),
        sm1=pltpu.VMEM((nr, 16, LANES), F32),
        sms=pltpu.VMEM((16, LANES), F32),
        sm2=pltpu.VMEM((nd, 16, LANES), F32),
        load_sems=pltpu.SemaphoreType.DMA((22,)),
        scale=pltpu.VMEM((8, LANES), F32),
        send_sems=pltpu.SemaphoreType.DMA((23,)),
        recv_sems=pltpu.SemaphoreType.DMA((23,)),
        **chunks,
    )
    operands = [features, edge_src.transpose(2, 0, 1), node_degree, send_rows, pair_src, pair_dst]
    operands.append(pair_live.T)
    operands += [w.T if i % 5 == 1 else w for i, w in enumerate(weights)]
    scalars = (jax.ShapeDtypeStruct((1, 1), F32),) * 2
    results = ()
    for operand in operands[7:12]:
        results += (jax.ShapeDtypeStruct(operand.shape, F32),) * 3
    whole = pl.BlockSpec(memory_space=pltpu.VMEM)
    anywhere = pl.BlockSpec(memory_space=pl.ANY)
    made = pl.pallas_call(
        functools.partial(step_kernel, dims, tuple(scratch)),
        out_shape=(jax.ShapeDtypeStruct((16, LANES), F32),) + results,
        in_specs=[anywhere] * 22,
        out_specs=(whole,) * 16,
        scratch_shapes=[pltpu.VMEM(a.shape, a.dtype) for a in operands] + list(scratch.values()),
        compiler_params=pltpu.CompilerParams(
            collective_id=0, has_side_effects=True, vmem_limit_bytes=44 * 1024 * 1024
        ),
    )(*(pltpu.with_memory_space_constraint(a, pltpu.HBM) for a in operands))
    made = pl.pallas_call(
        write_kernel,
        out_shape=scalars + results,
        in_specs=[whole] * 16,
        out_specs=(anywhere,) * 17,
        scratch_shapes=[pltpu.VMEM((1, 1), F32)] * 2 + [pltpu.SemaphoreType.DMA((17,))],
        compiler_params=pltpu.CompilerParams(vmem_limit_bytes=1024 * 1024),
    )(*made)
    loss, count = (a.reshape(()) for a in made[:2])
    return (loss, count) + tuple(a.T if i // 3 == 1 else a for i, a in enumerate(made[2:]))


def solution(mesh):
    sharded = (
        P("rep", None, "dom", None),
        P("rep", None, "dom", None),
        P("rep", None, "dom"),
        P("rep", None, "dom", None),
        P("rep", None, "dom"),
        P("rep", None, "dom"),
        P("rep", None, "dom"),
    )
    return jax.shard_map(
        functools.partial(body, mesh.shape["dom"], mesh.shape["rep"]),
        mesh=mesh,
        in_specs=sharded + (P(),) * 15,
        out_specs=(P(),) * 17,
        check_vma=False,
    )
```

```python
import functools
from types import SimpleNamespace

import jax
import jax.numpy as jnp
from jax import lax
from jax.experimental import pallas as pl
from jax.experimental.pallas import tpu as pltpu
from jax.sharding import PartitionSpec as P

HEADS = 4
STEP = 5
LANES = 128

eps_norm = 1e-05
beta_one = 0.9
beta_two = 0.999
rate_step = 0.05
decay_rate = 0.01
eps_adam = 1e-08

F32 = jnp.float32
BF16 = jnp.bfloat16
MESH = pl.DeviceIdType.MESH


def contract(left, right, left_dim, right_dim):
    return lax.dot_general(
        left, right, (((left_dim,), (right_dim,)), ((), ())), preferred_element_type=F32
    )


def nn(left, right):
    return contract(left, right, 1, 0)


def nt(left, right):
    return contract(left, right, 1, 1)


def tn(left, right):
    return contract(left, right, 0, 0)


def split(value):
    high = value.astype(BF16)
    return high, (value - high.astype(F32)).astype(BF16)


def sigmoid(value):
    return 0.5 * jnp.tanh(0.5 * value) + 0.5


def row_iota(rows, columns):
    return lax.broadcasted_iota(jnp.int32, (rows, columns), 0)


def lane_iota(rows, columns):
    return lax.broadcasted_iota(jnp.int32, (rows, columns), 1)


def aligned(index, size):
    return pl.ds(pl.multiple_of(index * size, size), size)


def step_kernel(dims, names, *refs):
    held, outs, rest_refs = refs[:22], refs[22:38], refs[38:]
    staged = rest_refs[:22]
    s = SimpleNamespace(**dict(zip(names, rest_refs[22:])))
    (feats, edges, degree, sends, psrc, pdst, plive, w1, w2, wh, vec, bias) = staged[:12]
    firsts, seconds = staged[12:17], staged[17:22]
    nd, nr, mb, nodes, fan, hid, head, ext, halo, pairs, bounds = dims
    half = pairs // 2
    tiles = nodes // LANES
    me = lax.axis_index("dom")
    mine = lax.axis_index("rep")

    def peers(axis, index, count, send):
        def one(step, carry):
            send(lax.rem(index + step, count))
            return carry

        lax.fori_loop(1, count, one, 0)

    def others(send):
        def one(step, carry):
            at = lax.rem(me * nr + mine + step, nd * nr)
            send({"dom": lax.div(at, nr), "rep": lax.rem(at, nr)})
            return carry

        lax.fori_loop(1, nd * nr, one, 0)

    def push(there, src, dst, send_sem, recv_sem):
        pltpu.make_async_remote_copy(
            src_ref=src,
            dst_ref=dst,
            send_sem=send_sem,
            recv_sem=recv_sem,
            device_id=there,
            device_id_type=MESH,
        ).start()

    incoming, outgoing = {}, []

    def arrived(ref, sem):
        pltpu.make_async_copy(ref, ref, sem).wait()

    def receive(number):
        arrived(incoming.pop(number), s.recv_sems.at[number])

    def finish():
        for number in list(incoming):
            receive(number)
        for number, ref in outgoing:
            arrived(ref, s.send_sems.at[number])

    def load(*which):
        for i in which:
            pltpu.make_async_copy(held[i], staged[i], s.load_sems.at[i]).start()

    def loaded(*which):
        for i in which:
            arrived(staged[i], s.load_sems.at[i])

    def scatter_out(src, dst, number):
        send_sem, recv_sem = s.send_sems.at[number], s.recv_sems.at[number]
        peers(
            "dom",
            me,
            nd,
            lambda peer: push({"dom": peer}, src.at[peer], dst.at[me], send_sem, recv_sem),
        )
        pltpu.make_async_copy(src.at[me], dst.at[me], recv_sem).start()
        incoming[number] = dst
        outgoing.append((number, src.at[pl.ds(0, nd - 1)]))

    load(3, 0)
    barrier = pltpu.get_barrier_semaphore()
    others(lambda there: pl.semaphore_signal(barrier, inc=1, device_id=there, device_id_type=MESH))
    load(7, 8, 9, 10, 11, 1, 2, 4, 5, 6)
    loaded(3, 0)
    for b in range(mb):
        spread = (
            lax.div(row_iota(halo, nd), halo // nd) == lane_iota(halo, nd)
        ).astype(F32).astype(BF16)
        listed = nn(spread, sends[b].astype(F32).astype(BF16))
        pick = lax.rem(row_iota(halo, halo // nd), halo // nd) == lane_iota(halo, halo // nd)
        column = jnp.sum(jnp.where(pick, listed, 0.0), axis=1, keepdims=True)
        s.ohs[b] = (lane_iota(halo, nodes).astype(F32) == column).astype(F32).astype(BF16)
        s.fext[b, :nodes, :] = feats[b].astype(BF16)

    parts = [
        nn(s.ohs[b], s.fext[b, :nodes, :]).reshape(nd, halo // nd, LANES) for b in range(mb)
    ]
    s.fsend[...] = jnp.concatenate(parts, axis=1).astype(BF16)
    pl.semaphore_wait(barrier, nd * nr - 1)
    scatter_out(s.fsend, s.frecv, 0)
    load(*range(12, 22))

    loaded(7, 8, 9, 10, 11)
    s.w1t[...] = w1[...].T.astype(BF16)
    s.w2t[...] = w2[...].astype(BF16)
    s.w2b[...] = w2[...].T.astype(BF16)
    whb = wh[...].astype(BF16)
    for j in range(5):
        s.vb[j] = jnp.broadcast_to(vec[j : j + 1, :], (LANES, hid)).T
    s.bb[...] = jnp.broadcast_to(bias[0:1, :], (LANES, head)).T
    s.acc[...] = jnp.zeros_like(s.acc)
    s.accb[...] = jnp.zeros_like(s.accb)
    s.sm[...] = jnp.zeros_like(s.sm)
    loaded(1, 2, 4, 5, 6)

    for b in range(mb):

        def one_hot(k, carry):
            index = edges[k, b : b + 1, :]
            s.oht[b, :, aligned(k, nodes)] = (
                (row_iota(ext, nodes) == index).astype(F32).astype(BF16)
            )
            return carry

        lax.fori_loop(0, fan, one_hot, 0)

        s.tab[b, :, :nodes] = nt(s.w1t[:hid, :], s.fext[b, :nodes, :]).astype(BF16)
        rest = nt(s.w1t[hid:, :], s.fext[b, :nodes, :])
        s.tgt[0, b] = rest[:hid]
        s.res1[b] = rest[hid:]

        slot = lax.rem(lane_iota(1, pairs), half)
        count = jnp.sum(
            jnp.where(lane_iota(1, mb) == b, plive[...].astype(F32), 0.0), axis=1, keepdims=True
        )
        live = slot.astype(F32) < count
        from_src = (row_iota(nodes, pairs) == psrc[b : b + 1, :]).astype(F32).astype(BF16)
        to_dst = (
            ((row_iota(ext, pairs) == pdst[b : b + 1, :]) & live).astype(F32).astype(BF16)
        )
        s.cpos[b] = nt(from_src[:, :half], to_dst[:, :half])
        s.cneg[b] = nt(from_src[:, half:], to_dst[:, half:])

    def place(index):
        tile, which = divmod(index, HEADS)
        rows = slice(which * head, (which + 1) * head)
        return tile, rows, slice(tile * LANES, (tile + 1) * LANES)

    def slot_at(k, tile):
        return slice(k * nodes + tile * LANES, k * nodes + (tile + 1) * LANES)

    def attend(layer, b):
        att = 0 if layer == 0 else 4
        s.g[layer, b] = nn(s.tab[b], s.oht[b])

        for index in range(tiles * HEADS):
            tile, rows, cols = place(index)
            target = s.tgt[layer, b, rows, cols]
            weight = s.vb[att, rows, :]
            count = degree[b : b + 1, cols]
            scores = []
            for k in range(fan):
                u = s.g[layer, b, rows, slot_at(k, tile)] + target
                mixed = u * sigmoid(u)
                score = jnp.sum(mixed * weight, axis=0, keepdims=True)
                scores.append(jnp.where(count > k, score, -1e30))
            top = functools.reduce(jnp.maximum, scores)
            weights = [
                jnp.where(count > k, jnp.exp(scores[k] - top), 0.0) for k in range(fan)
            ]
            inverse = 1.0 / functools.reduce(jnp.add, weights)
            message = jnp.zeros((head, LANES), F32)
            for k in range(fan):
                alpha = weights[k] * inverse
                s.al[layer, b, index, k : k + 1, :] = alpha
                message = message + alpha * s.g[layer, b, rows, slot_at(k, tile)]
            s.msg[rows, cols] = message

    def attend_back(layer, b, first=0, last=None):
        att = 0 if layer == 0 else 4

        for index in range(first, tiles * HEADS if last is None else last):
            tile, rows, cols = place(index)
            target = s.tgt[layer, b, rows, cols]
            weight = s.vb[att, rows, :]
            if layer == 0:
                d_message = s.dmsg[rows, cols]
            else:
                d_message = s.dmsg[:head, cols]
            alphas = [s.al[layer, b, index, k : k + 1, :] for k in range(fan)]
            d_alphas = [
                jnp.sum(d_message * s.g[layer, b, rows, slot_at(k, tile)], axis=0, keepdims=True)
                for k in range(fan)
            ]
            total = functools.reduce(jnp.add, [a * d for a, d in zip(alphas, d_alphas)])
            d_target = jnp.zeros((head, LANES), F32)
            d_att = jnp.zeros((head, LANES), F32)
            for k in range(fan):
                d_score = alphas[k] * (d_alphas[k] - total)
                u = s.g[layer, b, rows, slot_at(k, tile)] + target
                gate = sigmoid(u)
                mixed = u * gate
                slope = gate * (1.0 + (u - mixed))
                d_u = (d_score * weight) * slope
                d_target = d_target + d_u
                d_att = d_att + d_score * mixed
                s.dg[rows, slot_at(k, tile)] = (alphas[k] * d_message + d_u).astype(BF16)
            s.dtgt[rows, cols] = d_target
            s.acc[att, rows, :] += d_att

    def pack_rows(value):
        blocks = value.reshape(nd, halo // nd, hid)
        return jnp.concatenate([blocks[:, :, :LANES], blocks[:, :, LANES:]], axis=1).astype(BF16)

    def unpack_rows(ref):
        blocks = ref[...].astype(F32)
        per = halo // nd
        return jnp.concatenate([blocks[:, :per, :], blocks[:, per:, :]], axis=2).reshape(halo, hid)

    def layer_one(b):
        s.fext[b, nodes:, :] = (
            s.frecv[...].astype(F32)[:, b * (halo // nd) : (b + 1) * (halo // nd), :]
            .reshape(halo, LANES)
            .astype(BF16)
        )
        s.tab[b, :, nodes:] = nt(s.w1t[:hid, :], s.fext[b, nodes:, :]).astype(BF16)
        attend(0, b)
        for t in range(tiles):
            cols = slice(t * LANES, (t + 1) * LANES)
            y = s.msg[:, cols] + s.vb[1] + s.res1[b, :, cols]
            centred = y - jnp.sum(y, axis=0, keepdims=True) * (1.0 / hid)
            spread = jnp.sum(centred * centred, axis=0, keepdims=True) * (1.0 / hid)
            rstd = lax.rsqrt(spread + eps_norm)
            normed = centred * rstd
            s.xhat[b, :, cols] = normed
            s.rstd[b, 0:1, cols] = rstd
            n = normed * s.vb[2] + s.vb[3]
            s.h1t[b, :, cols] = jnp.where(n > 0.0, n, jnp.exp(jnp.minimum(n, 0.0)) - 1.0).astype(BF16)
        s.hsend[b] = pack_rows(nt(s.ohs[b], s.h1t[b]))
        scatter_out(s.hsend.at[b], s.hrecv.at[b], 1 + b)
        own = nn(s.w2t[...], s.h1t[b])
        s.own2[b] = own[:hid].astype(BF16)
        s.tgt[1, b] = own[hid : 2 * hid]
        s.res2[b] = own[2 * hid :]

    def layer_two(b):
        receive(1 + b)
        s.tab[b, :, :nodes] = s.own2[b]
        s.tab[b, :, nodes:] = nt(s.w2t[:hid, :], unpack_rows(s.hrecv.at[b]).astype(BF16)).astype(BF16)
        attend(1, b)
        for t in range(tiles):
            cols = slice(t * LANES, (t + 1) * LANES)
            message = functools.reduce(
                jnp.add, [s.msg[h * head : (h + 1) * head, cols] for h in range(HEADS)]
            )
            s.h2[:, cols] = message * (1.0 / HEADS) + s.bb[...] + s.res2[b, :, cols]
        s.h2t[b] = s.h2[...].astype(BF16)
        rows = nt(s.ohs[b], s.h2t[b])
        s.zsend[b, :, :, :head] = rows.reshape(nd, halo // nd, head)
        scatter_out(s.zsend.at[b], s.zrecv.at[b], 3 + b)
        s.h2r[b] = s.h2[...].T.astype(BF16)

    def pair_terms(score, pos, neg):
        small = jnp.exp(-jnp.abs(score))
        terms = (
            (pos + neg) * jnp.log1p(small)
            + pos * jnp.maximum(-score, 0.0)
            + neg * jnp.maximum(score, 0.0)
        )
        s.sm[12:13, 0:1] += jnp.sum(jnp.sum(terms, axis=0, keepdims=True), axis=1, keepdims=True)
        big = 1.0 / (1.0 + small)
        little = small * big
        up = score > 0.0
        return (neg * jnp.where(up, big, little) - pos * jnp.where(up, little, big)).astype(BF16)

    def pair_own(b):
        high, low = split(nn(s.h2r[b], whb) + bias[1:2, :])
        s.left[b] = jnp.concatenate([high, high, low], axis=1)
        score = nt(s.left[b], jnp.concatenate([high, low, high], axis=1))
        d_score = pair_terms(score, s.cpos[b, :, :nodes], s.cneg[b, :, :nodes])
        s.dz[b] = nn(d_score, high) + tn(d_score, high)

    def pair_halo(b):
        receive(3 + b)
        rows = s.zrecv[b].reshape(halo, LANES)[:, :head].astype(BF16)
        high, low = split(nn(rows, whb) + bias[1:2, :])
        score = nt(s.left[b], jnp.concatenate([high, low, high], axis=1))
        d_score = pair_terms(score, s.cpos[b, :, nodes:], s.cneg[b, :, nodes:])
        s.ysend[b, :, :, :head] = tn(d_score, s.left[b, :, :head]).reshape(nd, halo // nd, head)
        scatter_out(s.ysend.at[b], s.yrecv.at[b], 5 + b)
        s.dz[b] += nn(d_score, high)

    def add_to(ref, value, b):
        if b == 0:
            ref[...] = value
        else:
            ref[...] += value

    def back_two(b):
        receive(5 + b)
        returned = s.yrecv[b].reshape(halo, LANES)[:, :head].astype(BF16)
        dz = s.dz[b] + tn(s.ohs[b], returned)
        s.sm[11:12, :head] += jnp.sum(dz, axis=0, keepdims=True)
        dz_low = dz.astype(BF16)
        d_out = nt(whb, dz_low)
        s.dmsg[:head, :] = d_out * (1.0 / HEADS)
        s.dproj2[b, 2 * hid :, :] = d_out.astype(BF16)
        attend_back(1, b)
        d_table = nt(s.dg[...], s.oht[b])
        s.gsend[b] = pack_rows(d_table[:, nodes:].T)
        scatter_out(s.gsend.at[b], s.grecv.at[b], 7 + b)
        s.dsrc[b] = d_table[:, :nodes]
        s.dproj2[b, hid : 2 * hid, :] = s.dtgt[...].astype(BF16)
        s.dhp[b] = nn(s.w2b[:, hid:], s.dproj2[b, hid:, :])
        add_to(s.gw2.at[hid:, :], nt(s.dproj2[b, hid:, :], s.h1t[b]), b)
        add_to(s.gwh, nn(s.h2t[b], dz_low), b)
        s.accb[...] += functools.reduce(
            jnp.add, [d_out[:, t * LANES : (t + 1) * LANES] for t in range(tiles)]
        )

    def finish_two(b):
        receive(7 + b)
        returned = unpack_rows(s.grecv.at[b]).astype(BF16)
        s.dproj2[b, :hid, :] = (s.dsrc[b] + tn(returned, s.ohs[b])).astype(BF16)
        s.dh[...] = s.dhp[b] + nn(s.w2b[:, :hid], s.dproj2[b, :hid, :])
        add_to(s.gw2.at[:hid, :], nt(s.dproj2[b, :hid, :], s.h1t[b]), b)

    def norm_back(b):
        for t in range(tiles):
            cols = slice(t * LANES, (t + 1) * LANES)
            normed = s.xhat[b, :, cols]
            n = normed * s.vb[2] + s.vb[3]
            dn = s.dh[:, cols] * jnp.where(n > 0.0, 1.0, jnp.exp(jnp.minimum(n, 0.0)))
            s.acc[3] += dn
            s.acc[2] += dn * normed
            dx = dn * s.vb[2]
            mean = jnp.sum(dx, axis=0, keepdims=True) * (1.0 / hid)
            along = jnp.sum(dx * normed, axis=0, keepdims=True) * (1.0 / hid)
            dy = s.rstd[b, 0:1, cols] * (dx - mean - normed * along)
            s.acc[1] += dy
            s.dmsg[:, cols] = dy
        add_to(s.gw1.at[2 * hid :, :], nn(s.dmsg[...].astype(BF16), s.fext[b, :nodes, :]), b)

    def weights_one(b):
        d_table = nt(s.dg[...], s.oht[b]).astype(BF16)
        add_to(s.gw1.at[:hid, :], nn(d_table, s.fext[b]), b)
        d_target = nn(s.dtgt[...].astype(BF16), s.fext[b, :nodes, :])
        add_to(s.gw1.at[hid : 2 * hid, :], d_target, b)

    def part(ref, index, count):
        return ref.at[aligned(index, count), :]

    def exchange(axis, number, src_of, dst, own=True):
        index, count = (me, nd) if axis == "dom" else (mine, nr)
        send_sem, recv_sem = s.send_sems.at[number], s.recv_sems.at[number]
        peers(
            axis,
            index,
            count,
            lambda peer: push({axis: peer}, src_of(peer), dst.at[index], send_sem, recv_sem),
        )
        if own:
            pltpu.make_async_copy(src_of(index), dst.at[index], recv_sem).start()
            incoming[number] = dst
        else:
            incoming[number] = dst.at[pl.ds(0, count - 1)]
        outgoing.append((number, dst.at[pl.ds(0, count - 1)]))

    def summed(ref, count):
        return functools.reduce(jnp.add, [ref[i].astype(F32) for i in range(count)])

    chunks = len(bounds) - 1
    in_one, in_two = 3 * hid, 2 * hid + head
    regions = [(i * in_two, s.gw2, slice(None), slice(i * LANES, (i + 1) * LANES)) for i in range(hid // LANES)]
    start = (hid // LANES) * in_two
    regions.append((start, s.gwh, slice(None), slice(None)))
    regions.append((start + head, s.gw1, slice(2 * hid, None), slice(None)))
    regions.append((bounds[-1] - 2 * hid, s.gw1, slice(0, 2 * hid), slice(None)))

    def spans(chunk):
        low, high = bounds[chunk], bounds[chunk + 1]
        for at, ref, rows, cols in regions:
            first, last, _ = rows.indices(ref.shape[0])
            begin, end = max(low, at), min(high, at + last - first)
            if begin < end:
                width = len(range(*cols.indices(ref.shape[1])))
                yield begin, end, ref, slice(first + begin - at, first + end - at), cols, width

    def pack(chunk):
        for begin, end, ref, rows, cols, width in spans(chunk):
            s.gb[begin:end, :width] = ref[rows, cols].astype(BF16)

    def chunk_of(chunk):
        return [getattr(s, f"{name}{chunk}") for name in ("rb", "gd", "rd", "fin", "ag")]

    def sum_rep(chunk):
        pack(chunk)
        low, high = bounds[chunk], bounds[chunk + 1]
        size = (high - low) // nr
        here = s.gb.at[low:high, :]
        exchange("rep", 11 + 4 * chunk, lambda peer: part(here, peer, size), chunk_of(chunk)[0])

    def sum_dom(chunk):
        rb, gd, rd, fin, ag = chunk_of(chunk)
        receive(11 + 4 * chunk)
        gd[...] = summed(rb, nr).astype(BF16)
        size = gd.shape[0] // nd
        exchange("dom", 12 + 4 * chunk, lambda peer: part(gd, peer, size), rd)

    def share_dom(chunk):
        rb, gd, rd, fin, ag = chunk_of(chunk)
        receive(12 + 4 * chunk)
        fin[...] = summed(rd, nd).astype(BF16)
        exchange("dom", 13 + 4 * chunk, lambda peer: fin, ag.at[mine])

    def share_rep(chunk):
        ag = chunk_of(chunk)[4]
        receive(13 + 4 * chunk)
        exchange("rep", 14 + 4 * chunk, lambda peer: ag.at[mine], ag, own=False)

    def exchange_all(number, src_of, dst):
        index = me * nr + mine
        send_sem, recv_sem = s.send_sems.at[number], s.recv_sems.at[number]
        others(
            lambda there: push(
                there, src_of(there["dom"] * nr + there["rep"]), dst.at[index], send_sem, recv_sem
            )
        )
        pltpu.make_async_copy(src_of(index), dst.at[index], recv_sem).start()
        incoming[number] = dst
        outgoing.append((number, dst.at[pl.ds(0, nd * nr - 1)]))

    def sum_all():
        pack(chunks - 1)
        size = (bounds[-1] - bounds[-2]) // (nd * nr)
        here = s.gb.at[bounds[-2] : bounds[-1], :]
        exchange_all(19, lambda at: part(here, at, size), s.rl)

    def share_all():
        receive(19)
        s.finl[...] = summed(s.rl, nd * nr).astype(BF16)
        exchange_all(20, lambda at: s.finl, s.agl)

    def vector_sum(j):
        total = jnp.sum(s.acc[j].T, axis=0, keepdims=True)
        for p in range(hid // LANES):
            row = (hid // LANES) * j + p
            s.sm[row : row + 1, :] = total[:, p * LANES : (p + 1) * LANES]

    def small_rep():
        exchange("rep", 9, lambda peer: s.sm, s.sm1)

    def small_dom():
        receive(9)
        s.sms[...] = summed(s.sm1, nr)
        exchange("dom", 10, lambda peer: s.sms, s.sm2)

    params = (w1, w2, wh, vec, bias)

    def update(index, grad, rows, cols):
        made = adamw(
            params[index][rows, cols], grad, firsts[index][rows, cols], seconds[index][rows, cols]
        )
        for offset in range(3):
            outs[1 + 3 * index + offset][rows, cols] = made[offset]

    def small_update():
        receive(10)
        total = summed(s.sm2, nd)
        outs[0][...] = total
        scale = 1.0 / total[13:14, 0:1]
        s.scale[...] = jnp.broadcast_to(scale, s.scale.shape)
        for j in range(5):
            for p in range(hid // LANES):
                row = (hid // LANES) * j + p
                cols = slice(p * LANES, (p + 1) * LANES)
                update(3, total[row : row + 1, :] * scale, slice(j, j + 1), cols)
        for j in range(2):
            update(4, total[10 + j : 11 + j, :head] * scale, slice(j, j + 1), slice(None))

    def chunk_update(chunk):
        ag = s.agl if chunk == chunks - 1 else chunk_of(chunk)[4]
        receive(20 if chunk == chunks - 1 else 14 + 4 * chunk)
        low, high = bounds[chunk], bounds[chunk + 1]
        whole = ag[...].reshape(high - low, LANES)
        scale = s.scale[0:1, 0:1]
        for begin, end, ref, rows, cols, width in spans(chunk):
            if ref is s.gw1:
                for at in range(0, end - begin, LANES):
                    grad = whole[begin - low + at : begin - low + at + LANES].astype(F32).T * scale
                    update(0, grad, slice(None), slice(rows.start + at, rows.start + at + LANES))
            else:
                grad = whole[begin - low : end - low].astype(F32)[:, :width] * scale
                update(1 if ref is s.gw2 else 2, grad, rows, cols)

    s.zsend[...] = jnp.zeros_like(s.zsend)
    s.ysend[...] = jnp.zeros_like(s.ysend)
    s.gb[...] = jnp.zeros_like(s.gb)
    s.sm[13:14, 0:1] = 2.0 * jnp.sum(plive[...].astype(F32), axis=1, keepdims=True)
    receive(0)
    stages = [(stage, b) for stage in (layer_one, layer_two, pair_own, pair_halo, back_two) for b in range(mb)]
    for stage, b in stages:
        stage(b)

    split_sum = chunks == 3
    middle = tiles * HEADS // 2
    for b in range(mb):
        final = b == mb - 1
        finish_two(b)
        if final:
            if split_sum:
                sum_rep(0)
            vector_sum(4)
            s.sm[10:11, :head] = jnp.sum(s.accb[...].T, axis=0, keepdims=True)
        norm_back(b)
        if final and split_sum:
            sum_rep(1)
            for j in (1, 2, 3):
                vector_sum(j)
            attend_back(0, b, 0, middle)
            sum_dom(0)
            attend_back(0, b, middle)
        else:
            if final:
                for j in (1, 2, 3):
                    vector_sum(j)
            attend_back(0, b)
        weights_one(b)
    sum_all()
    vector_sum(0)
    small_rep()
    loaded(*range(12, 22))
    if split_sum:
        sum_dom(1)
        share_dom(0)
        small_dom()
        share_dom(1)
    else:
        small_dom()
    share_all()
    if split_sum:
        share_rep(0)
        share_rep(1)
    small_update()
    for chunk in range(chunks):
        chunk_update(chunk)
    finish()


def adamw(param, grad, first, second):
    first = beta_one * first + (1.0 - beta_one) * grad
    second = beta_two * second + (1.0 - beta_two) * grad * grad
    fhat = first * (1.0 / (1.0 - beta_one**STEP))
    shat = second * (1.0 / (1.0 - beta_two**STEP))
    return (
        first,
        second,
        param - rate_step * (fhat / (jnp.sqrt(shat) + eps_adam) + decay_rate * param),
    )


def write_kernel(*refs):
    small, held, outs = refs[0], refs[1:16], refs[16:33]
    loss, count, sems = refs[33:]
    loss[...] = small[12:13, 0:1]
    count[...] = small[13:14, 0:1]
    copies = [
        pltpu.make_async_copy(src, dst, sems.at[i])
        for i, (src, dst) in enumerate(zip((loss, count) + held, outs))
    ]
    for copy in copies:
        copy.start()
    for copy in copies:
        copy.wait()


def body(nd, nr, *args):
    data, weights = args[:7], args[7:]
    features, edge_src, node_degree, send_rows, pair_src, pair_dst, pair_live = (
        a.reshape(a.shape[1:]) for a in data
    )
    mb, nodes, width = features.shape
    fan = edge_src.shape[-1]
    per = send_rows.shape[-1]
    halo = nd * per
    ext = nodes + halo
    pairs = pair_src.shape[-1]
    hid = weights[3].shape[1]
    head = weights[2].shape[0]
    in_one, in_two = 3 * hid, 2 * hid + head
    unit = nd * nr * 16
    early = (hid // LANES) * in_two
    rows_all = -(-(early + in_one + head) // unit) * unit
    bounds = (0, rows_all)
    middle = rows_all - 2 * hid
    if middle % unit == 0 and early >= unit and middle >= early + head + hid:
        bounds = (0, early // unit * unit, middle, rows_all)
    dims = (nd, nr, mb, nodes, fan, hid, head, ext, halo, pairs, bounds)
    chunks = {}
    last = bounds[-1] - bounds[-2]
    for name in ("rl", "agl"):
        chunks[name] = pltpu.VMEM((nd * nr, last // (nd * nr), LANES), BF16)
    chunks["finl"] = pltpu.VMEM((last // (nd * nr), LANES), BF16)
    for chunk in range(len(bounds) - 2):
        size = (bounds[chunk + 1] - bounds[chunk]) // nr
        chunks[f"rb{chunk}"] = pltpu.VMEM((nr, size, LANES), BF16)
        chunks[f"gd{chunk}"] = pltpu.VMEM((size, LANES), BF16)
        chunks[f"rd{chunk}"] = pltpu.VMEM((nd, size // nd, LANES), BF16)
        chunks[f"fin{chunk}"] = pltpu.VMEM((size // nd, LANES), BF16)
        chunks[f"ag{chunk}"] = pltpu.VMEM((nr, nd, size // nd, LANES), BF16)
    scratch = dict(
        ohs=pltpu.VMEM((mb, halo, nodes), BF16),
        fext=pltpu.VMEM((mb, ext, width), BF16),
        fsend=pltpu.VMEM((nd, mb * per, LANES), BF16),
        frecv=pltpu.VMEM((nd, mb * per, LANES), BF16),
        w1t=pltpu.VMEM((in_one, width), BF16),
        w2b=pltpu.VMEM((hid, in_two), BF16),
        w2t=pltpu.VMEM((in_two, hid), BF16),
        vb=pltpu.VMEM((5, hid, LANES), F32),
        bb=pltpu.VMEM((head, LANES), F32),
        acc=pltpu.VMEM((5, hid, LANES), F32),
        accb=pltpu.VMEM((head, LANES), F32),
        sm=pltpu.VMEM((16, LANES), F32),
        oht=pltpu.VMEM((mb, ext, fan * nodes), BF16),
        tgt=pltpu.VMEM((2, mb, hid, nodes), F32),
        res1=pltpu.VMEM((mb, hid, nodes), F32),
        res2=pltpu.VMEM((mb, head, nodes), F32),
        cpos=pltpu.VMEM((mb, nodes, ext), F32),
        cneg=pltpu.VMEM((mb, nodes, ext), F32),
        tab=pltpu.VMEM((mb, hid, ext), BF16),
        g=pltpu.VMEM((2, mb, hid, fan * nodes), F32),
        al=pltpu.VMEM((2, mb, (nodes // LANES) * HEADS, 16, LANES), F32),
        msg=pltpu.VMEM((hid, nodes), F32),
        xhat=pltpu.VMEM((mb, hid, nodes), F32),
        rstd=pltpu.VMEM((mb, 8, nodes), F32),
        h1t=pltpu.VMEM((mb, hid, nodes), BF16),
        hsend=pltpu.VMEM((mb, nd, 2 * per, LANES), BF16),
        hrecv=pltpu.VMEM((mb, nd, 2 * per, LANES), BF16),
        own2=pltpu.VMEM((mb, hid, nodes), BF16),
        h2=pltpu.VMEM((head, nodes), F32),
        h2t=pltpu.VMEM((mb, head, nodes), BF16),
        h2r=pltpu.VMEM((mb, nodes, head), BF16),
        left=pltpu.VMEM((mb, nodes, 3 * head), BF16),
        dhp=pltpu.VMEM((mb, hid, nodes), F32),
        zsend=pltpu.VMEM((mb, nd, per, LANES), F32),
        zrecv=pltpu.VMEM((mb, nd, per, LANES), F32),
        ysend=pltpu.VMEM((mb, nd, per, LANES), F32),
        yrecv=pltpu.VMEM((mb, nd, per, LANES), F32),
        dz=pltpu.VMEM((mb, nodes, head), F32),
        dmsg=pltpu.VMEM((hid, nodes), F32),
        dtgt=pltpu.VMEM((hid, nodes), F32),
        dg=pltpu.VMEM((hid, fan * nodes), BF16),
        dproj2=pltpu.VMEM((mb, in_two, nodes), BF16),
        dsrc=pltpu.VMEM((mb, hid, nodes), F32),
        gsend=pltpu.VMEM((mb, nd, 2 * per, LANES), BF16),
        grecv=pltpu.VMEM((mb, nd, 2 * per, LANES), BF16),
        dh=pltpu.VMEM((hid, nodes), F32),
        gw1=pltpu.VMEM((in_one, LANES), F32),
        gw2=pltpu.VMEM((in_two, hid), F32),
        gwh=pltpu.VMEM((head, head), F32),
        gb=pltpu.VMEM((rows_all, LANES), BF16),
        sm1=pltpu.VMEM((nr, 16, LANES), F32),
        sms=pltpu.VMEM((16, LANES), F32),
        sm2=pltpu.VMEM((nd, 16, LANES), F32),
        load_sems=pltpu.SemaphoreType.DMA((22,)),
        scale=pltpu.VMEM((8, LANES), F32),
        send_sems=pltpu.SemaphoreType.DMA((21,)),
        recv_sems=pltpu.SemaphoreType.DMA((21,)),
        **chunks,
    )
    operands = [features, edge_src.transpose(2, 0, 1), node_degree, send_rows, pair_src, pair_dst]
    operands.append(pair_live.T)
    operands += [w.T if i % 5 == 1 else w for i, w in enumerate(weights)]
    scalars = (jax.ShapeDtypeStruct((1, 1), F32),) * 2
    results = ()
    for operand in operands[7:12]:
        results += (jax.ShapeDtypeStruct(operand.shape, F32),) * 3
    whole = pl.BlockSpec(memory_space=pltpu.VMEM)
    anywhere = pl.BlockSpec(memory_space=pl.ANY)
    made = pl.pallas_call(
        functools.partial(step_kernel, dims, tuple(scratch)),
        out_shape=(jax.ShapeDtypeStruct((16, LANES), F32),) + results,
        in_specs=[anywhere] * 22,
        out_specs=(whole,) * 16,
        scratch_shapes=[pltpu.VMEM(a.shape, a.dtype) for a in operands] + list(scratch.values()),
        compiler_params=pltpu.CompilerParams(
            collective_id=0, has_side_effects=True, vmem_limit_bytes=44 * 1024 * 1024
        ),
    )(*(pltpu.with_memory_space_constraint(a, pltpu.HBM) for a in operands))
    made = pl.pallas_call(
        write_kernel,
        out_shape=scalars + results,
        in_specs=[whole] * 16,
        out_specs=(anywhere,) * 17,
        scratch_shapes=[pltpu.VMEM((1, 1), F32)] * 2 + [pltpu.SemaphoreType.DMA((17,))],
        compiler_params=pltpu.CompilerParams(vmem_limit_bytes=1024 * 1024),
    )(*made)
    loss, count = (a.reshape(()) for a in made[:2])
    return (loss, count) + tuple(a.T if i // 3 == 1 else a for i, a in enumerate(made[2:]))


def solution(mesh):
    sharded = (
        P("rep", None, "dom", None),
        P("rep", None, "dom", None),
        P("rep", None, "dom"),
        P("rep", None, "dom", None),
        P("rep", None, "dom"),
        P("rep", None, "dom"),
        P("rep", None, "dom"),
    )
    return jax.shard_map(
        functools.partial(body, mesh.shape["dom"], mesh.shape["rep"]),
        mesh=mesh,
        in_specs=sharded + (P(),) * 15,
        out_specs=(P(),) * 17,
        check_vma=False,
    )
```

```python
import functools
from types import SimpleNamespace

import jax
import jax.numpy as jnp
from jax import lax
from jax.experimental import pallas as pl
from jax.experimental.pallas import tpu as pltpu
from jax.sharding import PartitionSpec as P

HEADS = 4
STEP = 5
LANES = 128

eps_norm = 1e-05
beta_one = 0.9
beta_two = 0.999
rate_step = 0.05
decay_rate = 0.01
eps_adam = 1e-08

F32 = jnp.float32
BF16 = jnp.bfloat16
MESH = pl.DeviceIdType.MESH


def contract(left, right, left_dim, right_dim):
    return lax.dot_general(
        left, right, (((left_dim,), (right_dim,)), ((), ())), preferred_element_type=F32
    )


def nn(left, right):
    return contract(left, right, 1, 0)


def nt(left, right):
    return contract(left, right, 1, 1)


def tn(left, right):
    return contract(left, right, 0, 0)


def split(value):
    high = value.astype(BF16)
    return high, (value - high.astype(F32)).astype(BF16)


def sigmoid(value):
    return 0.5 * jnp.tanh(0.5 * value) + 0.5


def row_iota(rows, columns):
    return lax.broadcasted_iota(jnp.int32, (rows, columns), 0)


def lane_iota(rows, columns):
    return lax.broadcasted_iota(jnp.int32, (rows, columns), 1)


def aligned(index, size):
    return pl.ds(pl.multiple_of(index * size, size), size)


def step_kernel(dims, names, *refs):
    held, outs, rest_refs = refs[:22], refs[22:38], refs[38:]
    staged = rest_refs[:22]
    s = SimpleNamespace(**dict(zip(names, rest_refs[22:])))
    (feats, edges, degree, sends, psrc, pdst, plive, w1, w2, wh, vec, bias) = staged[:12]
    firsts, seconds = staged[12:17], staged[17:22]
    nd, nr, mb, nodes, fan, hid, head, ext, halo, pairs, bounds = dims
    half = pairs // 2
    tiles = nodes // LANES
    me = lax.axis_index("dom")
    mine = lax.axis_index("rep")

    def peers(axis, index, count, send):
        def one(step, carry):
            send(lax.rem(index + step, count))
            return carry

        lax.fori_loop(1, count, one, 0)

    def others(send):
        def one(step, carry):
            at = lax.rem(me * nr + mine + step, nd * nr)
            send({"dom": lax.div(at, nr), "rep": lax.rem(at, nr)})
            return carry

        lax.fori_loop(1, nd * nr, one, 0)

    def push(there, src, dst, send_sem, recv_sem):
        pltpu.make_async_remote_copy(
            src_ref=src,
            dst_ref=dst,
            send_sem=send_sem,
            recv_sem=recv_sem,
            device_id=there,
            device_id_type=MESH,
        ).start()

    incoming, outgoing = {}, []

    def arrived(ref, sem):
        pltpu.make_async_copy(ref, ref, sem).wait()

    def receive(number):
        arrived(incoming.pop(number), s.recv_sems.at[number])

    def finish():
        for number in list(incoming):
            receive(number)
        for number, ref in outgoing:
            arrived(ref, s.send_sems.at[number])

    def load(*which):
        for i in which:
            pltpu.make_async_copy(held[i], staged[i], s.load_sems.at[i]).start()

    def loaded(*which):
        for i in which:
            arrived(staged[i], s.load_sems.at[i])

    def scatter_out(src, dst, number):
        send_sem, recv_sem = s.send_sems.at[number], s.recv_sems.at[number]
        peers(
            "dom",
            me,
            nd,
            lambda peer: push({"dom": peer}, src.at[peer], dst.at[me], send_sem, recv_sem),
        )
        pltpu.make_async_copy(src.at[me], dst.at[me], recv_sem).start()
        incoming[number] = dst
        outgoing.append((number, src.at[pl.ds(0, nd - 1)]))

    load(3, 0)
    barrier = pltpu.get_barrier_semaphore()
    others(lambda there: pl.semaphore_signal(barrier, inc=1, device_id=there, device_id_type=MESH))
    load(7, 8, 9, 10, 11, 1, 2, 4, 5, 6)
    loaded(3)
    for b in range(mb):
        spread = (
            lax.div(row_iota(halo, nd), halo // nd) == lane_iota(halo, nd)
        ).astype(F32).astype(BF16)
        listed = nn(spread, sends[b].astype(F32).astype(BF16))
        pick = lax.rem(row_iota(halo, halo // nd), halo // nd) == lane_iota(halo, halo // nd)
        column = jnp.sum(jnp.where(pick, listed, 0.0), axis=1, keepdims=True)
        s.ohs[b] = (lane_iota(halo, nodes).astype(F32) == column).astype(F32).astype(BF16)

    loaded(0)
    for b in range(mb):
        s.fext[b, :nodes, :] = feats[b].astype(BF16)
    parts = [
        nn(s.ohs[b], s.fext[b, :nodes, :]).reshape(nd, halo // nd, LANES) for b in range(mb)
    ]
    s.fsend[...] = jnp.concatenate(parts, axis=1).astype(BF16)
    pl.semaphore_wait(barrier, nd * nr - 1)
    scatter_out(s.fsend, s.frecv, 0)
    load(*range(12, 22))

    loaded(7, 8, 9, 10, 11)
    s.w1t[...] = w1[...].T.astype(BF16)
    s.w2t[...] = w2[...].astype(BF16)
    s.w2b[...] = w2[...].T.astype(BF16)
    whb = wh[...].astype(BF16)
    for j in range(5):
        s.vb[j] = jnp.broadcast_to(vec[j : j + 1, :], (LANES, hid)).T
    s.bb[...] = jnp.broadcast_to(bias[0:1, :], (LANES, head)).T
    s.acc[...] = jnp.zeros_like(s.acc)
    s.accb[...] = jnp.zeros_like(s.accb)
    s.sm[...] = jnp.zeros_like(s.sm)
    loaded(1, 2, 4, 5, 6)

    for b in range(mb):

        def one_hot(k, carry):
            index = edges[k, b : b + 1, :]
            s.oht[b, :, aligned(k, nodes)] = (
                (row_iota(ext, nodes) == index).astype(F32).astype(BF16)
            )
            return carry

        lax.fori_loop(0, fan, one_hot, 0)

        s.tab[b, :, :nodes] = nt(s.w1t[:hid, :], s.fext[b, :nodes, :]).astype(BF16)
        rest = nt(s.w1t[hid:, :], s.fext[b, :nodes, :])
        s.tgt[0, b] = rest[:hid]
        s.res1[b] = rest[hid:]

        slot = lax.rem(lane_iota(1, pairs), half)
        count = jnp.sum(
            jnp.where(lane_iota(1, mb) == b, plive[...].astype(F32), 0.0), axis=1, keepdims=True
        )
        live = slot.astype(F32) < count
        from_src = (row_iota(nodes, pairs) == psrc[b : b + 1, :]).astype(F32).astype(BF16)
        to_dst = (
            ((row_iota(ext, pairs) == pdst[b : b + 1, :]) & live).astype(F32).astype(BF16)
        )
        s.cpos[b] = nt(from_src[:, :half], to_dst[:, :half])
        s.cneg[b] = nt(from_src[:, half:], to_dst[:, half:])

    def place(index):
        tile, which = divmod(index, HEADS)
        rows = slice(which * head, (which + 1) * head)
        return tile, rows, slice(tile * LANES, (tile + 1) * LANES)

    def slot_at(k, tile):
        return slice(k * nodes + tile * LANES, k * nodes + (tile + 1) * LANES)

    def attend(layer, b):
        att = 0 if layer == 0 else 4
        s.g[layer, b] = nn(s.tab[b], s.oht[b])

        for index in range(tiles * HEADS):
            tile, rows, cols = place(index)
            target = s.tgt[layer, b, rows, cols]
            weight = s.vb[att, rows, :]
            count = degree[b : b + 1, cols]
            scores = []
            for k in range(fan):
                u = s.g[layer, b, rows, slot_at(k, tile)] + target
                mixed = u * sigmoid(u)
                score = jnp.sum(mixed * weight, axis=0, keepdims=True)
                scores.append(jnp.where(count > k, score, -1e30))
            top = functools.reduce(jnp.maximum, scores)
            weights = [
                jnp.where(count > k, jnp.exp(scores[k] - top), 0.0) for k in range(fan)
            ]
            inverse = 1.0 / functools.reduce(jnp.add, weights)
            message = jnp.zeros((head, LANES), F32)
            for k in range(fan):
                alpha = weights[k] * inverse
                s.al[layer, b, index, k : k + 1, :] = alpha
                message = message + alpha * s.g[layer, b, rows, slot_at(k, tile)]
            s.msg[rows, cols] = message

    def attend_back(layer, b):
        att = 0 if layer == 0 else 4

        for index in range(tiles * HEADS):
            tile, rows, cols = place(index)
            if layer == 0:
                d_message = s.dmsg[rows, cols]
            else:
                d_message = s.dmsg[:head, cols]
            alphas = [s.al[layer, b, index, k : k + 1, :] for k in range(fan)]
            d_alphas = [
                jnp.sum(d_message * s.g[layer, b, rows, slot_at(k, tile)], axis=0, keepdims=True)
                for k in range(fan)
            ]
            total = functools.reduce(jnp.add, [a * d for a, d in zip(alphas, d_alphas)])
            d_target = jnp.zeros((head, LANES), F32)
            d_att = jnp.zeros((head, LANES), F32)
            for k in range(fan):
                d_score = alphas[k] * (d_alphas[k] - total)
                d_u = d_score * s.slope[layer, b, rows, slot_at(k, tile)].astype(F32)
                d_target = d_target + d_u
                d_att = d_att + d_score * s.mixed[layer, b, rows, slot_at(k, tile)].astype(F32)
                s.dg[rows, slot_at(k, tile)] = (alphas[k] * d_message + d_u).astype(BF16)
            s.dtgt[rows, cols] = d_target
            s.acc[att, rows, :] += d_att

    def slopes(layer, b):
        att = 0 if layer == 0 else 4
        for index in range(tiles * HEADS):
            tile, rows, cols = place(index)
            target = s.tgt[layer, b, rows, cols]
            weight = s.vb[att, rows, :]
            for k in range(fan):
                u = s.g[layer, b, rows, slot_at(k, tile)] + target
                gate = sigmoid(u)
                mixed = u * gate
                s.mixed[layer, b, rows, slot_at(k, tile)] = mixed.astype(BF16)
                slope = weight * (gate * (1.0 + (u - mixed)))
                s.slope[layer, b, rows, slot_at(k, tile)] = slope.astype(BF16)

    def pack_rows(value):
        blocks = value.reshape(nd, halo // nd, hid)
        return jnp.concatenate([blocks[:, :, :LANES], blocks[:, :, LANES:]], axis=1).astype(BF16)

    def unpack_rows(ref):
        blocks = ref[...].astype(F32)
        per = halo // nd
        return jnp.concatenate([blocks[:, :per, :], blocks[:, per:, :]], axis=2).reshape(halo, hid)

    def layer_one(b):
        s.fext[b, nodes:, :] = (
            s.frecv[...].astype(F32)[:, b * (halo // nd) : (b + 1) * (halo // nd), :]
            .reshape(halo, LANES)
            .astype(BF16)
        )
        s.tab[b, :, nodes:] = nt(s.w1t[:hid, :], s.fext[b, nodes:, :]).astype(BF16)
        attend(0, b)
        for t in range(tiles):
            cols = slice(t * LANES, (t + 1) * LANES)
            y = s.msg[:, cols] + s.vb[1] + s.res1[b, :, cols]
            centred = y - jnp.sum(y, axis=0, keepdims=True) * (1.0 / hid)
            spread = jnp.sum(centred * centred, axis=0, keepdims=True) * (1.0 / hid)
            rstd = lax.rsqrt(spread + eps_norm)
            normed = centred * rstd
            s.xhat[b, :, cols] = normed
            s.rstd[b, 0:1, cols] = rstd
            n = normed * s.vb[2] + s.vb[3]
            s.h1t[b, :, cols] = jnp.where(n > 0.0, n, jnp.exp(jnp.minimum(n, 0.0)) - 1.0).astype(BF16)
        s.hsend[b] = pack_rows(nt(s.ohs[b], s.h1t[b]))
        scatter_out(s.hsend.at[b], s.hrecv.at[b], 1 + b)
        own = nn(s.w2t[...], s.h1t[b])
        s.own2[b] = own[:hid].astype(BF16)
        s.tgt[1, b] = own[hid : 2 * hid]
        s.res2[b] = own[2 * hid :]

    def layer_two(b):
        receive(1 + b)
        s.tab[b, :, :nodes] = s.own2[b]
        s.h1h[b] = unpack_rows(s.hrecv.at[b]).astype(BF16)
        s.tab[b, :, nodes:] = nt(s.w2t[:hid, :], s.h1h[b]).astype(BF16)
        attend(1, b)
        for t in range(tiles):
            cols = slice(t * LANES, (t + 1) * LANES)
            message = functools.reduce(
                jnp.add, [s.msg[h * head : (h + 1) * head, cols] for h in range(HEADS)]
            )
            s.h2[:, cols] = message * (1.0 / HEADS) + s.bb[...] + s.res2[b, :, cols]
        s.h2t[b] = s.h2[...].astype(BF16)
        rows = nt(s.ohs[b], s.h2t[b])
        s.zsend[b, :, :, :head] = rows.reshape(nd, halo // nd, head)
        scatter_out(s.zsend.at[b], s.zrecv.at[b], 3 + b)
        s.h2r[b] = s.h2[...].T.astype(BF16)

    def pair_terms(score, pos, neg):
        small = jnp.exp(-jnp.abs(score))
        terms = (
            (pos + neg) * jnp.log1p(small)
            + pos * jnp.maximum(-score, 0.0)
            + neg * jnp.maximum(score, 0.0)
        )
        s.sm[12:13, 0:1] += jnp.sum(jnp.sum(terms, axis=0, keepdims=True), axis=1, keepdims=True)
        big = 1.0 / (1.0 + small)
        little = small * big
        up = score > 0.0
        return (neg * jnp.where(up, big, little) - pos * jnp.where(up, little, big)).astype(BF16)

    def pair_own(b):
        high, low = split(nn(s.h2r[b], whb) + bias[1:2, :])
        s.left[b] = jnp.concatenate([high, high, low], axis=1)
        score = nt(s.left[b], jnp.concatenate([high, low, high], axis=1))
        d_score = pair_terms(score, s.cpos[b, :, :nodes], s.cneg[b, :, :nodes])
        s.dz[b] = nn(d_score, high) + tn(d_score, high)

    def pair_halo(b):
        receive(3 + b)
        rows = s.zrecv[b].reshape(halo, LANES)[:, :head].astype(BF16)
        high, low = split(nn(rows, whb) + bias[1:2, :])
        score = nt(s.left[b], jnp.concatenate([high, low, high], axis=1))
        d_score = pair_terms(score, s.cpos[b, :, nodes:], s.cneg[b, :, nodes:])
        s.ysend[b, :, :, :head] = tn(d_score, s.left[b, :, :head]).reshape(nd, halo // nd, head)
        scatter_out(s.ysend.at[b], s.yrecv.at[b], 5 + b)
        s.dz[b] += nn(d_score, high)

    def add_to(ref, value, b):
        if b == 0:
            ref[...] = value
        else:
            ref[...] += value

    def back_two(b):
        receive(5 + b)
        returned = s.yrecv[b].reshape(halo, LANES)[:, :head].astype(BF16)
        dz = s.dz[b] + tn(s.ohs[b], returned)
        s.sm[11:12, :head] += jnp.sum(dz, axis=0, keepdims=True)
        dz_low = dz.astype(BF16)
        d_out = nt(whb, dz_low)
        s.dmsg[:head, :] = d_out * (1.0 / HEADS)
        s.dproj2[b, 2 * hid :, :] = d_out.astype(BF16)
        attend_back(1, b)
        d_table = nt(s.dg[...], s.oht[b])
        s.gsend[b] = pack_rows(d_table[:, nodes:].T)
        scatter_out(s.gsend.at[b], s.grecv.at[b], 7 + b)
        s.dtab[b] = d_table
        s.dzl[b] = dz_low
        s.accb[...] += functools.reduce(
            jnp.add, [d_out[:, t * LANES : (t + 1) * LANES] for t in range(tiles)]
        )
        s.dproj2[b, hid : 2 * hid, :] = s.dtgt[...].astype(BF16)

    def after_two(b):
        s.dhp[b] = nn(s.w2b[:, hid:], s.dproj2[b, hid:, :])
        add_to(s.gw2.at[hid:, :], nt(s.dproj2[b, hid:, :], s.h1t[b]), b)
        d_own = s.dtab[b, :, :nodes].astype(BF16)
        d_halo = s.dtab[b, :, nodes:].astype(BF16)
        add_to(s.gw2.at[:hid, :], nt(d_own, s.h1t[b]) + nn(d_halo, s.h1h[b]), b)
        add_to(s.gwh, nn(s.h2t[b], s.dzl[b]), b)

    def finish_two(b):
        receive(7 + b)
        returned = unpack_rows(s.grecv.at[b]).astype(BF16)
        d_source = s.dtab[b, :, :nodes] + tn(returned, s.ohs[b])
        s.dh[...] = s.dhp[b] + nn(s.w2b[:, :hid], d_source.astype(BF16))

    def norm_back(b):
        for t in range(tiles):
            cols = slice(t * LANES, (t + 1) * LANES)
            normed = s.xhat[b, :, cols]
            n = normed * s.vb[2] + s.vb[3]
            dn = s.dh[:, cols] * jnp.where(n > 0.0, 1.0, jnp.exp(jnp.minimum(n, 0.0)))
            s.acc[3] += dn
            s.acc[2] += dn * normed
            dx = dn * s.vb[2]
            mean = jnp.sum(dx, axis=0, keepdims=True) * (1.0 / hid)
            along = jnp.sum(dx * normed, axis=0, keepdims=True) * (1.0 / hid)
            dy = s.rstd[b, 0:1, cols] * (dx - mean - normed * along)
            s.acc[1] += dy
            s.dmsg[:, cols] = dy

    def resid_one(b):
        add_to(s.gw1.at[2 * hid :, :], nn(s.dmsg[...].astype(BF16), s.fext[b, :nodes, :]), b)

    def weights_one(b):
        d_table = nt(s.dg[...], s.oht[b]).astype(BF16)
        add_to(s.gw1.at[:hid, :], nn(d_table, s.fext[b]), b)
        d_target = nn(s.dtgt[...].astype(BF16), s.fext[b, :nodes, :])
        add_to(s.gw1.at[hid : 2 * hid, :], d_target, b)

    def part(ref, index, count):
        return ref.at[aligned(index, count), :]

    def exchange(axis, number, src_of, dst, own=True):
        index, count = (me, nd) if axis == "dom" else (mine, nr)
        send_sem, recv_sem = s.send_sems.at[number], s.recv_sems.at[number]
        peers(
            axis,
            index,
            count,
            lambda peer: push({axis: peer}, src_of(peer), dst.at[index], send_sem, recv_sem),
        )
        if own:
            pltpu.make_async_copy(src_of(index), dst.at[index], recv_sem).start()
            incoming[number] = dst
        else:
            incoming[number] = dst.at[pl.ds(0, count - 1)]
        outgoing.append((number, dst.at[pl.ds(0, count - 1)]))

    def summed(ref, count):
        return functools.reduce(jnp.add, [ref[i].astype(F32) for i in range(count)])

    chunks = len(bounds) - 1
    split_sum = chunks == 3
    in_one, in_two = 3 * hid, 2 * hid + head
    halves = [slice(i * LANES, (i + 1) * LANES) for i in range(hid // LANES)]
    regions, start = [], 0
    for rows in (slice(hid, 2 * hid), slice(0, hid), slice(2 * hid, in_two)):
        for cols in halves:
            regions.append((start, s.gw2, rows, cols))
            start += rows.stop - rows.start
    regions.append((start, s.gwh, slice(0, head), slice(None)))
    regions.append((start + head, s.gw1, slice(2 * hid, in_one), slice(None)))
    regions.append((bounds[-1] - 2 * hid, s.gw1, slice(0, 2 * hid), slice(None)))

    def spans(chunk):
        low, high = bounds[chunk], bounds[chunk + 1]
        for at, ref, rows, cols in regions:
            first, last, _ = rows.indices(ref.shape[0])
            begin, end = max(low, at), min(high, at + last - first)
            if begin < end:
                width = len(range(*cols.indices(ref.shape[1])))
                yield begin, end, ref, slice(first + begin - at, first + end - at), cols, width

    def pack(chunk):
        for begin, end, ref, rows, cols, width in spans(chunk):
            s.gb[begin:end, :width] = ref[rows, cols].astype(BF16)

    def chunk_of(chunk):
        return [getattr(s, f"{name}{chunk}") for name in ("rb", "gd", "rd", "fin", "ag")]

    def sum_rep(chunk):
        pack(chunk)
        low, high = bounds[chunk], bounds[chunk + 1]
        size = (high - low) // nr
        here = s.gb.at[low:high, :]
        exchange("rep", 11 + 4 * chunk, lambda peer: part(here, peer, size), chunk_of(chunk)[0])

    def sum_dom(chunk):
        rb, gd, rd, fin, ag = chunk_of(chunk)
        receive(11 + 4 * chunk)
        gd[...] = summed(rb, nr).astype(BF16)
        size = gd.shape[0] // nd
        exchange("dom", 12 + 4 * chunk, lambda peer: part(gd, peer, size), rd)

    def share_dom(chunk):
        rb, gd, rd, fin, ag = chunk_of(chunk)
        receive(12 + 4 * chunk)
        fin[...] = summed(rd, nd).astype(BF16)
        exchange("dom", 13 + 4 * chunk, lambda peer: fin, ag.at[mine])

    def share_rep(chunk):
        ag = chunk_of(chunk)[4]
        receive(13 + 4 * chunk)
        exchange("rep", 14 + 4 * chunk, lambda peer: ag.at[mine], ag, own=False)

    def exchange_all(number, src_of, dst):
        index = me * nr + mine
        send_sem, recv_sem = s.send_sems.at[number], s.recv_sems.at[number]
        others(
            lambda there: push(
                there, src_of(there["dom"] * nr + there["rep"]), dst.at[index], send_sem, recv_sem
            )
        )
        pltpu.make_async_copy(src_of(index), dst.at[index], recv_sem).start()
        incoming[number] = dst
        outgoing.append((number, dst.at[pl.ds(0, nd * nr - 1)]))

    def direct(chunk):
        return [getattr(s, f"{name}{chunk}") for name in ("rl", "finl", "agl")]

    def sum_all(chunk):
        pack(chunk)
        rl, finl, agl = direct(chunk)
        size = finl.shape[0]
        here = s.gb.at[bounds[chunk] : bounds[chunk + 1], :]
        exchange_all(11 + 4 * chunk, lambda at: part(here, at, size), rl)

    def share_all(chunk):
        rl, finl, agl = direct(chunk)
        receive(11 + 4 * chunk)
        finl[...] = summed(rl, nd * nr).astype(BF16)
        exchange_all(12 + 4 * chunk, lambda at: finl, agl)

    def vector_sum(j):
        total = jnp.sum(s.acc[j].T, axis=0, keepdims=True)
        for p in range(hid // LANES):
            row = (hid // LANES) * j + p
            s.sm[row : row + 1, :] = total[:, p * LANES : (p + 1) * LANES]

    def small_rep():
        exchange("rep", 9, lambda peer: s.sm, s.sm1)

    def small_dom():
        receive(9)
        s.sms[...] = summed(s.sm1, nr)
        exchange("dom", 10, lambda peer: s.sms, s.sm2)

    params = (w1, w2, wh, vec, bias)

    def update(index, grad, rows, cols):
        made = adamw(
            params[index][rows, cols], grad, firsts[index][rows, cols], seconds[index][rows, cols]
        )
        for offset in range(3):
            outs[1 + 3 * index + offset][rows, cols] = made[offset]

    def small_update():
        receive(10)
        total = summed(s.sm2, nd)
        outs[0][...] = total
        scale = 1.0 / total[13:14, 0:1]
        s.scale[...] = jnp.broadcast_to(scale, s.scale.shape)
        for j in range(5):
            for p in range(hid // LANES):
                row = (hid // LANES) * j + p
                cols = slice(p * LANES, (p + 1) * LANES)
                update(3, total[row : row + 1, :] * scale, slice(j, j + 1), cols)
        for j in range(2):
            update(4, total[10 + j : 11 + j, :head] * scale, slice(j, j + 1), slice(None))

    def chunk_update(chunk):
        staged_sum = split_sum and chunk < 2
        ag = chunk_of(chunk)[4] if staged_sum else direct(chunk)[2]
        receive(4 * chunk + (14 if staged_sum else 12))
        low, high = bounds[chunk], bounds[chunk + 1]
        whole = ag[...].reshape(high - low, LANES)
        scale = s.scale[0:1, 0:1]
        for begin, end, ref, rows, cols, width in spans(chunk):
            if ref is s.gw1:
                for at in range(0, end - begin, LANES):
                    grad = whole[begin - low + at : begin - low + at + LANES].astype(F32).T * scale
                    update(0, grad, slice(None), slice(rows.start + at, rows.start + at + LANES))
            else:
                grad = whole[begin - low : end - low].astype(F32)[:, :width] * scale
                update(1 if ref is s.gw2 else 2, grad, rows, cols)

    s.zsend[...] = jnp.zeros_like(s.zsend)
    s.ysend[...] = jnp.zeros_like(s.ysend)
    s.gb[...] = jnp.zeros_like(s.gb)
    s.sm[13:14, 0:1] = 2.0 * jnp.sum(plive[...].astype(F32), axis=1, keepdims=True)
    receive(0)
    stages = [(stage, b) for stage in (layer_one, layer_two, pair_own) for b in range(mb)]
    for b in range(mb):
        stages += [(pair_halo, b), (functools.partial(slopes, 1), b)]
    stages += [(functools.partial(slopes, 0), 0)]
    stages += [(back_two, b) for b in range(mb)]
    for stage, b in stages:
        stage(b)

    for b in range(mb):
        after_two(b)
    if split_sum:
        sum_rep(0)
    for b in range(1, mb):
        slopes(0, b)
    vector_sum(4)
    s.sm[10:11, :head] = jnp.sum(s.accb[...].T, axis=0, keepdims=True)
    for b in range(mb):
        final = split_sum and b == mb - 1
        finish_two(b)
        norm_back(b)
        resid_one(b)
        if final:
            sum_rep(1)
        attend_back(0, b)
        weights_one(b)
        if split_sum and b == mb - 2:
            sum_dom(0)
    sum_all(chunks - 1)
    if split_sum:
        sum_dom(1)
        share_dom(0)
    for j in range(4):
        vector_sum(j)
    small_rep()
    loaded(*range(12, 22))
    if split_sum:
        share_dom(1)
    share_all(chunks - 1)
    small_dom()
    if split_sum:
        share_rep(0)
    if split_sum:
        share_rep(1)
    small_update()
    for chunk in range(chunks):
        chunk_update(chunk)
    finish()


def adamw(param, grad, first, second):
    first = beta_one * first + (1.0 - beta_one) * grad
    second = beta_two * second + (1.0 - beta_two) * grad * grad
    fhat = first * (1.0 / (1.0 - beta_one**STEP))
    shat = second * (1.0 / (1.0 - beta_two**STEP))
    return (
        first,
        second,
        param - rate_step * (fhat / (jnp.sqrt(shat) + eps_adam) + decay_rate * param),
    )


def write_kernel(*refs):
    small, held, outs = refs[0], refs[1:16], refs[16:33]
    loss, count, sems = refs[33:]
    loss[...] = small[12:13, 0:1]
    count[...] = small[13:14, 0:1]
    copies = [
        pltpu.make_async_copy(src, dst, sems.at[i])
        for i, (src, dst) in enumerate(zip((loss, count) + held, outs))
    ]
    for copy in copies:
        copy.start()
    for copy in copies:
        copy.wait()


def body(nd, nr, *args):
    data, weights = args[:7], args[7:]
    features, edge_src, node_degree, send_rows, pair_src, pair_dst, pair_live = (
        a.reshape(a.shape[1:]) for a in data
    )
    mb, nodes, width = features.shape
    fan = edge_src.shape[-1]
    per = send_rows.shape[-1]
    halo = nd * per
    ext = nodes + halo
    pairs = pair_src.shape[-1]
    hid = weights[3].shape[1]
    head = weights[2].shape[0]
    in_one, in_two = 3 * hid, 2 * hid + head
    unit = nd * nr * 16
    quarter = (hid // LANES) * hid
    used = 2 * quarter + (hid // LANES + 1) * head + in_one
    rows_all = -(-used // unit) * unit
    bounds = (0, rows_all)
    if quarter % unit == 0 and 2 * hid % unit == 0:
        bounds = (0, 2 * quarter, rows_all - 2 * hid, rows_all)
    dims = (nd, nr, mb, nodes, fan, hid, head, ext, halo, pairs, bounds)
    chunks = {}
    for chunk in range(len(bounds) - 1):
        rows = bounds[chunk + 1] - bounds[chunk]
        if len(bounds) > 2 and chunk < 2:
            size = rows // nr
            chunks[f"rb{chunk}"] = pltpu.VMEM((nr, size, LANES), BF16)
            chunks[f"gd{chunk}"] = pltpu.VMEM((size, LANES), BF16)
            chunks[f"rd{chunk}"] = pltpu.VMEM((nd, size // nd, LANES), BF16)
            chunks[f"fin{chunk}"] = pltpu.VMEM((size // nd, LANES), BF16)
            chunks[f"ag{chunk}"] = pltpu.VMEM((nr, nd, size // nd, LANES), BF16)
        else:
            size = rows // (nd * nr)
            chunks[f"rl{chunk}"] = pltpu.VMEM((nd * nr, size, LANES), BF16)
            chunks[f"finl{chunk}"] = pltpu.VMEM((size, LANES), BF16)
            chunks[f"agl{chunk}"] = pltpu.VMEM((nd * nr, size, LANES), BF16)
    scratch = dict(
        ohs=pltpu.VMEM((mb, halo, nodes), BF16),
        fext=pltpu.VMEM((mb, ext, width), BF16),
        fsend=pltpu.VMEM((nd, mb * per, LANES), BF16),
        frecv=pltpu.VMEM((nd, mb * per, LANES), BF16),
        w1t=pltpu.VMEM((in_one, width), BF16),
        w2b=pltpu.VMEM((hid, in_two), BF16),
        w2t=pltpu.VMEM((in_two, hid), BF16),
        vb=pltpu.VMEM((5, hid, LANES), F32),
        bb=pltpu.VMEM((head, LANES), F32),
        acc=pltpu.VMEM((5, hid, LANES), F32),
        accb=pltpu.VMEM((head, LANES), F32),
        sm=pltpu.VMEM((16, LANES), F32),
        oht=pltpu.VMEM((mb, ext, fan * nodes), BF16),
        tgt=pltpu.VMEM((2, mb, hid, nodes), F32),
        res1=pltpu.VMEM((mb, hid, nodes), F32),
        res2=pltpu.VMEM((mb, head, nodes), F32),
        cpos=pltpu.VMEM((mb, nodes, ext), F32),
        cneg=pltpu.VMEM((mb, nodes, ext), F32),
        tab=pltpu.VMEM((mb, hid, ext), BF16),
        g=pltpu.VMEM((2, mb, hid, fan * nodes), F32),
        mixed=pltpu.VMEM((2, mb, hid, fan * nodes), BF16),
        slope=pltpu.VMEM((2, mb, hid, fan * nodes), BF16),
        al=pltpu.VMEM((2, mb, (nodes // LANES) * HEADS, 16, LANES), F32),
        msg=pltpu.VMEM((hid, nodes), F32),
        xhat=pltpu.VMEM((mb, hid, nodes), F32),
        rstd=pltpu.VMEM((mb, 8, nodes), F32),
        h1t=pltpu.VMEM((mb, hid, nodes), BF16),
        hsend=pltpu.VMEM((mb, nd, 2 * per, LANES), BF16),
        hrecv=pltpu.VMEM((mb, nd, 2 * per, LANES), BF16),
        own2=pltpu.VMEM((mb, hid, nodes), BF16),
        h2=pltpu.VMEM((head, nodes), F32),
        h2t=pltpu.VMEM((mb, head, nodes), BF16),
        h2r=pltpu.VMEM((mb, nodes, head), BF16),
        left=pltpu.VMEM((mb, nodes, 3 * head), BF16),
        dhp=pltpu.VMEM((mb, hid, nodes), F32),
        dzl=pltpu.VMEM((mb, nodes, head), BF16),
        zsend=pltpu.VMEM((mb, nd, per, LANES), F32),
        zrecv=pltpu.VMEM((mb, nd, per, LANES), F32),
        ysend=pltpu.VMEM((mb, nd, per, LANES), F32),
        yrecv=pltpu.VMEM((mb, nd, per, LANES), F32),
        dz=pltpu.VMEM((mb, nodes, head), F32),
        dmsg=pltpu.VMEM((hid, nodes), F32),
        dtgt=pltpu.VMEM((hid, nodes), F32),
        dg=pltpu.VMEM((hid, fan * nodes), BF16),
        dproj2=pltpu.VMEM((mb, in_two, nodes), BF16),
        dtab=pltpu.VMEM((mb, hid, ext), F32),
        h1h=pltpu.VMEM((mb, halo, hid), BF16),
        gsend=pltpu.VMEM((mb, nd, 2 * per, LANES), BF16),
        grecv=pltpu.VMEM((mb, nd, 2 * per, LANES), BF16),
        dh=pltpu.VMEM((hid, nodes), F32),
        gw1=pltpu.VMEM((in_one, LANES), F32),
        gw2=pltpu.VMEM((in_two, hid), F32),
        gwh=pltpu.VMEM((head, head), F32),
        gb=pltpu.VMEM((rows_all, LANES), BF16),
        sm1=pltpu.VMEM((nr, 16, LANES), F32),
        sms=pltpu.VMEM((16, LANES), F32),
        sm2=pltpu.VMEM((nd, 16, LANES), F32),
        load_sems=pltpu.SemaphoreType.DMA((22,)),
        scale=pltpu.VMEM((8, LANES), F32),
        send_sems=pltpu.SemaphoreType.DMA((27,)),
        recv_sems=pltpu.SemaphoreType.DMA((27,)),
        **chunks,
    )
    operands = [features, edge_src.transpose(2, 0, 1), node_degree, send_rows, pair_src, pair_dst]
    operands.append(pair_live.T)
    operands += [w.T if i % 5 == 1 else w for i, w in enumerate(weights)]
    scalars = (jax.ShapeDtypeStruct((1, 1), F32),) * 2
    results = ()
    for operand in operands[7:12]:
        results += (jax.ShapeDtypeStruct(operand.shape, F32),) * 3
    whole = pl.BlockSpec(memory_space=pltpu.VMEM)
    anywhere = pl.BlockSpec(memory_space=pl.ANY)
    made = pl.pallas_call(
        functools.partial(step_kernel, dims, tuple(scratch)),
        out_shape=(jax.ShapeDtypeStruct((16, LANES), F32),) + results,
        in_specs=[anywhere] * 22,
        out_specs=(whole,) * 16,
        scratch_shapes=[pltpu.VMEM(a.shape, a.dtype) for a in operands] + list(scratch.values()),
        compiler_params=pltpu.CompilerParams(
            collective_id=0, has_side_effects=True, vmem_limit_bytes=(34 + ext // 32) * 1024 * 1024
        ),
    )(*(pltpu.with_memory_space_constraint(a, pltpu.HBM) for a in operands))
    made = pl.pallas_call(
        write_kernel,
        out_shape=scalars + results,
        in_specs=[whole] * 16,
        out_specs=(anywhere,) * 17,
        scratch_shapes=[pltpu.VMEM((1, 1), F32)] * 2 + [pltpu.SemaphoreType.DMA((17,))],
        compiler_params=pltpu.CompilerParams(vmem_limit_bytes=1024 * 1024),
    )(*made)
    loss, count = (a.reshape(()) for a in made[:2])
    return (loss, count) + tuple(a.T if i // 3 == 1 else a for i, a in enumerate(made[2:]))


def solution(mesh):
    sharded = (
        P("rep", None, "dom", None),
        P("rep", None, "dom", None),
        P("rep", None, "dom"),
        P("rep", None, "dom", None),
        P("rep", None, "dom"),
        P("rep", None, "dom"),
        P("rep", None, "dom"),
    )
    return jax.shard_map(
        functools.partial(body, mesh.shape["dom"], mesh.shape["rep"]),
        mesh=mesh,
        in_specs=sharded + (P(),) * 15,
        out_specs=(P(),) * 17,
        check_vma=False,
    )
```

```python
import functools
from types import SimpleNamespace

import jax
import jax.numpy as jnp
from jax import lax
from jax.experimental import pallas as pl
from jax.experimental.pallas import tpu as pltpu
from jax.sharding import PartitionSpec as P

HEADS = 4
STEP = 5
LANES = 128

eps_norm = 1e-05
beta_one = 0.9
beta_two = 0.999
rate_step = 0.05
decay_rate = 0.01
eps_adam = 1e-08

F32 = jnp.float32
BF16 = jnp.bfloat16
MESH = pl.DeviceIdType.MESH


def contract(left, right, left_dim, right_dim):
    return lax.dot_general(
        left, right, (((left_dim,), (right_dim,)), ((), ())), preferred_element_type=F32
    )


def nn(left, right):
    return contract(left, right, 1, 0)


def nt(left, right):
    return contract(left, right, 1, 1)


def tn(left, right):
    return contract(left, right, 0, 0)


def split(value):
    high = value.astype(BF16)
    return high, (value - high.astype(F32)).astype(BF16)


def sigmoid(value):
    return 0.5 * jnp.tanh(0.5 * value) + 0.5


def row_iota(rows, columns):
    return lax.broadcasted_iota(jnp.int32, (rows, columns), 0)


def lane_iota(rows, columns):
    return lax.broadcasted_iota(jnp.int32, (rows, columns), 1)


def aligned(index, size):
    return pl.ds(pl.multiple_of(index * size, size), size)


def step_kernel(dims, names, *refs):
    held, outs, rest_refs = refs[:22], refs[22:38], refs[38:]
    staged = rest_refs[:22]
    s = SimpleNamespace(**dict(zip(names, rest_refs[22:])))
    (feats, edges, degree, sends, psrc, pdst, plive, w1, w2, wh, vec, bias) = staged[:12]
    firsts, seconds = staged[12:17], staged[17:22]
    nd, nr, mb, nodes, fan, hid, head, ext, halo, pairs, bounds = dims
    half = pairs // 2
    tiles = nodes // LANES
    me = lax.axis_index("dom")
    mine = lax.axis_index("rep")

    def peers(axis, index, count, send):
        def one(step, carry):
            send(lax.rem(index + step, count))
            return carry

        lax.fori_loop(1, count, one, 0)

    def others(send):
        def one(step, carry):
            at = lax.rem(me * nr + mine + step, nd * nr)
            send({"dom": lax.div(at, nr), "rep": lax.rem(at, nr)})
            return carry

        lax.fori_loop(1, nd * nr, one, 0)

    def push(there, src, dst, send_sem, recv_sem):
        pltpu.make_async_remote_copy(
            src_ref=src,
            dst_ref=dst,
            send_sem=send_sem,
            recv_sem=recv_sem,
            device_id=there,
            device_id_type=MESH,
        ).start()

    incoming, outgoing = {}, []

    def arrived(ref, sem):
        pltpu.make_async_copy(ref, ref, sem).wait()

    def receive(number):
        arrived(incoming.pop(number), s.recv_sems.at[number])

    def finish():
        for number in list(incoming):
            receive(number)
        for number, ref in outgoing:
            arrived(ref, s.send_sems.at[number])

    def load(*which):
        for i in which:
            pltpu.make_async_copy(held[i], staged[i], s.load_sems.at[i]).start()

    def loaded(*which):
        for i in which:
            arrived(staged[i], s.load_sems.at[i])

    def scatter_out(src, dst, number):
        send_sem, recv_sem = s.send_sems.at[number], s.recv_sems.at[number]
        peers(
            "dom",
            me,
            nd,
            lambda peer: push({"dom": peer}, src.at[peer], dst.at[me], send_sem, recv_sem),
        )
        pltpu.make_async_copy(src.at[me], dst.at[me], recv_sem).start()
        incoming[number] = dst
        outgoing.append((number, src.at[pl.ds(0, nd - 1)]))

    load(3, 0)
    barrier = pltpu.get_barrier_semaphore()
    others(lambda there: pl.semaphore_signal(barrier, inc=1, device_id=there, device_id_type=MESH))
    load(7, 8, 9, 10, 11, 1, 2, 4, 5, 6)
    loaded(3)
    for b in range(mb):
        spread = (
            lax.div(row_iota(halo, nd), halo // nd) == lane_iota(halo, nd)
        ).astype(F32).astype(BF16)
        listed = nn(spread, sends[b].astype(F32).astype(BF16))
        pick = lax.rem(row_iota(halo, halo // nd), halo // nd) == lane_iota(halo, halo // nd)
        column = jnp.sum(jnp.where(pick, listed, 0.0), axis=1, keepdims=True)
        s.ohs[b] = (lane_iota(halo, nodes).astype(F32) == column).astype(F32).astype(BF16)

    loaded(0)
    for b in range(mb):
        s.fext[b, :nodes, :] = feats[b].astype(BF16)
    parts = [
        nn(s.ohs[b], s.fext[b, :nodes, :]).reshape(nd, halo // nd, LANES) for b in range(mb)
    ]
    s.fsend[...] = jnp.concatenate(parts, axis=1).astype(BF16)
    pl.semaphore_wait(barrier, nd * nr - 1)
    scatter_out(s.fsend, s.frecv, 0)
    load(*range(12, 22))

    loaded(7, 8, 9, 10, 11)
    for b in range(mb):
        s.ohst[b] = s.ohs[b].astype(F32).T.astype(BF16)
    s.w1t[...] = w1[...].T.astype(BF16)
    s.w2t[...] = w2[...].astype(BF16)
    s.w2b[...] = w2[...].T.astype(BF16)
    whb = wh[...].astype(BF16)
    for j in range(5):
        s.vb[j] = jnp.broadcast_to(vec[j : j + 1, :], (LANES, hid)).T
    s.bb[...] = jnp.broadcast_to(bias[0:1, :], (LANES, head)).T
    s.acc[...] = jnp.zeros_like(s.acc)
    s.accb[...] = jnp.zeros_like(s.accb)
    s.sm[...] = jnp.zeros_like(s.sm)
    loaded(1, 2, 4, 5, 6)

    for b in range(mb):

        def one_hot(k, carry):
            index = edges[k, b : b + 1, :]
            s.oht[b, :, aligned(k, nodes)] = (
                (row_iota(ext, nodes) == index).astype(F32).astype(BF16)
            )
            return carry

        lax.fori_loop(0, fan, one_hot, 0)

        s.tab[b, :, :nodes] = nt(s.w1t[:hid, :], s.fext[b, :nodes, :]).astype(BF16)
        rest = nt(s.w1t[hid:, :], s.fext[b, :nodes, :])
        s.tgt[0, b] = rest[:hid]
        s.res1[b] = rest[hid:]

        slot = lax.rem(lane_iota(1, pairs), half)
        count = jnp.sum(
            jnp.where(lane_iota(1, mb) == b, plive[...].astype(F32), 0.0), axis=1, keepdims=True
        )
        live = slot.astype(F32) < count
        from_src = (row_iota(nodes, pairs) == psrc[b : b + 1, :]).astype(F32).astype(BF16)
        to_dst = (
            ((row_iota(ext, pairs) == pdst[b : b + 1, :]) & live).astype(F32).astype(BF16)
        )
        s.cpos[b] = nt(from_src[:, :half], to_dst[:, :half])
        s.cneg[b] = nt(from_src[:, half:], to_dst[:, half:])

    def place(index):
        tile, which = divmod(index, HEADS)
        rows = slice(which * head, (which + 1) * head)
        return tile, rows, slice(tile * LANES, (tile + 1) * LANES)

    def slot_at(k, tile):
        return slice(k * nodes + tile * LANES, k * nodes + (tile + 1) * LANES)

    def attend(layer, b):
        att = 0 if layer == 0 else 4
        s.g[layer, b] = nn(s.tab[b], s.oht[b])

        for index in range(tiles * HEADS):
            tile, rows, cols = place(index)
            target = s.tgt[layer, b, rows, cols]
            weight = s.vb[att, rows, :]
            count = degree[b : b + 1, cols]
            scores = []
            for k in range(fan):
                u = s.g[layer, b, rows, slot_at(k, tile)] + target
                mixed = u * sigmoid(u)
                score = jnp.sum(mixed * weight, axis=0, keepdims=True)
                scores.append(jnp.where(count > k, score, -1e30))
            top = functools.reduce(jnp.maximum, scores)
            weights = [
                jnp.where(count > k, jnp.exp(scores[k] - top), 0.0) for k in range(fan)
            ]
            inverse = 1.0 / functools.reduce(jnp.add, weights)
            message = jnp.zeros((head, LANES), F32)
            for k in range(fan):
                alpha = weights[k] * inverse
                s.al[layer, b, index, k : k + 1, :] = alpha
                message = message + alpha * s.g[layer, b, rows, slot_at(k, tile)]
            s.msg[rows, cols] = message

    def attend_back(layer, b):
        att = 0 if layer == 0 else 4

        for index in range(tiles * HEADS):
            tile, rows, cols = place(index)
            if layer == 0:
                d_message = s.dmsg[rows, cols]
            else:
                d_message = s.dmsg[:head, cols]
            alphas = [s.al[layer, b, index, k : k + 1, :] for k in range(fan)]
            d_alphas = [
                jnp.sum(d_message * s.g[layer, b, rows, slot_at(k, tile)], axis=0, keepdims=True)
                for k in range(fan)
            ]
            total = functools.reduce(jnp.add, [a * d for a, d in zip(alphas, d_alphas)])
            d_target = jnp.zeros((head, LANES), F32)
            d_att = jnp.zeros((head, LANES), F32)
            for k in range(fan):
                d_score = alphas[k] * (d_alphas[k] - total)
                d_u = d_score * s.slope[layer, b, rows, slot_at(k, tile)].astype(F32)
                d_target = d_target + d_u
                d_att = d_att + d_score * s.mixed[layer, b, rows, slot_at(k, tile)].astype(F32)
                s.dg[rows, slot_at(k, tile)] = (alphas[k] * d_message + d_u).astype(BF16)
            s.dtgt[rows, cols] = d_target
            s.acc[att, rows, :] += d_att

    def slopes(layer, b):
        att = 0 if layer == 0 else 4
        for index in range(tiles * HEADS):
            tile, rows, cols = place(index)
            target = s.tgt[layer, b, rows, cols]
            weight = s.vb[att, rows, :]
            for k in range(fan):
                u = s.g[layer, b, rows, slot_at(k, tile)] + target
                gate = sigmoid(u)
                mixed = u * gate
                s.mixed[layer, b, rows, slot_at(k, tile)] = mixed.astype(BF16)
                slope = weight * (gate * (1.0 + (u - mixed)))
                s.slope[layer, b, rows, slot_at(k, tile)] = slope.astype(BF16)

    def pack_rows(value):
        blocks = value.reshape(nd, halo // nd, hid)
        return jnp.concatenate([blocks[:, :, :LANES], blocks[:, :, LANES:]], axis=1).astype(BF16)

    def unpack_rows(ref):
        blocks = ref[...].astype(F32)
        per = halo // nd
        return jnp.concatenate([blocks[:, :per, :], blocks[:, per:, :]], axis=2).reshape(halo, hid)

    def layer_one(b):
        s.fext[b, nodes:, :] = (
            s.frecv[...].astype(F32)[:, b * (halo // nd) : (b + 1) * (halo // nd), :]
            .reshape(halo, LANES)
            .astype(BF16)
        )
        s.tab[b, :, nodes:] = nt(s.w1t[:hid, :], s.fext[b, nodes:, :]).astype(BF16)
        attend(0, b)
        for t in range(tiles):
            cols = slice(t * LANES, (t + 1) * LANES)
            y = s.msg[:, cols] + s.vb[1] + s.res1[b, :, cols]
            centred = y - jnp.sum(y, axis=0, keepdims=True) * (1.0 / hid)
            spread = jnp.sum(centred * centred, axis=0, keepdims=True) * (1.0 / hid)
            rstd = lax.rsqrt(spread + eps_norm)
            normed = centred * rstd
            s.xhat[b, :, cols] = normed
            s.rstd[b, 0:1, cols] = rstd
            n = normed * s.vb[2] + s.vb[3]
            s.h1t[b, :, cols] = jnp.where(n > 0.0, n, jnp.exp(jnp.minimum(n, 0.0)) - 1.0).astype(BF16)
        s.hsend[b] = pack_rows(nt(s.ohs[b], s.h1t[b]))
        scatter_out(s.hsend.at[b], s.hrecv.at[b], 1 + b)

    def project_two(b):
        own = nn(s.w2t[...], s.h1t[b])
        s.own2[b] = own[:hid].astype(BF16)
        s.tgt[1, b] = own[hid : 2 * hid]
        s.res2[b] = own[2 * hid :]

    def layer_two(b):
        receive(1 + b)
        s.tab[b, :, :nodes] = s.own2[b]
        s.h1h[b] = unpack_rows(s.hrecv.at[b]).astype(BF16)
        s.tab[b, :, nodes:] = nt(s.w2t[:hid, :], s.h1h[b]).astype(BF16)
        attend(1, b)
        for t in range(tiles):
            cols = slice(t * LANES, (t + 1) * LANES)
            message = functools.reduce(
                jnp.add, [s.msg[h * head : (h + 1) * head, cols] for h in range(HEADS)]
            )
            s.h2[:, cols] = message * (1.0 / HEADS) + s.bb[...] + s.res2[b, :, cols]
        s.h2t[b] = s.h2[...].astype(BF16)
        rows = nt(s.ohs[b], s.h2t[b])
        s.zsend[b, :, :, :head] = rows.reshape(nd, halo // nd, head)
        scatter_out(s.zsend.at[b], s.zrecv.at[b], 3 + b)
        s.h2r[b] = s.h2[...].T.astype(BF16)

    def pair_terms(score, pos, neg):
        small = jnp.exp(-jnp.abs(score))
        terms = (
            (pos + neg) * jnp.log1p(small)
            + pos * jnp.maximum(-score, 0.0)
            + neg * jnp.maximum(score, 0.0)
        )
        total = jnp.sum(jnp.sum(terms, axis=0, keepdims=True), axis=1, keepdims=True)
        big = 1.0 / (1.0 + small)
        little = small * big
        up = score > 0.0
        d_score = neg * jnp.where(up, big, little) - pos * jnp.where(up, little, big)
        return d_score.astype(BF16), total

    def pair_own(b):
        high, low = split(nn(s.h2r[b], whb) + bias[1:2, :])
        s.left[b] = jnp.concatenate([high, high, low], axis=1)
        score = nt(s.left[b], jnp.concatenate([high, low, high], axis=1))
        d_score, total = pair_terms(score, s.cpos[b, :, :nodes], s.cneg[b, :, :nodes])
        s.sm[12:13, 0:1] += total
        s.dz[b] = nn(d_score, high) + tn(d_score, high)

    def pair_halo(b):
        receive(3 + b)
        rows = s.zrecv[b].reshape(halo, LANES)[:, :head].astype(BF16)
        high, low = split(nn(rows, whb) + bias[1:2, :])
        score = nt(s.left[b], jnp.concatenate([high, low, high], axis=1))
        d_score, total = pair_terms(score, s.cpos[b, :, nodes:], s.cneg[b, :, nodes:])
        s.ysend[b, :, :, :head] = tn(d_score, s.left[b, :, :head]).reshape(nd, halo // nd, head)
        scatter_out(s.ysend.at[b], s.yrecv.at[b], 5 + b)
        s.dz[b] += nn(d_score, high)
        s.sm[12:13, 0:1] += total

    def add_to(ref, value, b):
        if b == 0:
            ref[...] = value
        else:
            ref[...] += value

    def back_two(b):
        receive(5 + b)
        returned = s.yrecv[b].reshape(halo, LANES)[:, :head].astype(BF16)
        dz = s.dz[b] + nn(s.ohst[b], returned)
        s.sm[11:12, :head] += jnp.sum(dz, axis=0, keepdims=True)
        dz_low = dz.astype(BF16)
        d_out = nt(whb, dz_low)
        s.dmsg[:head, :] = d_out * (1.0 / HEADS)
        s.dproj2[b, 2 * hid :, :] = d_out.astype(BF16)
        attend_back(1, b)
        d_table = nt(s.dg[...], s.oht[b])
        s.gsend[b] = pack_rows(d_table[:, nodes:].T)
        scatter_out(s.gsend.at[b], s.grecv.at[b], 7 + b)
        s.dtab[b] = d_table
        s.dzl[b] = dz_low
        s.accb[...] += functools.reduce(
            jnp.add, [d_out[:, t * LANES : (t + 1) * LANES] for t in range(tiles)]
        )
        s.dproj2[b, hid : 2 * hid, :] = s.dtgt[...].astype(BF16)

    def after_two(b):
        s.dhp[b] = nn(s.w2b[:, hid:], s.dproj2[b, hid:, :])
        add_to(s.gw2.at[hid:, :], nt(s.dproj2[b, hid:, :], s.h1t[b]), b)
        d_own = s.dtab[b, :, :nodes].astype(BF16)
        d_halo = s.dtab[b, :, nodes:].astype(BF16)
        add_to(s.gw2.at[:hid, :], nt(d_own, s.h1t[b]) + nn(d_halo, s.h1h[b]), b)
        add_to(s.gwh, nn(s.h2t[b], s.dzl[b]), b)

    def finish_two(b):
        receive(7 + b)
        returned = unpack_rows(s.grecv.at[b]).astype(BF16)
        d_source = s.dtab[b, :, :nodes] + tn(returned, s.ohs[b])
        s.dh[...] = s.dhp[b] + nn(s.w2b[:, :hid], d_source.astype(BF16))

    def norm_back(b):
        for t in range(tiles):
            cols = slice(t * LANES, (t + 1) * LANES)
            normed = s.xhat[b, :, cols]
            n = normed * s.vb[2] + s.vb[3]
            dn = s.dh[:, cols] * jnp.where(n > 0.0, 1.0, jnp.exp(jnp.minimum(n, 0.0)))
            s.acc[3] += dn
            s.acc[2] += dn * normed
            dx = dn * s.vb[2]
            mean = jnp.sum(dx, axis=0, keepdims=True) * (1.0 / hid)
            along = jnp.sum(dx * normed, axis=0, keepdims=True) * (1.0 / hid)
            dy = s.rstd[b, 0:1, cols] * (dx - mean - normed * along)
            s.acc[1] += dy
            s.dmsg[:, cols] = dy

    def resid_one(b):
        add_to(s.gw1.at[2 * hid :, :], nn(s.dmsg[...].astype(BF16), s.fext[b, :nodes, :]), b)

    def weights_one(b):
        d_table = nt(s.dg[...], s.oht[b]).astype(BF16)
        add_to(s.gw1.at[:hid, :], nn(d_table, s.fext[b]), b)
        d_target = nn(s.dtgt[...].astype(BF16), s.fext[b, :nodes, :])
        add_to(s.gw1.at[hid : 2 * hid, :], d_target, b)

    def part(ref, index, count):
        return ref.at[aligned(index, count), :]

    def exchange(axis, number, src_of, dst, own=True):
        index, count = (me, nd) if axis == "dom" else (mine, nr)
        send_sem, recv_sem = s.send_sems.at[number], s.recv_sems.at[number]
        peers(
            axis,
            index,
            count,
            lambda peer: push({axis: peer}, src_of(peer), dst.at[index], send_sem, recv_sem),
        )
        if own:
            pltpu.make_async_copy(src_of(index), dst.at[index], recv_sem).start()
            incoming[number] = dst
        else:
            incoming[number] = dst.at[pl.ds(0, count - 1)]
        outgoing.append((number, dst.at[pl.ds(0, count - 1)]))

    def summed(ref, count):
        return functools.reduce(jnp.add, [ref[i].astype(F32) for i in range(count)])

    chunks = len(bounds) - 1
    split_sum = chunks == 3
    in_one, in_two = 3 * hid, 2 * hid + head
    halves = [slice(i * LANES, (i + 1) * LANES) for i in range(hid // LANES)]
    regions, start = [], 0
    for rows in (slice(hid, 2 * hid), slice(0, hid), slice(2 * hid, in_two)):
        for cols in halves:
            regions.append((start, s.gw2, rows, cols))
            start += rows.stop - rows.start
    regions.append((start, s.gwh, slice(0, head), slice(None)))
    regions.append((start + head, s.gw1, slice(2 * hid, in_one), slice(None)))
    regions.append((bounds[-1] - 2 * hid, s.gw1, slice(0, 2 * hid), slice(None)))

    def spans(chunk):
        low, high = bounds[chunk], bounds[chunk + 1]
        for at, ref, rows, cols in regions:
            first, last, _ = rows.indices(ref.shape[0])
            begin, end = max(low, at), min(high, at + last - first)
            if begin < end:
                width = len(range(*cols.indices(ref.shape[1])))
                yield begin, end, ref, slice(first + begin - at, first + end - at), cols, width

    def pack(chunk):
        for begin, end, ref, rows, cols, width in spans(chunk):
            s.gb[begin:end, :width] = ref[rows, cols].astype(BF16)

    def chunk_of(chunk):
        return [getattr(s, f"{name}{chunk}") for name in ("rb", "gd", "rd", "fin", "ag")]

    def sum_rep(chunk):
        pack(chunk)
        low, high = bounds[chunk], bounds[chunk + 1]
        size = (high - low) // nr
        here = s.gb.at[low:high, :]
        exchange("rep", 11 + 4 * chunk, lambda peer: part(here, peer, size), chunk_of(chunk)[0])

    def sum_dom(chunk):
        rb, gd, rd, fin, ag = chunk_of(chunk)
        receive(11 + 4 * chunk)
        gd[...] = summed(rb, nr).astype(BF16)
        size = gd.shape[0] // nd
        exchange("dom", 12 + 4 * chunk, lambda peer: part(gd, peer, size), rd)

    def share_dom(chunk):
        rb, gd, rd, fin, ag = chunk_of(chunk)
        receive(12 + 4 * chunk)
        fin[...] = summed(rd, nd).astype(BF16)
        exchange("dom", 13 + 4 * chunk, lambda peer: fin, ag.at[mine])

    def share_rep(chunk):
        ag = chunk_of(chunk)[4]
        receive(13 + 4 * chunk)
        exchange("rep", 14 + 4 * chunk, lambda peer: ag.at[mine], ag, own=False)

    def exchange_all(number, src_of, dst):
        index = me * nr + mine
        send_sem, recv_sem = s.send_sems.at[number], s.recv_sems.at[number]
        others(
            lambda there: push(
                there, src_of(there["dom"] * nr + there["rep"]), dst.at[index], send_sem, recv_sem
            )
        )
        pltpu.make_async_copy(src_of(index), dst.at[index], recv_sem).start()
        incoming[number] = dst
        outgoing.append((number, dst.at[pl.ds(0, nd * nr - 1)]))

    def direct(chunk):
        return [getattr(s, f"{name}{chunk}") for name in ("rl", "finl", "agl")]

    def sum_all(chunk):
        pack(chunk)
        rl, finl, agl = direct(chunk)
        size = finl.shape[0]
        here = s.gb.at[bounds[chunk] : bounds[chunk + 1], :]
        exchange_all(11 + 4 * chunk, lambda at: part(here, at, size), rl)

    def share_all(chunk):
        rl, finl, agl = direct(chunk)
        receive(11 + 4 * chunk)
        finl[...] = summed(rl, nd * nr).astype(BF16)
        exchange_all(12 + 4 * chunk, lambda at: finl, agl)

    def vector_sum(j):
        total = jnp.sum(s.acc[j].T, axis=0, keepdims=True)
        for p in range(hid // LANES):
            row = (hid // LANES) * j + p
            s.sm[row : row + 1, :] = total[:, p * LANES : (p + 1) * LANES]

    def small_rep():
        exchange("rep", 9, lambda peer: s.sm, s.sm1)

    def small_dom():
        receive(9)
        s.sms[...] = summed(s.sm1, nr)
        exchange("dom", 10, lambda peer: s.sms, s.sm2)

    params = (w1, w2, wh, vec, bias)

    def update(index, grad, rows, cols):
        made = adamw(
            params[index][rows, cols], grad, firsts[index][rows, cols], seconds[index][rows, cols]
        )
        for offset in range(3):
            outs[1 + 3 * index + offset][rows, cols] = made[offset]

    def small_update():
        receive(10)
        total = summed(s.sm2, nd)
        outs[0][...] = total
        scale = 1.0 / total[13:14, 0:1]
        s.scale[...] = jnp.broadcast_to(scale, s.scale.shape)
        for j in range(5):
            for p in range(hid // LANES):
                row = (hid // LANES) * j + p
                cols = slice(p * LANES, (p + 1) * LANES)
                update(3, total[row : row + 1, :] * scale, slice(j, j + 1), cols)
        for j in range(2):
            update(4, total[10 + j : 11 + j, :head] * scale, slice(j, j + 1), slice(None))

    def chunk_update(chunk):
        staged_sum = split_sum and chunk < 2
        ag = chunk_of(chunk)[4] if staged_sum else direct(chunk)[2]
        receive(4 * chunk + (14 if staged_sum else 12))
        low, high = bounds[chunk], bounds[chunk + 1]
        whole = ag[...].reshape(high - low, LANES)
        scale = s.scale[0:1, 0:1]
        for begin, end, ref, rows, cols, width in spans(chunk):
            if ref is s.gw1:
                for at in range(0, end - begin, LANES):
                    grad = whole[begin - low + at : begin - low + at + LANES].astype(F32).T * scale
                    update(0, grad, slice(None), slice(rows.start + at, rows.start + at + LANES))
            else:
                grad = whole[begin - low : end - low].astype(F32)[:, :width] * scale
                update(1 if ref is s.gw2 else 2, grad, rows, cols)

    s.zsend[...] = jnp.zeros_like(s.zsend)
    s.ysend[...] = jnp.zeros_like(s.ysend)
    s.gb[...] = jnp.zeros_like(s.gb)
    s.sm[13:14, 0:1] = 2.0 * jnp.sum(plive[...].astype(F32), axis=1, keepdims=True)
    receive(0)
    slope_one, slope_two = functools.partial(slopes, 0), functools.partial(slopes, 1)
    stages = [(stage, b) for stage in (layer_one, project_two) for b in range(mb)]
    stages += [(slope_one, 0)]
    stages += [(stage, b) for stage in (layer_two, pair_own) for b in range(mb)]
    for b in range(mb):
        stages += [(pair_halo, b), (slope_two, b)]
    stages += [(slope_one, b) for b in range(1, mb)]
    stages += [(back_two, b) for b in range(mb)]
    for stage, b in stages:
        stage(b)

    for b in range(mb):
        after_two(b)
    if split_sum:
        sum_rep(0)
    vector_sum(4)
    s.sm[10:11, :head] = jnp.sum(s.accb[...].T, axis=0, keepdims=True)
    for b in range(mb):
        final = split_sum and b == mb - 1
        finish_two(b)
        norm_back(b)
        resid_one(b)
        if final:
            sum_rep(1)
        attend_back(0, b)
        weights_one(b)
        if split_sum and b == mb - 2:
            sum_dom(0)
    sum_all(chunks - 1)
    if split_sum:
        sum_dom(1)
        share_dom(0)
    for j in range(4):
        vector_sum(j)
    small_rep()
    loaded(*range(12, 22))
    if split_sum:
        share_dom(1)
    share_all(chunks - 1)
    small_dom()
    if split_sum:
        share_rep(0)
    if split_sum:
        share_rep(1)
    small_update()
    for chunk in range(chunks):
        chunk_update(chunk)
    finish()


def adamw(param, grad, first, second):
    first = beta_one * first + (1.0 - beta_one) * grad
    second = beta_two * second + (1.0 - beta_two) * grad * grad
    fhat = first * (1.0 / (1.0 - beta_one**STEP))
    shat = second * (1.0 / (1.0 - beta_two**STEP))
    return (
        first,
        second,
        param - rate_step * (fhat / (jnp.sqrt(shat) + eps_adam) + decay_rate * param),
    )


def write_kernel(*refs):
    small, held, outs = refs[0], refs[1:16], refs[16:33]
    loss, count, sems = refs[33:]
    loss[...] = small[12:13, 0:1]
    count[...] = small[13:14, 0:1]
    copies = [
        pltpu.make_async_copy(src, dst, sems.at[i])
        for i, (src, dst) in enumerate(zip((loss, count) + held, outs))
    ]
    for copy in copies:
        copy.start()
    for copy in copies:
        copy.wait()


def body(nd, nr, *args):
    data, weights = args[:7], args[7:]
    features, edge_src, node_degree, send_rows, pair_src, pair_dst, pair_live = (
        a.reshape(a.shape[1:]) for a in data
    )
    mb, nodes, width = features.shape
    fan = edge_src.shape[-1]
    per = send_rows.shape[-1]
    halo = nd * per
    ext = nodes + halo
    pairs = pair_src.shape[-1]
    hid = weights[3].shape[1]
    head = weights[2].shape[0]
    in_one, in_two = 3 * hid, 2 * hid + head
    unit = nd * nr * 16
    quarter = (hid // LANES) * hid
    used = 2 * quarter + (hid // LANES + 1) * head + in_one
    rows_all = -(-used // unit) * unit
    bounds = (0, rows_all)
    if quarter % unit == 0 and 2 * hid % unit == 0:
        bounds = (0, 2 * quarter, rows_all - 2 * hid, rows_all)
    dims = (nd, nr, mb, nodes, fan, hid, head, ext, halo, pairs, bounds)
    chunks = {}
    for chunk in range(len(bounds) - 1):
        rows = bounds[chunk + 1] - bounds[chunk]
        if len(bounds) > 2 and chunk < 2:
            size = rows // nr
            chunks[f"rb{chunk}"] = pltpu.VMEM((nr, size, LANES), BF16)
            chunks[f"gd{chunk}"] = pltpu.VMEM((size, LANES), BF16)
            chunks[f"rd{chunk}"] = pltpu.VMEM((nd, size // nd, LANES), BF16)
            chunks[f"fin{chunk}"] = pltpu.VMEM((size // nd, LANES), BF16)
            chunks[f"ag{chunk}"] = pltpu.VMEM((nr, nd, size // nd, LANES), BF16)
        else:
            size = rows // (nd * nr)
            chunks[f"rl{chunk}"] = pltpu.VMEM((nd * nr, size, LANES), BF16)
            chunks[f"finl{chunk}"] = pltpu.VMEM((size, LANES), BF16)
            chunks[f"agl{chunk}"] = pltpu.VMEM((nd * nr, size, LANES), BF16)
    scratch = dict(
        ohs=pltpu.VMEM((mb, halo, nodes), BF16),
        ohst=pltpu.VMEM((mb, nodes, halo), BF16),
        fext=pltpu.VMEM((mb, ext, width), BF16),
        fsend=pltpu.VMEM((nd, mb * per, LANES), BF16),
        frecv=pltpu.VMEM((nd, mb * per, LANES), BF16),
        w1t=pltpu.VMEM((in_one, width), BF16),
        w2b=pltpu.VMEM((hid, in_two), BF16),
        w2t=pltpu.VMEM((in_two, hid), BF16),
        vb=pltpu.VMEM((5, hid, LANES), F32),
        bb=pltpu.VMEM((head, LANES), F32),
        acc=pltpu.VMEM((5, hid, LANES), F32),
        accb=pltpu.VMEM((head, LANES), F32),
        sm=pltpu.VMEM((16, LANES), F32),
        oht=pltpu.VMEM((mb, ext, fan * nodes), BF16),
        tgt=pltpu.VMEM((2, mb, hid, nodes), F32),
        res1=pltpu.VMEM((mb, hid, nodes), F32),
        res2=pltpu.VMEM((mb, head, nodes), F32),
        cpos=pltpu.VMEM((mb, nodes, ext), F32),
        cneg=pltpu.VMEM((mb, nodes, ext), F32),
        tab=pltpu.VMEM((mb, hid, ext), BF16),
        g=pltpu.VMEM((2, mb, hid, fan * nodes), F32),
        mixed=pltpu.VMEM((2, mb, hid, fan * nodes), BF16),
        slope=pltpu.VMEM((2, mb, hid, fan * nodes), BF16),
        al=pltpu.VMEM((2, mb, (nodes // LANES) * HEADS, 16, LANES), F32),
        msg=pltpu.VMEM((hid, nodes), F32),
        xhat=pltpu.VMEM((mb, hid, nodes), F32),
        rstd=pltpu.VMEM((mb, 8, nodes), F32),
        h1t=pltpu.VMEM((mb, hid, nodes), BF16),
        hsend=pltpu.VMEM((mb, nd, 2 * per, LANES), BF16),
        hrecv=pltpu.VMEM((mb, nd, 2 * per, LANES), BF16),
        own2=pltpu.VMEM((mb, hid, nodes), BF16),
        h2=pltpu.VMEM((head, nodes), F32),
        h2t=pltpu.VMEM((mb, head, nodes), BF16),
        h2r=pltpu.VMEM((mb, nodes, head), BF16),
        left=pltpu.VMEM((mb, nodes, 3 * head), BF16),
        dhp=pltpu.VMEM((mb, hid, nodes), F32),
        dzl=pltpu.VMEM((mb, nodes, head), BF16),
        zsend=pltpu.VMEM((mb, nd, per, LANES), F32),
        zrecv=pltpu.VMEM((mb, nd, per, LANES), F32),
        ysend=pltpu.VMEM((mb, nd, per, LANES), F32),
        yrecv=pltpu.VMEM((mb, nd, per, LANES), F32),
        dz=pltpu.VMEM((mb, nodes, head), F32),
        dmsg=pltpu.VMEM((hid, nodes), F32),
        dtgt=pltpu.VMEM((hid, nodes), F32),
        dg=pltpu.VMEM((hid, fan * nodes), BF16),
        dproj2=pltpu.VMEM((mb, in_two, nodes), BF16),
        dtab=pltpu.VMEM((mb, hid, ext), F32),
        h1h=pltpu.VMEM((mb, halo, hid), BF16),
        gsend=pltpu.VMEM((mb, nd, 2 * per, LANES), BF16),
        grecv=pltpu.VMEM((mb, nd, 2 * per, LANES), BF16),
        dh=pltpu.VMEM((hid, nodes), F32),
        gw1=pltpu.VMEM((in_one, LANES), F32),
        gw2=pltpu.VMEM((in_two, hid), F32),
        gwh=pltpu.VMEM((head, head), F32),
        gb=pltpu.VMEM((rows_all, LANES), BF16),
        sm1=pltpu.VMEM((nr, 16, LANES), F32),
        sms=pltpu.VMEM((16, LANES), F32),
        sm2=pltpu.VMEM((nd, 16, LANES), F32),
        load_sems=pltpu.SemaphoreType.DMA((22,)),
        scale=pltpu.VMEM((8, LANES), F32),
        send_sems=pltpu.SemaphoreType.DMA((27,)),
        recv_sems=pltpu.SemaphoreType.DMA((27,)),
        **chunks,
    )
    operands = [features, edge_src.transpose(2, 0, 1), node_degree, send_rows, pair_src, pair_dst]
    operands.append(pair_live.T)
    operands += [w.T if i % 5 == 1 else w for i, w in enumerate(weights)]
    scalars = (jax.ShapeDtypeStruct((1, 1), F32),) * 2
    results = ()
    for operand in operands[7:12]:
        results += (jax.ShapeDtypeStruct(operand.shape, F32),) * 3
    whole = pl.BlockSpec(memory_space=pltpu.VMEM)
    anywhere = pl.BlockSpec(memory_space=pl.ANY)
    made = pl.pallas_call(
        functools.partial(step_kernel, dims, tuple(scratch)),
        out_shape=(jax.ShapeDtypeStruct((16, LANES), F32),) + results,
        in_specs=[anywhere] * 22,
        out_specs=(whole,) * 16,
        scratch_shapes=[pltpu.VMEM(a.shape, a.dtype) for a in operands] + list(scratch.values()),
        compiler_params=pltpu.CompilerParams(
            collective_id=0, has_side_effects=True, vmem_limit_bytes=(34 + ext // 32) * 1024 * 1024
        ),
    )(*(pltpu.with_memory_space_constraint(a, pltpu.HBM) for a in operands))
    made = pl.pallas_call(
        write_kernel,
        out_shape=scalars + results,
        in_specs=[whole] * 16,
        out_specs=(anywhere,) * 17,
        scratch_shapes=[pltpu.VMEM((1, 1), F32)] * 2 + [pltpu.SemaphoreType.DMA((17,))],
        compiler_params=pltpu.CompilerParams(vmem_limit_bytes=1024 * 1024),
    )(*made)
    loss, count = (a.reshape(()) for a in made[:2])
    return (loss, count) + tuple(a.T if i // 3 == 1 else a for i, a in enumerate(made[2:]))


def solution(mesh):
    sharded = (
        P("rep", None, "dom", None),
        P("rep", None, "dom", None),
        P("rep", None, "dom"),
        P("rep", None, "dom", None),
        P("rep", None, "dom"),
        P("rep", None, "dom"),
        P("rep", None, "dom"),
    )
    return jax.shard_map(
        functools.partial(body, mesh.shape["dom"], mesh.shape["rep"]),
        mesh=mesh,
        in_specs=sharded + (P(),) * 15,
        out_specs=(P(),) * 17,
        check_vma=False,
    )
```

```python
import functools
from types import SimpleNamespace

import jax
import jax.numpy as jnp
from jax import lax
from jax.experimental import pallas as pl
from jax.experimental.pallas import tpu as pltpu
from jax.sharding import PartitionSpec as P

HEADS = 4
STEP = 5
LANES = 128

eps_norm = 1e-05
beta_one = 0.9
beta_two = 0.999
rate_step = 0.05
decay_rate = 0.01
eps_adam = 1e-08

F32 = jnp.float32
BF16 = jnp.bfloat16
MESH = pl.DeviceIdType.MESH


def contract(left, right, left_dim, right_dim):
    return lax.dot_general(
        left, right, (((left_dim,), (right_dim,)), ((), ())), preferred_element_type=F32
    )


def nn(left, right):
    return contract(left, right, 1, 0)


def nt(left, right):
    return contract(left, right, 1, 1)


def tn(left, right):
    return contract(left, right, 0, 0)


def split(value):
    high = value.astype(BF16)
    return high, (value - high.astype(F32)).astype(BF16)


def sigmoid(value):
    return 0.5 * jnp.tanh(0.5 * value) + 0.5


def row_iota(rows, columns):
    return lax.broadcasted_iota(jnp.int32, (rows, columns), 0)


def lane_iota(rows, columns):
    return lax.broadcasted_iota(jnp.int32, (rows, columns), 1)


def aligned(index, size):
    return pl.ds(pl.multiple_of(index * size, size), size)


def step_kernel(dims, names, *refs):
    held, outs, rest_refs = refs[:22], refs[22:38], refs[38:]
    staged = rest_refs[:22]
    s = SimpleNamespace(**dict(zip(names, rest_refs[22:])))
    (feats, edges, degree, sends, psrc, pdst, plive, w1, w2, wh, vec, bias) = staged[:12]
    firsts, seconds = staged[12:17], staged[17:22]
    nd, nr, mb, nodes, fan, hid, head, ext, halo, pairs, bounds = dims
    half = pairs // 2
    tiles = nodes // LANES
    me = lax.axis_index("dom")
    mine = lax.axis_index("rep")

    def peers(axis, index, count, send):
        def one(step, carry):
            send(lax.rem(index + step, count))
            return carry

        lax.fori_loop(1, count, one, 0)

    def others(send):
        def one(step, carry):
            at = lax.rem(me * nr + mine + step, nd * nr)
            send({"dom": lax.div(at, nr), "rep": lax.rem(at, nr)})
            return carry

        lax.fori_loop(1, nd * nr, one, 0)

    def push(there, src, dst, send_sem, recv_sem):
        pltpu.make_async_remote_copy(
            src_ref=src,
            dst_ref=dst,
            send_sem=send_sem,
            recv_sem=recv_sem,
            device_id=there,
            device_id_type=MESH,
        ).start()

    incoming, outgoing = {}, []

    def arrived(ref, sem):
        pltpu.make_async_copy(ref, ref, sem).wait()

    def receive(number):
        arrived(incoming.pop(number), s.recv_sems.at[number])

    def finish():
        for number in list(incoming):
            receive(number)
        for number, ref in outgoing:
            arrived(ref, s.send_sems.at[number])

    def load(*which):
        for i in which:
            pltpu.make_async_copy(held[i], staged[i], s.load_sems.at[i]).start()

    def loaded(*which):
        for i in which:
            arrived(staged[i], s.load_sems.at[i])

    def scatter_out(src, dst, number):
        send_sem, recv_sem = s.send_sems.at[number], s.recv_sems.at[number]
        peers(
            "dom",
            me,
            nd,
            lambda peer: push({"dom": peer}, src.at[peer], dst.at[me], send_sem, recv_sem),
        )
        pltpu.make_async_copy(src.at[me], dst.at[me], recv_sem).start()
        incoming[number] = dst
        outgoing.append((number, src.at[pl.ds(0, nd - 1)]))

    load(3, 0)
    barrier = pltpu.get_barrier_semaphore()
    others(lambda there: pl.semaphore_signal(barrier, inc=1, device_id=there, device_id_type=MESH))
    load(7, 8, 9, 10, 11, 1, 2, 4, 5, 6)
    loaded(3)
    for b in range(mb):
        spread = (
            lax.div(row_iota(halo, nd), halo // nd) == lane_iota(halo, nd)
        ).astype(F32).astype(BF16)
        listed = nn(spread, sends[b].astype(F32).astype(BF16))
        pick = lax.rem(row_iota(halo, halo // nd), halo // nd) == lane_iota(halo, halo // nd)
        column = jnp.sum(jnp.where(pick, listed, 0.0), axis=1, keepdims=True)
        s.ohs[b] = (lane_iota(halo, nodes).astype(F32) == column).astype(F32).astype(BF16)

    loaded(0)
    for b in range(mb):
        s.fext[b, :nodes, :] = feats[b].astype(BF16)
    parts = [
        nn(s.ohs[b], s.fext[b, :nodes, :]).reshape(nd, halo // nd, LANES) for b in range(mb)
    ]
    s.fsend[...] = jnp.concatenate(parts, axis=1).astype(BF16)
    pl.semaphore_wait(barrier, nd * nr - 1)
    scatter_out(s.fsend, s.frecv, 0)
    load(*range(12, 22))

    loaded(7, 8, 9, 10, 11)
    for b in range(mb):
        s.ohst[b] = s.ohs[b].astype(F32).T.astype(BF16)
    s.w1t[...] = w1[...].T.astype(BF16)
    s.w2t[...] = w2[...].astype(BF16)
    s.w2b[...] = w2[...].T.astype(BF16)
    whb = wh[...].astype(BF16)
    for j in range(5):
        s.vb[j] = jnp.broadcast_to(vec[j : j + 1, :], (LANES, hid)).T
    s.bb[...] = jnp.broadcast_to(bias[0:1, :], (LANES, head)).T
    s.acc[...] = jnp.zeros_like(s.acc)
    s.accb[...] = jnp.zeros_like(s.accb)
    s.sm[...] = jnp.zeros_like(s.sm)
    loaded(1, 2, 4, 5, 6)

    for b in range(mb):

        def one_hot(k, carry):
            index = edges[k, b : b + 1, :]
            s.oht[b, :, aligned(k, nodes)] = (
                (row_iota(ext, nodes) == index).astype(F32).astype(BF16)
            )
            return carry

        lax.fori_loop(0, fan, one_hot, 0)

        s.tab[b, :, :nodes] = nt(s.w1t[:hid, :], s.fext[b, :nodes, :]).astype(BF16)
        rest = nt(s.w1t[hid:, :], s.fext[b, :nodes, :])
        s.tgt[0, b] = rest[:hid]
        s.res1[b] = rest[hid:]

        slot = lax.rem(lane_iota(1, pairs), half)
        count = jnp.sum(
            jnp.where(lane_iota(1, mb) == b, plive[...].astype(F32), 0.0), axis=1, keepdims=True
        )
        live = slot.astype(F32) < count
        from_src = (row_iota(nodes, pairs) == psrc[b : b + 1, :]).astype(F32).astype(BF16)
        to_dst = (
            ((row_iota(ext, pairs) == pdst[b : b + 1, :]) & live).astype(F32).astype(BF16)
        )
        s.cpos[b] = nt(from_src[:, :half], to_dst[:, :half])
        s.cneg[b] = nt(from_src[:, half:], to_dst[:, half:])

    def place(index):
        tile, which = divmod(index, HEADS)
        rows = slice(which * head, (which + 1) * head)
        return tile, rows, slice(tile * LANES, (tile + 1) * LANES)

    def slot_at(k, tile):
        return slice(k * nodes + tile * LANES, k * nodes + (tile + 1) * LANES)

    def attend(layer, b):
        att = 0 if layer == 0 else 4
        s.g[layer, b] = nn(s.tab[b], s.oht[b])

        for index in range(tiles * HEADS):
            tile, rows, cols = place(index)
            target = s.tgt[layer, b, rows, cols]
            weight = s.vb[att, rows, :]
            count = degree[b : b + 1, cols]
            scores = []
            for k in range(fan):
                u = s.g[layer, b, rows, slot_at(k, tile)] + target
                mixed = u * sigmoid(u)
                score = jnp.sum(mixed * weight, axis=0, keepdims=True)
                scores.append(jnp.where(count > k, score, -1e30))
            top = functools.reduce(jnp.maximum, scores)
            weights = [
                jnp.where(count > k, jnp.exp(scores[k] - top), 0.0) for k in range(fan)
            ]
            inverse = 1.0 / functools.reduce(jnp.add, weights)
            message = jnp.zeros((head, LANES), F32)
            for k in range(fan):
                alpha = weights[k] * inverse
                s.al[layer, b, index, k : k + 1, :] = alpha
                message = message + alpha * s.g[layer, b, rows, slot_at(k, tile)]
            s.msg[rows, cols] = message

    def attend_back(layer, b):
        att = 0 if layer == 0 else 4

        for index in range(tiles * HEADS):
            tile, rows, cols = place(index)
            if layer == 0:
                d_message = s.dmsg[rows, cols]
            else:
                d_message = s.dmsg[:head, cols]
            alphas = [s.al[layer, b, index, k : k + 1, :] for k in range(fan)]
            d_alphas = [
                jnp.sum(d_message * s.g[layer, b, rows, slot_at(k, tile)], axis=0, keepdims=True)
                for k in range(fan)
            ]
            total = functools.reduce(jnp.add, [a * d for a, d in zip(alphas, d_alphas)])
            d_target = jnp.zeros((head, LANES), F32)
            d_att = jnp.zeros((head, LANES), F32)
            for k in range(fan):
                d_score = alphas[k] * (d_alphas[k] - total)
                d_u = d_score * s.slope[layer, b, rows, slot_at(k, tile)].astype(F32)
                d_target = d_target + d_u
                d_att = d_att + d_score * s.mixed[layer, b, rows, slot_at(k, tile)].astype(F32)
                s.dg[rows, slot_at(k, tile)] = (alphas[k] * d_message + d_u).astype(BF16)
            s.dtgt[rows, cols] = d_target
            s.acc[att, rows, :] += d_att

    def slopes(layer, b):
        att = 0 if layer == 0 else 4
        for index in range(tiles * HEADS):
            tile, rows, cols = place(index)
            target = s.tgt[layer, b, rows, cols]
            weight = s.vb[att, rows, :]
            for k in range(fan):
                u = s.g[layer, b, rows, slot_at(k, tile)] + target
                gate = sigmoid(u)
                mixed = u * gate
                s.mixed[layer, b, rows, slot_at(k, tile)] = mixed.astype(BF16)
                slope = weight * (gate * (1.0 + (u - mixed)))
                s.slope[layer, b, rows, slot_at(k, tile)] = slope.astype(BF16)

    def pack_rows(value):
        blocks = value.reshape(nd, halo // nd, hid)
        return jnp.concatenate([blocks[:, :, :LANES], blocks[:, :, LANES:]], axis=1).astype(BF16)

    def unpack_rows(ref):
        blocks = ref[...].astype(F32)
        per = halo // nd
        return jnp.concatenate([blocks[:, :per, :], blocks[:, per:, :]], axis=2).reshape(halo, hid)

    def layer_one(b):
        s.fext[b, nodes:, :] = (
            s.frecv[...].astype(F32)[:, b * (halo // nd) : (b + 1) * (halo // nd), :]
            .reshape(halo, LANES)
            .astype(BF16)
        )
        s.tab[b, :, nodes:] = nt(s.w1t[:hid, :], s.fext[b, nodes:, :]).astype(BF16)
        attend(0, b)
        for t in range(tiles):
            cols = slice(t * LANES, (t + 1) * LANES)
            y = s.msg[:, cols] + s.vb[1] + s.res1[b, :, cols]
            centred = y - jnp.sum(y, axis=0, keepdims=True) * (1.0 / hid)
            spread = jnp.sum(centred * centred, axis=0, keepdims=True) * (1.0 / hid)
            rstd = lax.rsqrt(spread + eps_norm)
            normed = centred * rstd
            s.xhat[b, :, cols] = normed
            s.rstd[b, 0:1, cols] = rstd
            n = normed * s.vb[2] + s.vb[3]
            s.h1t[b, :, cols] = jnp.where(n > 0.0, n, jnp.exp(jnp.minimum(n, 0.0)) - 1.0).astype(BF16)
        s.hsend[b] = pack_rows(nt(s.ohs[b], s.h1t[b]))
        scatter_out(s.hsend.at[b], s.hrecv.at[b], 1 + b)

    def project_two(b):
        own = nn(s.w2t[...], s.h1t[b])
        s.own2[b] = own[:hid].astype(BF16)
        s.tgt[1, b] = own[hid : 2 * hid]
        s.res2[b] = own[2 * hid :]

    def layer_two(b):
        receive(1 + b)
        s.tab[b, :, :nodes] = s.own2[b]
        s.h1h[b] = unpack_rows(s.hrecv.at[b]).astype(BF16)
        s.tab[b, :, nodes:] = nt(s.w2t[:hid, :], s.h1h[b]).astype(BF16)
        attend(1, b)
        for t in range(tiles):
            cols = slice(t * LANES, (t + 1) * LANES)
            message = functools.reduce(
                jnp.add, [s.msg[h * head : (h + 1) * head, cols] for h in range(HEADS)]
            )
            s.h2[:, cols] = message * (1.0 / HEADS) + s.bb[...] + s.res2[b, :, cols]
        s.h2t[b] = s.h2[...].astype(BF16)
        rows = nt(s.ohs[b], s.h2t[b])
        s.zsend[b, :, :, :head] = rows.reshape(nd, halo // nd, head)
        scatter_out(s.zsend.at[b], s.zrecv.at[b], 3 + b)
        s.h2r[b] = s.h2[...].T.astype(BF16)

    def pair_terms(score, pos, neg):
        small = jnp.exp(-jnp.abs(score))
        terms = (
            (pos + neg) * jnp.log1p(small)
            + pos * jnp.maximum(-score, 0.0)
            + neg * jnp.maximum(score, 0.0)
        )
        total = jnp.sum(jnp.sum(terms, axis=0, keepdims=True), axis=1, keepdims=True)
        big = 1.0 / (1.0 + small)
        little = small * big
        up = score > 0.0
        d_score = neg * jnp.where(up, big, little) - pos * jnp.where(up, little, big)
        return d_score.astype(BF16), total

    def pair_own(b):
        high, low = split(nn(s.h2r[b], whb) + bias[1:2, :])
        s.left[b] = jnp.concatenate([high, high, low], axis=1)
        score = nt(s.left[b], jnp.concatenate([high, low, high], axis=1))
        d_score, total = pair_terms(score, s.cpos[b, :, :nodes], s.cneg[b, :, :nodes])
        s.sm[12:13, 0:1] += total
        s.dz[b] = nn(d_score, high) + tn(d_score, high)

    def pair_halo(b):
        receive(3 + b)
        rows = s.zrecv[b].reshape(halo, LANES)[:, :head].astype(BF16)
        high, low = split(nn(rows, whb) + bias[1:2, :])
        score = nt(s.left[b], jnp.concatenate([high, low, high], axis=1))
        d_score, total = pair_terms(score, s.cpos[b, :, nodes:], s.cneg[b, :, nodes:])
        s.ysend[b, :, :, :head] = tn(d_score, s.left[b, :, :head]).reshape(nd, halo // nd, head)
        scatter_out(s.ysend.at[b], s.yrecv.at[b], 5 + b)
        s.dz[b] += nn(d_score, high)
        s.sm[12:13, 0:1] += total

    def add_to(ref, value, b):
        if b == 0:
            ref[...] = value
        else:
            ref[...] += value

    def back_two(b):
        receive(5 + b)
        returned = s.yrecv[b].reshape(halo, LANES)[:, :head].astype(BF16)
        dz = s.dz[b] + nn(s.ohst[b], returned)
        s.sm[11:12, :head] += jnp.sum(dz, axis=0, keepdims=True)
        dz_low = dz.astype(BF16)
        d_out = nt(whb, dz_low)
        s.dmsg[:head, :] = d_out * (1.0 / HEADS)
        s.dproj2[b, 2 * hid :, :] = d_out.astype(BF16)
        attend_back(1, b)
        d_table = nt(s.dg[...], s.oht[b])
        s.gsend[b] = pack_rows(d_table[:, nodes:].T)
        scatter_out(s.gsend.at[b], s.grecv.at[b], 7 + b)
        s.dtab[b] = d_table
        s.dzl[b] = dz_low
        s.accb[...] += functools.reduce(
            jnp.add, [d_out[:, t * LANES : (t + 1) * LANES] for t in range(tiles)]
        )
        s.dproj2[b, hid : 2 * hid, :] = s.dtgt[...].astype(BF16)

    def after_two(b):
        s.dhp[b] = nn(s.w2b[:, hid:], s.dproj2[b, hid:, :])
        add_to(s.gw2.at[hid:, :], nt(s.dproj2[b, hid:, :], s.h1t[b]), b)
        d_own = s.dtab[b, :, :nodes].astype(BF16)
        d_halo = s.dtab[b, :, nodes:].astype(BF16)
        add_to(s.gw2.at[:hid, :], nt(d_own, s.h1t[b]) + nn(d_halo, s.h1h[b]), b)
        add_to(s.gwh, nn(s.h2t[b], s.dzl[b]), b)

    def finish_two(b):
        receive(7 + b)
        returned = unpack_rows(s.grecv.at[b]).astype(BF16)
        d_source = s.dtab[b, :, :nodes] + tn(returned, s.ohs[b])
        s.dh[...] = s.dhp[b] + nn(s.w2b[:, :hid], d_source.astype(BF16))

    def norm_back(b):
        for t in range(tiles):
            cols = slice(t * LANES, (t + 1) * LANES)
            normed = s.xhat[b, :, cols]
            n = normed * s.vb[2] + s.vb[3]
            dn = s.dh[:, cols] * jnp.where(n > 0.0, 1.0, jnp.exp(jnp.minimum(n, 0.0)))
            s.acc[3] += dn
            s.acc[2] += dn * normed
            dx = dn * s.vb[2]
            mean = jnp.sum(dx, axis=0, keepdims=True) * (1.0 / hid)
            along = jnp.sum(dx * normed, axis=0, keepdims=True) * (1.0 / hid)
            dy = s.rstd[b, 0:1, cols] * (dx - mean - normed * along)
            s.acc[1] += dy
            s.dmsg[:, cols] = dy

    def resid_one(b):
        add_to(s.gw1.at[2 * hid :, :], nn(s.dmsg[...].astype(BF16), s.fext[b, :nodes, :]), b)

    def weights_one(b):
        d_table = nt(s.dg[...], s.oht[b]).astype(BF16)
        add_to(s.gw1.at[:hid, :], nn(d_table, s.fext[b]), b)
        d_target = nn(s.dtgt[...].astype(BF16), s.fext[b, :nodes, :])
        add_to(s.gw1.at[hid : 2 * hid, :], d_target, b)

    def part(ref, index, count):
        return ref.at[aligned(index, count), :]

    def exchange(axis, number, src_of, dst, own=True):
        index, count = (me, nd) if axis == "dom" else (mine, nr)
        send_sem, recv_sem = s.send_sems.at[number], s.recv_sems.at[number]
        peers(
            axis,
            index,
            count,
            lambda peer: push({axis: peer}, src_of(peer), dst.at[index], send_sem, recv_sem),
        )
        if own:
            pltpu.make_async_copy(src_of(index), dst.at[index], recv_sem).start()
            incoming[number] = dst
        else:
            incoming[number] = dst.at[pl.ds(0, count - 1)]
        outgoing.append((number, dst.at[pl.ds(0, count - 1)]))

    def summed(ref, count):
        return functools.reduce(jnp.add, [ref[i].astype(F32) for i in range(count)])

    chunks = len(bounds) - 1
    split_sum = chunks == 4
    in_one, in_two = 3 * hid, 2 * hid + head
    halves = [slice(i * LANES, (i + 1) * LANES) for i in range(hid // LANES)]
    regions, start = [], 0
    for rows in (slice(hid, 2 * hid), slice(0, hid), slice(2 * hid, in_two)):
        for cols in halves:
            regions.append((start, s.gw2, rows, cols))
            start += rows.stop - rows.start
    regions.append((start, s.gwh, slice(0, head), slice(None)))
    regions.append((start + head, s.gw1, slice(2 * hid, in_one), slice(None)))
    regions.append((bounds[-1] - 2 * hid, s.gw1, slice(0, 2 * hid), slice(None)))

    def spans(chunk):
        low, high = bounds[chunk], bounds[chunk + 1]
        for at, ref, rows, cols in regions:
            first, last, _ = rows.indices(ref.shape[0])
            begin, end = max(low, at), min(high, at + last - first)
            if begin < end:
                width = len(range(*cols.indices(ref.shape[1])))
                yield begin, end, ref, slice(first + begin - at, first + end - at), cols, width

    def pack(chunk):
        for begin, end, ref, rows, cols, width in spans(chunk):
            s.gb[begin:end, :width] = ref[rows, cols].astype(BF16)

    def chunk_of(chunk):
        return [getattr(s, f"{name}{chunk}") for name in ("rb", "gd", "rd", "fin", "ag")]

    def sum_rep(chunk):
        pack(chunk)
        low, high = bounds[chunk], bounds[chunk + 1]
        size = (high - low) // nr
        here = s.gb.at[low:high, :]
        exchange("rep", 11 + 4 * chunk, lambda peer: part(here, peer, size), chunk_of(chunk)[0])

    def sum_dom(chunk):
        rb, gd, rd, fin, ag = chunk_of(chunk)
        receive(11 + 4 * chunk)
        gd[...] = summed(rb, nr).astype(BF16)
        size = gd.shape[0] // nd
        exchange("dom", 12 + 4 * chunk, lambda peer: part(gd, peer, size), rd)

    def share_dom(chunk):
        rb, gd, rd, fin, ag = chunk_of(chunk)
        receive(12 + 4 * chunk)
        fin[...] = summed(rd, nd).astype(BF16)
        exchange("dom", 13 + 4 * chunk, lambda peer: fin, ag.at[mine])

    def share_rep(chunk):
        ag = chunk_of(chunk)[4]
        receive(13 + 4 * chunk)
        exchange("rep", 14 + 4 * chunk, lambda peer: ag.at[mine], ag, own=False)

    def exchange_all(number, src_of, dst):
        index = me * nr + mine
        send_sem, recv_sem = s.send_sems.at[number], s.recv_sems.at[number]
        others(
            lambda there: push(
                there, src_of(there["dom"] * nr + there["rep"]), dst.at[index], send_sem, recv_sem
            )
        )
        pltpu.make_async_copy(src_of(index), dst.at[index], recv_sem).start()
        incoming[number] = dst
        outgoing.append((number, dst.at[pl.ds(0, nd * nr - 1)]))

    def direct(chunk):
        return [getattr(s, f"{name}{chunk}") for name in ("rl", "finl", "agl")]

    def sum_all(chunk):
        pack(chunk)
        rl, finl, agl = direct(chunk)
        size = finl.shape[0]
        here = s.gb.at[bounds[chunk] : bounds[chunk + 1], :]
        exchange_all(11 + 4 * chunk, lambda at: part(here, at, size), rl)

    def share_all(chunk):
        rl, finl, agl = direct(chunk)
        receive(11 + 4 * chunk)
        finl[...] = summed(rl, nd * nr).astype(BF16)
        exchange_all(12 + 4 * chunk, lambda at: finl, agl)

    def vector_sum(j):
        total = jnp.sum(s.acc[j].T, axis=0, keepdims=True)
        for p in range(hid // LANES):
            row = (hid // LANES) * j + p
            s.sm[row : row + 1, :] = total[:, p * LANES : (p + 1) * LANES]

    def small_rep():
        exchange("rep", 9, lambda peer: s.sm, s.sm1)

    def small_dom():
        receive(9)
        s.sms[...] = summed(s.sm1, nr)
        exchange("dom", 10, lambda peer: s.sms, s.sm2)

    params = (w1, w2, wh, vec, bias)

    def update(index, grad, rows, cols):
        made = adamw(
            params[index][rows, cols], grad, firsts[index][rows, cols], seconds[index][rows, cols]
        )
        for offset in range(3):
            outs[1 + 3 * index + offset][rows, cols] = made[offset]

    def small_update():
        receive(10)
        total = summed(s.sm2, nd)
        outs[0][...] = total
        scale = 1.0 / total[13:14, 0:1]
        s.scale[...] = jnp.broadcast_to(scale, s.scale.shape)
        for j in range(5):
            for p in range(hid // LANES):
                row = (hid // LANES) * j + p
                cols = slice(p * LANES, (p + 1) * LANES)
                update(3, total[row : row + 1, :] * scale, slice(j, j + 1), cols)
        for j in range(2):
            update(4, total[10 + j : 11 + j, :head] * scale, slice(j, j + 1), slice(None))

    def chunk_update(chunk):
        staged_sum = split_sum and chunk < 3
        ag = chunk_of(chunk)[4] if staged_sum else direct(chunk)[2]
        receive(4 * chunk + (14 if staged_sum else 12))
        low, high = bounds[chunk], bounds[chunk + 1]
        whole = ag[...].reshape(high - low, LANES)
        scale = s.scale[0:1, 0:1]
        for begin, end, ref, rows, cols, width in spans(chunk):
            if ref is s.gw1:
                for at in range(0, end - begin, LANES):
                    grad = whole[begin - low + at : begin - low + at + LANES].astype(F32).T * scale
                    update(0, grad, slice(None), slice(rows.start + at, rows.start + at + LANES))
            else:
                grad = whole[begin - low : end - low].astype(F32)[:, :width] * scale
                update(1 if ref is s.gw2 else 2, grad, rows, cols)

    s.zsend[...] = jnp.zeros_like(s.zsend)
    s.ysend[...] = jnp.zeros_like(s.ysend)
    s.gb[...] = jnp.zeros_like(s.gb)
    s.sm[13:14, 0:1] = 2.0 * jnp.sum(plive[...].astype(F32), axis=1, keepdims=True)
    receive(0)
    slope_one, slope_two = functools.partial(slopes, 0), functools.partial(slopes, 1)
    stages = [(stage, b) for stage in (layer_one, project_two) for b in range(mb)]
    stages += [(slope_one, 0)]
    stages += [(stage, b) for stage in (layer_two, pair_own) for b in range(mb)]
    for b in range(mb):
        stages += [(pair_halo, b), (slope_two, b)]
    stages += [(slope_one, b) for b in range(1, mb)]
    stages += [(back_two, b) for b in range(mb)]
    for stage, b in stages:
        stage(b)

    for b in range(mb):
        after_two(b)
    if split_sum:
        sum_rep(0)
        sum_rep(1)
    vector_sum(4)
    s.sm[10:11, :head] = jnp.sum(s.accb[...].T, axis=0, keepdims=True)
    for b in range(mb):
        final = split_sum and b == mb - 1
        finish_two(b)
        norm_back(b)
        resid_one(b)
        if final:
            sum_rep(2)
            sum_dom(1)
        attend_back(0, b)
        weights_one(b)
        if split_sum and b == mb - 2:
            sum_dom(0)
    sum_all(chunks - 1)
    if split_sum:
        sum_dom(2)
        share_dom(0)
        share_dom(1)
    for j in range(4):
        vector_sum(j)
    small_rep()
    loaded(*range(12, 22))
    if split_sum:
        share_dom(2)
    share_all(chunks - 1)
    small_dom()
    if split_sum:
        share_rep(0)
        share_rep(1)
    if split_sum:
        share_rep(2)
    small_update()
    for chunk in range(chunks):
        chunk_update(chunk)
    finish()


def adamw(param, grad, first, second):
    first = beta_one * first + (1.0 - beta_one) * grad
    second = beta_two * second + (1.0 - beta_two) * grad * grad
    fhat = first * (1.0 / (1.0 - beta_one**STEP))
    shat = second * (1.0 / (1.0 - beta_two**STEP))
    return (
        first,
        second,
        param - rate_step * (fhat / (jnp.sqrt(shat) + eps_adam) + decay_rate * param),
    )


def write_kernel(*refs):
    small, held, outs = refs[0], refs[1:16], refs[16:33]
    loss, count, sems = refs[33:]
    loss[...] = small[12:13, 0:1]
    count[...] = small[13:14, 0:1]
    copies = [
        pltpu.make_async_copy(src, dst, sems.at[i])
        for i, (src, dst) in enumerate(zip((loss, count) + held, outs))
    ]
    for copy in copies:
        copy.start()
    for copy in copies:
        copy.wait()


def body(nd, nr, *args):
    data, weights = args[:7], args[7:]
    features, edge_src, node_degree, send_rows, pair_src, pair_dst, pair_live = (
        a.reshape(a.shape[1:]) for a in data
    )
    mb, nodes, width = features.shape
    fan = edge_src.shape[-1]
    per = send_rows.shape[-1]
    halo = nd * per
    ext = nodes + halo
    pairs = pair_src.shape[-1]
    hid = weights[3].shape[1]
    head = weights[2].shape[0]
    in_one, in_two = 3 * hid, 2 * hid + head
    unit = nd * nr * 16
    quarter = (hid // LANES) * hid
    used = 2 * quarter + (hid // LANES + 1) * head + in_one
    rows_all = -(-used // unit) * unit
    bounds = (0, rows_all)
    if quarter % unit == 0 and 2 * hid % unit == 0:
        bounds = (0, quarter, 2 * quarter, rows_all - 2 * hid, rows_all)
    dims = (nd, nr, mb, nodes, fan, hid, head, ext, halo, pairs, bounds)
    chunks = {}
    for chunk in range(len(bounds) - 1):
        rows = bounds[chunk + 1] - bounds[chunk]
        if len(bounds) > 2 and chunk < 3:
            size = rows // nr
            chunks[f"rb{chunk}"] = pltpu.VMEM((nr, size, LANES), BF16)
            chunks[f"gd{chunk}"] = pltpu.VMEM((size, LANES), BF16)
            chunks[f"rd{chunk}"] = pltpu.VMEM((nd, size // nd, LANES), BF16)
            chunks[f"fin{chunk}"] = pltpu.VMEM((size // nd, LANES), BF16)
            chunks[f"ag{chunk}"] = pltpu.VMEM((nr, nd, size // nd, LANES), BF16)
        else:
            size = rows // (nd * nr)
            chunks[f"rl{chunk}"] = pltpu.VMEM((nd * nr, size, LANES), BF16)
            chunks[f"finl{chunk}"] = pltpu.VMEM((size, LANES), BF16)
            chunks[f"agl{chunk}"] = pltpu.VMEM((nd * nr, size, LANES), BF16)
    scratch = dict(
        ohs=pltpu.VMEM((mb, halo, nodes), BF16),
        ohst=pltpu.VMEM((mb, nodes, halo), BF16),
        fext=pltpu.VMEM((mb, ext, width), BF16),
        fsend=pltpu.VMEM((nd, mb * per, LANES), BF16),
        frecv=pltpu.VMEM((nd, mb * per, LANES), BF16),
        w1t=pltpu.VMEM((in_one, width), BF16),
        w2b=pltpu.VMEM((hid, in_two), BF16),
        w2t=pltpu.VMEM((in_two, hid), BF16),
        vb=pltpu.VMEM((5, hid, LANES), F32),
        bb=pltpu.VMEM((head, LANES), F32),
        acc=pltpu.VMEM((5, hid, LANES), F32),
        accb=pltpu.VMEM((head, LANES), F32),
        sm=pltpu.VMEM((16, LANES), F32),
        oht=pltpu.VMEM((mb, ext, fan * nodes), BF16),
        tgt=pltpu.VMEM((2, mb, hid, nodes), F32),
        res1=pltpu.VMEM((mb, hid, nodes), F32),
        res2=pltpu.VMEM((mb, head, nodes), F32),
        cpos=pltpu.VMEM((mb, nodes, ext), F32),
        cneg=pltpu.VMEM((mb, nodes, ext), F32),
        tab=pltpu.VMEM((mb, hid, ext), BF16),
        g=pltpu.VMEM((2, mb, hid, fan * nodes), F32),
        mixed=pltpu.VMEM((2, mb, hid, fan * nodes), BF16),
        slope=pltpu.VMEM((2, mb, hid, fan * nodes), BF16),
        al=pltpu.VMEM((2, mb, (nodes // LANES) * HEADS, 16, LANES), F32),
        msg=pltpu.VMEM((hid, nodes), F32),
        xhat=pltpu.VMEM((mb, hid, nodes), F32),
        rstd=pltpu.VMEM((mb, 8, nodes), F32),
        h1t=pltpu.VMEM((mb, hid, nodes), BF16),
        hsend=pltpu.VMEM((mb, nd, 2 * per, LANES), BF16),
        hrecv=pltpu.VMEM((mb, nd, 2 * per, LANES), BF16),
        own2=pltpu.VMEM((mb, hid, nodes), BF16),
        h2=pltpu.VMEM((head, nodes), F32),
        h2t=pltpu.VMEM((mb, head, nodes), BF16),
        h2r=pltpu.VMEM((mb, nodes, head), BF16),
        left=pltpu.VMEM((mb, nodes, 3 * head), BF16),
        dhp=pltpu.VMEM((mb, hid, nodes), F32),
        dzl=pltpu.VMEM((mb, nodes, head), BF16),
        zsend=pltpu.VMEM((mb, nd, per, LANES), F32),
        zrecv=pltpu.VMEM((mb, nd, per, LANES), F32),
        ysend=pltpu.VMEM((mb, nd, per, LANES), F32),
        yrecv=pltpu.VMEM((mb, nd, per, LANES), F32),
        dz=pltpu.VMEM((mb, nodes, head), F32),
        dmsg=pltpu.VMEM((hid, nodes), F32),
        dtgt=pltpu.VMEM((hid, nodes), F32),
        dg=pltpu.VMEM((hid, fan * nodes), BF16),
        dproj2=pltpu.VMEM((mb, in_two, nodes), BF16),
        dtab=pltpu.VMEM((mb, hid, ext), F32),
        h1h=pltpu.VMEM((mb, halo, hid), BF16),
        gsend=pltpu.VMEM((mb, nd, 2 * per, LANES), BF16),
        grecv=pltpu.VMEM((mb, nd, 2 * per, LANES), BF16),
        dh=pltpu.VMEM((hid, nodes), F32),
        gw1=pltpu.VMEM((in_one, LANES), F32),
        gw2=pltpu.VMEM((in_two, hid), F32),
        gwh=pltpu.VMEM((head, head), F32),
        gb=pltpu.VMEM((rows_all, LANES), BF16),
        sm1=pltpu.VMEM((nr, 16, LANES), F32),
        sms=pltpu.VMEM((16, LANES), F32),
        sm2=pltpu.VMEM((nd, 16, LANES), F32),
        load_sems=pltpu.SemaphoreType.DMA((22,)),
        scale=pltpu.VMEM((8, LANES), F32),
        send_sems=pltpu.SemaphoreType.DMA((27,)),
        recv_sems=pltpu.SemaphoreType.DMA((27,)),
        **chunks,
    )
    operands = [features, edge_src.transpose(2, 0, 1), node_degree, send_rows, pair_src, pair_dst]
    operands.append(pair_live.T)
    operands += [w.T if i % 5 == 1 else w for i, w in enumerate(weights)]
    scalars = (jax.ShapeDtypeStruct((1, 1), F32),) * 2
    results = ()
    for operand in operands[7:12]:
        results += (jax.ShapeDtypeStruct(operand.shape, F32),) * 3
    whole = pl.BlockSpec(memory_space=pltpu.VMEM)
    anywhere = pl.BlockSpec(memory_space=pl.ANY)
    made = pl.pallas_call(
        functools.partial(step_kernel, dims, tuple(scratch)),
        out_shape=(jax.ShapeDtypeStruct((16, LANES), F32),) + results,
        in_specs=[anywhere] * 22,
        out_specs=(whole,) * 16,
        scratch_shapes=[pltpu.VMEM(a.shape, a.dtype) for a in operands] + list(scratch.values()),
        compiler_params=pltpu.CompilerParams(
            collective_id=0, has_side_effects=True, vmem_limit_bytes=(34 + ext // 32) * 1024 * 1024
        ),
    )(*(pltpu.with_memory_space_constraint(a, pltpu.HBM) for a in operands))
    made = pl.pallas_call(
        write_kernel,
        out_shape=scalars + results,
        in_specs=[whole] * 16,
        out_specs=(anywhere,) * 17,
        scratch_shapes=[pltpu.VMEM((1, 1), F32)] * 2 + [pltpu.SemaphoreType.DMA((17,))],
        compiler_params=pltpu.CompilerParams(vmem_limit_bytes=1024 * 1024),
    )(*made)
    loss, count = (a.reshape(()) for a in made[:2])
    return (loss, count) + tuple(a.T if i // 3 == 1 else a for i, a in enumerate(made[2:]))


def solution(mesh):
    sharded = (
        P("rep", None, "dom", None),
        P("rep", None, "dom", None),
        P("rep", None, "dom"),
        P("rep", None, "dom", None),
        P("rep", None, "dom"),
        P("rep", None, "dom"),
        P("rep", None, "dom"),
    )
    return jax.shard_map(
        functools.partial(body, mesh.shape["dom"], mesh.shape["rep"]),
        mesh=mesh,
        in_specs=sharded + (P(),) * 15,
        out_specs=(P(),) * 17,
        check_vma=False,
    )
```
